256 devices in a mesh: ens: 4 (over y), space: 64 (over z, x, core).
Axes of the slice: x: 4, y: 4, z: 8, core: 2. Of those that a mesh axis runs over, the one named last changes fastest.
Arguments:
- hidden: bfloat16 [16, 32768, 1024], P('ens', 'space'), as said below
- decoder_weight: float32 [99, 1024], replicated, may hold values from -0.1875 to 0.1875
- decoder_intercept: float32 [99], replicated, may hold values from -3 to 3
- analysis_truth: float32 [99, 32768], P(None, 'space'), may hold values from -12 to 12
- var_weight: float32 [99], replicated, may hold values from 1 to 10
- lat_weight: float32 [640], replicated, as said below
- area_bin: int32 [32768], P('space'), may hold values from 0 to 639
- train_step: int32 [1], replicated, may hold values from 500 to 999
Outputs:
- grad_hidden: bfloat16 [16, 32768, 1024], P('ens', 'space')
- new_weight: float32 [99, 1024], replicated
- new_bias: float32 [99], replicated
The draws below stay inside these ranges and needn't reach their ends.
Inputs may be any that keep to these rules, and one draw needn't show every extreme that they name: `hidden`: decoder input features. `lat_weight`: positive area weights.
All inputs are finite; a program needn't handle non-finite values.
Results may differ from the reference program's by a relative error of at most 0.0015.
The reference program's roundings to bfloat16 on the way count: a program that leaves them out, or rounds other values in their place, can miss the bound.
Values may be sent and summed in bfloat16 or wider, within the bound.
No kernel may reach another device: no remote copies, remote signals or barrier semaphores. Data moves between devices by JAX's collectives and lax.ppermute only.
A program may use at most 64 MiB of HBM per device.

```python
import math
import jax
import jax.numpy as jnp
from jax import lax

D = 1024
V = 99
NLAT = 640
WARMUP = 1000
MEMBERS = 16
PTS = 32768


def draw_hidden(key, part):
    key = jax.random.fold_in(key, 11)
    key_base, roughness_key = jax.random.split(key, 2)
    position = jnp.arange(D, dtype=jnp.float32) / (D - 1)
    values = jnp.clip(jax.random.normal(key_base, (MEMBERS, PTS, D), jnp.float32), -6.0, 6.0)
    column_scale = jnp.exp(math.log(0.5) + math.log(10.0) * position)
    roughness = jax.random.uniform(roughness_key, (D,), jnp.float32, 0.8, 1.25)
    return (values * (column_scale * roughness)[None, None, :]).astype(jnp.bfloat16)


def draw_lat_weight(key, part):
    key = jax.random.fold_in(key, 12)
    centre = (jnp.arange(NLAT, dtype=jnp.float32) + 0.5) / NLAT
    values = 0.1 + 0.9 * jnp.sin(0.5 * math.pi * centre)
    roughness = jax.random.uniform(key, (NLAT,), jnp.float32, 0.7, 1.4)
    return values * roughness


def draw_area_bin(key, part):
    key = jax.random.fold_in(key, 13)
    indices = jnp.arange(PTS, dtype=jnp.int32)
    jitter = jax.random.randint(key, (PTS,), -2, 3, jnp.int32)
    bands = jnp.clip(indices * NLAT // PTS + jitter, 0, NLAT - 1)
    return bands.at[0].set(0).at[PTS - 1].set(NLAT - 1)


def level_of(own_key, extent, cuts, least, top_value):
    def one(dim, shards_of):
        steps = jax.random.uniform(jax.random.fold_in(jax.random.fold_in(own_key, 6), dim), (shards_of,), jnp.float32, least / len(cuts), top_value / len(cuts))
        return jnp.repeat(jnp.exp(steps), extent[dim] // shards_of).reshape((-1,) + (1,) * (len(extent) - dim - 1))

    gain = one(*cuts[0])
    for cut in cuts[1:]:
        gain = gain * one(*cut)
    return gain


def scatter_about(own_key, extent, deviation, most, cuts=(), kind=jnp.bfloat16):
    result = jax.random.normal(own_key, extent, jnp.float32) * deviation
    if len(cuts) > 0:
        result = level_of(own_key, extent, cuts, -0.22, 0.18) * result
    return jnp.clip(result, min=-most, max=most).astype(kind)


def setup_inputs(seed: int = 0) -> dict:
    keys = jax.random.split(jax.random.key(seed), 9)
    hidden = draw_hidden(jax.random.fold_in(keys[8], 71), 0)
    decoder_weight = scatter_about(keys[1], (V, D), D ** -0.5, 0.1875, (), jnp.float32)
    decoder_intercept = scatter_about(keys[2], (V,), 0.5, 3.0, (), jnp.float32)
    analysis_truth = scatter_about(keys[3], (V, PTS), 2.0, 12.0, ((1, 64),), jnp.float32)
    var_weight = jnp.clip(jnp.exp(jax.random.uniform(keys[4], (V,), jnp.float32, math.log(1.0), math.log(10.0))), 1.0, 10.0)
    lat_weight = draw_lat_weight(jax.random.fold_in(keys[8], 71), 0)
    area_bin = draw_area_bin(jax.random.fold_in(keys[8], 71), 0)
    train_step = jax.random.randint(keys[7], (1,), WARMUP // 2, WARMUP).astype(jnp.int32)
    return dict(hidden=hidden, decoder_weight=decoder_weight, decoder_intercept=decoder_intercept, analysis_truth=analysis_truth, var_weight=var_weight, lat_weight=lat_weight, area_bin=area_bin, train_step=train_step)


smooth_sq = 0.0025
fair_alpha = 0.95

def smoothed_signum(difference):
    return difference / jnp.sqrt(difference * difference + smooth_sq)

def reference(hidden, decoder_weight, decoder_intercept, analysis_truth, var_weight, lat_weight, area_bin, train_step):
    ensemble_realizations = hidden.shape[0]
    half_weight = decoder_weight.astype(jnp.bfloat16)

    def forward_pass(member_hidden):
        return lax.dot_general(half_weight, member_hidden, (((1,), (1,)), ((), ())), preferred_element_type=jnp.float32)
    decoded_prognosis = lax.map(forward_pass, hidden) + decoder_intercept[None, :, None]
    prognosis_misfit = decoded_prognosis - analysis_truth[None]

    def couple_accumulated(member_rows):
        return lax.optimization_barrier(jnp.sum(smoothed_signum(member_rows[:, None, :] - member_rows[None, :, :]), axis=1))
    couple_grand_figure = lax.map(couple_accumulated, jnp.transpose(prognosis_misfit, (1, 0, 2)))
    couple_grand_figure = jnp.transpose(couple_grand_figure, (1, 0, 2))
    fair_eps = (1.0 - fair_alpha) / ensemble_realizations
    couple_normalizer = (1.0 - fair_eps) / (ensemble_realizations * (ensemble_realizations - 1))
    ensemble_rank_interval = (smoothed_signum(prognosis_misfit) / ensemble_realizations - couple_normalizer * couple_grand_figure).astype(jnp.bfloat16)
    area_weight = lat_weight[area_bin]
    mean_area = jnp.sum(area_weight) / PTS
    weighted = (area_weight[None, None, :] * var_weight[None, :, None] * ensemble_rank_interval.astype(jnp.float32)).astype(jnp.bfloat16)

    def backward(member_weighted):
        product = lax.dot_general(member_weighted, half_weight, (((0,), (0,)), ((), ())), preferred_element_type=jnp.float32)
        return (product / mean_area).astype(jnp.bfloat16)
    grad_hidden = lax.map(backward, weighted)

    def accumulate(running, pieces):
        return (running + jnp.dot(pieces[0], pieces[1], preferred_element_type=jnp.float32), None)
    weight_raw, unused = lax.scan(accumulate, jnp.zeros((V, D), jnp.float32), (weighted, hidden))
    weight_grad = weight_raw / mean_area
    bias_grad = lax.optimization_barrier(jnp.sum(weighted.astype(jnp.float32), axis=(0, 2))) / mean_area
    square_sum = jnp.sum(weight_grad * weight_grad) + jnp.sum(bias_grad * bias_grad)
    grad_rms = jnp.sqrt(square_sum / (V * D + V) + 1e-06)
    step_scale = (train_step[0] + 1).astype(jnp.float32) / WARMUP * jnp.minimum(1.0, 1.0 / grad_rms)
    new_weight = decoder_weight - step_scale * weight_grad
    new_bias = decoder_intercept - step_scale * bias_grad
    return (grad_hidden, new_weight, new_bias)
```

```python
import jax
import jax.numpy as jnp
from jax import lax
from jax.experimental import pallas as pl
from jax.experimental.pallas import tpu as pltpu
from jax.sharding import Mesh, PartitionSpec as P

WARMUP = 1000
smooth_sq = 0.0025
fair_alpha = 0.95

GROUPS = 4
PIECES = 16
PIECE_ROWS = 7
BIG = 48 * 1024 * 1024
VMEM = pl.BlockSpec(memory_space=pltpu.VMEM)
SMEM = pl.BlockSpec(memory_space=pltpu.SMEM)
ANY = pl.BlockSpec(memory_space=pl.ANY)
F32 = jnp.float32
BF16 = jnp.bfloat16


def soft(d):
    return d * lax.rsqrt(d * d + smooth_sq)


def as_column(row, rows):
    n = row.shape[1]
    pick = lax.broadcasted_iota(jnp.int32, (rows, n), 0) == lax.broadcasted_iota(jnp.int32, (rows, n), 1)
    return jnp.sum(jnp.where(pick, jnp.broadcast_to(row, (rows, n)), 0.0), axis=1, keepdims=True)


def padded(value, rows):
    return jnp.concatenate([value, jnp.zeros((rows - value.shape[0], value.shape[1]), value.dtype)], axis=0)


def forward_kernel(where, hidden, weight, intercept, truth, *rest):
    outs, (held, half, sem) = rest[:GROUPS], rest[GROUPS:]
    rows = half.shape[0]
    chunk = outs[0].shape[2]
    copies = []
    for k in range(GROUPS):
        start = pl.multiple_of(lax.rem(where[0] + k, GROUPS) * chunk, chunk)
        copies.append(pltpu.make_async_copy(hidden.at[:, pl.ds(start, chunk), :], held.at[k], sem.at[k]))
    for k in (2, 1, 3, 0):
        copies[k].start()
    half[...] = padded(weight[...], rows).astype(BF16)
    bias = as_column(intercept[...], rows)
    for k in (2, 1, 3, 0):
        start = pl.multiple_of(lax.rem(where[0] + k, GROUPS) * chunk, chunk)
        shift = bias - padded(truth[:, pl.ds(start, chunk)], rows)
        copies[k].wait()
        for m in range(outs[0].shape[0]):
            outs[k][m] = lax.dot_general(
                half[...], held[k, m], (((1,), (1,)), ((), ())), preferred_element_type=F32
            ) + shift


def pairs_kernel(members, *rest):
    ins, outs, (scratch,) = rest[:GROUPS], rest[GROUPS : 2 * GROUPS], rest[2 * GROUPS :]
    local = ins[0].shape[0]
    eps = (1.0 - fair_alpha) / members
    normalizer = (1.0 - eps) / (members * (members - 1))

    def tile(t, carry):
        at = pl.ds(pl.multiple_of(t * 8, 8), 8)
        r = [ins[j // local][j % local, at, :] for j in range(members)]
        total = [None] * members
        for i in range(members):
            for j in range(i + 1, members):
                s = soft(r[i] - r[j])
                total[i] = s if total[i] is None else total[i] + s
                total[j] = -s if total[j] is None else total[j] - s
        for j in range(members):
            scratch[j, at, :] = soft(r[j]) * (1.0 / members) - normalizer * total[j]
        return carry

    lax.fori_loop(0, ins[0].shape[1] // 8, tile, 0)
    for j in range(members):
        outs[j // local][j % local] = scratch[j].astype(BF16)


def area_kernel(lat, area_bin, out):
    cells, width = lat.shape
    points = area_bin.shape[1]
    bins = jnp.broadcast_to(area_bin[...], (width, points))
    level = lax.broadcasted_iota(jnp.int32, (width, points), 0)
    total = jnp.zeros((width, points), F32)
    for q in range(cells):
        column = as_column(lat[q : q + 1, :], width)
        total = total + jnp.where(bins == level + q * width, column, 0.0)
    out[...] = jnp.sum(total, axis=0, keepdims=True)


def backward_kernel(where, hidden, b0, b1, b2, b3, var, area, weighted, mine, other, held, acc, sem):
    brackets = (b0, b1, b2, b3)
    local, rows, chunk = b0.shape
    depth = local * chunk
    features = held.shape[-1]
    copies = []
    for k in range(GROUPS):
        start = pl.multiple_of(lax.rem(where[0] + k, GROUPS) * chunk, chunk)
        copies.append(pltpu.make_async_copy(hidden.at[:, pl.ds(start, chunk), :], held.at[k], sem.at[k]))
        copies[-1].start()
    scale = as_column(var[...], rows)
    ones = jnp.ones((8, depth), BF16)
    bias = jnp.zeros((8, rows), F32)
    for k in range(GROUPS):
        start = pl.multiple_of(lax.rem(where[0] + k, GROUPS) * chunk, chunk)
        point_scale = area[:, pl.ds(start, chunk)] * scale
        w = jnp.concatenate(
            [(point_scale * brackets[k][m].astype(F32)).astype(BF16) for m in range(local)], axis=1
        )
        weighted[k] = w
        bias = bias + lax.dot_general(ones, w, (((1,), (1,)), ((), ())), preferred_element_type=F32)
        copies[k].wait()
        product = jnp.dot(w, held[k].reshape(depth, features), preferred_element_type=F32)
        if k == 0:
            acc[0:rows, :] = product
        else:
            acc[0:rows, :] += product
    acc[rows:, :] = jnp.zeros((acc.shape[0] - rows, features), F32)
    half = features // 2
    total = jnp.sum(area[...], axis=1, keepdims=True)
    extra = jnp.concatenate(
        [
            bias[0:1],
            jnp.zeros((1, 128 - rows), F32),
            jnp.broadcast_to(total, (1, 128)),
            jnp.zeros((1, half - 256), F32),
        ],
        axis=1,
    )
    extra = jnp.broadcast_to(extra, (8, half))
    last = lax.broadcasted_iota(jnp.int32, (8, half), 0) == PIECE_ROWS
    for side, out in ((where[1], mine), (1 - where[1], other)):
        lanes = pl.ds(pl.multiple_of(side * half, half), half)
        for r in range(PIECES):
            out[r] = jnp.where(last, extra, acc[PIECE_ROWS * r : PIECE_ROWS * r + 8, lanes])


def grad_hidden_kernel(where, weighted, weight, piece, out, half, *, replicas):
    rows = half.shape[0]

    @pl.when(pl.program_id(0) == 0)
    def _():
        half[...] = padded(weight[...], rows).astype(BF16)

    inverse = 1.0 / (piece[PIECE_ROWS : PIECE_ROWS + 1, 128:129] * (1.0 / replicas))
    chunk = out.shape[1]
    for m in range(out.shape[0]):
        product = lax.dot_general(
            weighted[0, :, m * chunk : (m + 1) * chunk], half[...], (((0,), (0,)), ((), ())), preferred_element_type=F32
        )
        out[m] = (product * inverse).astype(BF16)


def update_kernel(where, step, own, partner, weight, intercept, new_weight, new_bias, *, replicas):
    variables, features = weight.shape
    half = features // 2
    first = where[1] == 0
    mean_area = own[0, PIECE_ROWS : PIECE_ROWS + 1, 128:129] * (1.0 / replicas)
    bias_grad = own[0, PIECE_ROWS : PIECE_ROWS + 1, 0:variables] / mean_area
    keep = lax.broadcasted_iota(jnp.int32, (8, half), 0) < PIECE_ROWS
    squares = jnp.zeros((8, half), F32)
    for r in range(PIECES):
        for side in (own, partner):
            g = jnp.where(keep, side[r] / mean_area, 0.0)
            squares = squares + g * g
    total = jnp.sum(jnp.sum(squares, axis=0, keepdims=True), axis=1, keepdims=True)
    total = total + jnp.sum(bias_grad * bias_grad, axis=1, keepdims=True)
    count = variables * features + variables
    rms = jnp.sqrt(total / count + 1e-06)
    warm = (step[0] + 1).astype(F32) / WARMUP
    scale = warm * jnp.minimum(1.0, 1.0 / rms)
    for r in range(PIECES):
        low = PIECE_ROWS * r
        n = min(PIECE_ROWS, variables - low)
        if n <= 0:
            continue
        a, b = own[r, 0:n, :], partner[r, 0:n, :]
        left, right = jnp.where(first, a, b), jnp.where(first, b, a)
        new_weight[low : low + n, :half] = weight[low : low + n, :half] - scale * (left / mean_area)
        new_weight[low : low + n, half:] = weight[low : low + n, half:] - scale * (right / mean_area)
    new_bias[...] = intercept[...] - scale * bias_grad


def on_device(hidden, decoder_weight, decoder_intercept, analysis_truth, var_weight, lat_weight, area_bin, train_step):
    local, points, features = hidden.shape
    variables = decoder_weight.shape[0]
    rows = -(-variables // 8) * 8
    chunk = points // GROUPS
    members = local * GROUPS
    replicas = points * lax.axis_size("z") * lax.axis_size("x") * lax.axis_size("c") * GROUPS
    me, core = lax.axis_index("y"), lax.axis_index("c")
    where = jnp.stack([me, core]).astype(jnp.int32)
    big = pltpu.CompilerParams(vmem_limit_bytes=BIG)
    intercept_row = decoder_intercept.reshape(1, variables)
    var_row = var_weight.reshape(1, variables)

    def turn(value, k):
        return value if k % GROUPS == 0 else lax.ppermute(value, "y", [(i, (i + k) % GROUPS) for i in range(GROUPS)])

    with jax.named_scope("forward"):
        residual = pl.pallas_call(
            forward_kernel,
            out_shape=[jax.ShapeDtypeStruct((local, rows, chunk), F32)] * GROUPS,
            in_specs=[SMEM, ANY, VMEM, VMEM, VMEM],
            out_specs=[VMEM] * GROUPS,
            scratch_shapes=[
                pltpu.VMEM((GROUPS, local, chunk, features), BF16),
                pltpu.VMEM((rows, features), BF16),
                pltpu.SemaphoreType.DMA((GROUPS,)),
            ],
            compiler_params=big,
            name="forward",
        )(where, hidden, decoder_weight, intercept_row, analysis_truth)
    with jax.named_scope("residual_exchange"):
        gathered = [residual[0], None, None, None]
        for k in (2, 1, 3):
            gathered[k] = turn(residual[k], k)
    with jax.named_scope("area"):
        area = pl.pallas_call(
            area_kernel,
            out_shape=jax.ShapeDtypeStruct((1, points), F32),
            in_specs=[VMEM, VMEM],
            out_specs=VMEM,
            name="area",
        )(lat_weight.reshape(-1, 128), area_bin.reshape(1, points))
    with jax.named_scope("pairs"):
        brackets = pl.pallas_call(
            lambda *refs: pairs_kernel(members, *refs),
            out_shape=[jax.ShapeDtypeStruct((local, rows, chunk), BF16)] * GROUPS,
            in_specs=[VMEM] * GROUPS,
            out_specs=[VMEM] * GROUPS,
            scratch_shapes=[pltpu.VMEM((members, rows, chunk), F32)],
            compiler_params=big,
            name="pairs",
        )(*gathered)
    with jax.named_scope("bracket_exchange"):
        returned = [brackets[0], None, None, None]
        for k in (2, 1, 3):
            returned[k] = turn(brackets[k], -k)
    with jax.named_scope("backward"):
        half = features // 2
        weighted, mine, other = pl.pallas_call(
            backward_kernel,
            out_shape=[
                jax.ShapeDtypeStruct((GROUPS, rows, local * chunk), BF16),
                jax.ShapeDtypeStruct((PIECES, 8, half), F32),
                jax.ShapeDtypeStruct((PIECES, 8, half), F32),
            ],
            in_specs=[SMEM, ANY] + [VMEM] * 6,
            out_specs=[VMEM] * 3,
            scratch_shapes=[
                pltpu.VMEM((GROUPS, local, chunk, features), BF16),
                pltpu.VMEM((PIECES * 8, features), F32),
                pltpu.SemaphoreType.DMA((GROUPS,)),
            ],
            compiler_params=big,
            name="backward",
        )(where, hidden, *returned, var_row, area)
    with jax.named_scope("gradient_sum"):
        swap = [(0, 1), (1, 0)]
        part = mine + lax.ppermute(other, "c", swap)
        part = lax.all_to_all(part, ("y", "x"), 0, 0, tiled=True)
        depth = lax.axis_size("z")
        part = jnp.broadcast_to(jnp.sum(part, axis=0), (depth, 8, half))
        part = lax.all_to_all(part, "z", 0, 0, tiled=True)
        piece = jnp.sum(part, axis=0)
        own = lax.all_to_all(jnp.broadcast_to(piece, (PIECES, 8, half)), ("y", "x"), 0, 0, tiled=True)
        partner = lax.ppermute(own, "c", swap)
    with jax.named_scope("grad_hidden"):
        grad_hidden = pl.pallas_call(
            lambda *refs: grad_hidden_kernel(*refs, replicas=replicas),
            out_shape=jax.ShapeDtypeStruct(hidden.shape, BF16),
            grid_spec=pltpu.PrefetchScalarGridSpec(
                num_scalar_prefetch=1,
                grid=(GROUPS,),
                in_specs=[
                    pl.BlockSpec((1, rows, local * chunk), lambda g, s: (g, 0, 0)),
                    pl.BlockSpec((variables, features), lambda g, s: (0, 0)),
                    pl.BlockSpec((8, half), lambda g, s: (0, 0)),
                ],
                out_specs=pl.BlockSpec((local, chunk, features), lambda g, s: (0, lax.rem(s[0] + g, GROUPS), 0)),
                scratch_shapes=[pltpu.VMEM((rows, features), BF16)],
            ),
            compiler_params=big,
            cost_estimate=pl.CostEstimate(
                flops=2 * rows * local * points * features, bytes_accessed=2 * hidden.size, transcendentals=0
            ),
            name="grad_hidden",
        )(where, weighted, decoder_weight, piece)
    with jax.named_scope("update"):
        new_weight, new_bias = pl.pallas_call(
            lambda *refs: update_kernel(*refs, replicas=replicas),
            out_shape=[
                jax.ShapeDtypeStruct((variables, features), F32),
                jax.ShapeDtypeStruct((1, variables), F32),
            ],
            in_specs=[SMEM, SMEM] + [VMEM] * 4,
            out_specs=[VMEM] * 2,
            compiler_params=big,
            name="update",
        )(where, train_step, own, partner, decoder_weight, intercept_row)
    return grad_hidden, new_weight, new_bias.reshape(variables)


def solution(mesh):
    fine = Mesh(mesh.devices.reshape(GROUPS, 8, 4, 2), ("y", "z", "x", "c"))
    space = ("z", "x", "c")
    return jax.shard_map(
        on_device,
        mesh=fine,
        in_specs=(P("y", space, None), P(), P(), P(None, space), P(), P(), P(space), P()),
        out_specs=(P("y", space, None), P(), P()),
        check_vma=False,
    )
```

```python
import jax
import jax.numpy as jnp
from jax import lax
from jax.experimental import pallas as pl
from jax.experimental.pallas import tpu as pltpu
from jax.sharding import Mesh, PartitionSpec as P

WARMUP = 1000
smooth_sq = 0.0025
fair_alpha = 0.95

GROUPS = 4
PIECES = 16
PIECE_ROWS = 7
MIB = 1024 * 1024
ORDER = (2, 1, 3, 0)
VMEM = pl.BlockSpec(memory_space=pltpu.VMEM)
SMEM = pl.BlockSpec(memory_space=pltpu.SMEM)
HBM = pl.BlockSpec(memory_space=pltpu.HBM)
F32 = jnp.float32
BF16 = jnp.bfloat16


def soft(d):
    return d * lax.rsqrt(d * d + smooth_sq)


def as_column(row, rows):
    n = row.shape[1]
    pick = lax.broadcasted_iota(jnp.int32, (rows, n), 0) == lax.broadcasted_iota(jnp.int32, (rows, n), 1)
    return jnp.sum(jnp.where(pick, jnp.broadcast_to(row, (rows, n)), 0.0), axis=1, keepdims=True)


def padded(value, rows):
    return jnp.concatenate([value, jnp.zeros((rows - value.shape[0], value.shape[1]), value.dtype)], axis=0)


def forward_kernel(where, hidden, weight, *rest):
    outs, half = rest[:GROUPS], rest[GROUPS]
    held, w, sem, weight_sem = rest[GROUPS + 1 :]
    rows = half.shape[0]
    chunk = outs[0].shape[2]
    fetch = pltpu.make_async_copy(weight, w, weight_sem)
    fetch.start()
    copies = {}
    for k in ORDER:
        start = pl.multiple_of(lax.rem(where[0] + k, GROUPS) * chunk, chunk)
        copies[k] = pltpu.make_async_copy(hidden.at[:, pl.ds(start, chunk), :], held.at[k], sem.at[k])
        copies[k].start()
    fetch.wait()
    half[...] = padded(w[...], rows).astype(BF16)
    for k in ORDER:
        copies[k].wait()
        for m in range(outs[0].shape[0]):
            outs[k][m] = lax.dot_general(
                half[...], held[k, m], (((1,), (1,)), ((), ())), preferred_element_type=F32
            )


def pairs_kernel(members, *rest):
    ins, shift, outs, scratch = rest[:GROUPS], rest[GROUPS], rest[GROUPS + 1 : 2 * GROUPS + 1], rest[2 * GROUPS + 1]
    local = ins[0].shape[0]
    eps = (1.0 - fair_alpha) / members
    normalizer = (1.0 - eps) / (members * (members - 1))

    def tile(t, carry):
        at = pl.ds(pl.multiple_of(t * 8, 8), 8)
        r = [ins[j // local][j % local, at, :] + shift[at, :] for j in range(members)]
        total = [None] * members
        for i in range(members):
            for j in range(i + 1, members):
                s = soft(r[i] - r[j])
                total[i] = s if total[i] is None else total[i] + s
                total[j] = -s if total[j] is None else total[j] - s
        for j in range(members):
            scratch[j, at, :] = soft(r[j]) * (1.0 / members) - normalizer * total[j]
        return carry

    lax.fori_loop(0, ins[0].shape[1] // 8, tile, 0)
    for j in range(members):
        outs[j // local][j % local] = scratch[j].astype(BF16)


def area_kernel(where, hidden, lat, area_bin, intercept, truth, out, shift, held, sem):
    chunk = held.shape[2]
    copies = []
    for k in range(GROUPS):
        start = pl.multiple_of(lax.rem(where[0] + k, GROUPS) * chunk, chunk)
        copies.append(pltpu.make_async_copy(hidden.at[:, pl.ds(start, chunk), :], held.at[k], sem.at[k]))
        copies[k].start()
    cells, width = lat.shape
    points = area_bin.shape[1]
    bins = jnp.broadcast_to(area_bin[...], (width, points))
    level = lax.broadcasted_iota(jnp.int32, (width, points), 0)
    total = jnp.zeros((width, points), F32)
    for q in range(cells):
        column = as_column(lat[q : q + 1, :], width)
        total = total + jnp.where(bins == level + q * width, column, 0.0)
    out[...] = jnp.sum(total, axis=0, keepdims=True)
    mine = pl.multiple_of(where[0] * chunk, chunk)
    shift[...] = as_column(intercept[...], shift.shape[0]) - padded(truth[:, pl.ds(mine, chunk)], shift.shape[0])
    for copy in copies:
        copy.wait()


def backward_kernel(where, held, b0, b1, b2, b3, var, area, weighted, mine, other, acc):
    brackets = (b0, b1, b2, b3)
    local, rows, chunk = b0.shape
    depth = local * chunk
    features = held.shape[-1]
    scale = as_column(var[...], rows)
    ones = jnp.ones((8, depth), BF16)
    bias = jnp.zeros((8, rows), F32)
    for k in range(GROUPS):
        start = pl.multiple_of(lax.rem(where[0] + k, GROUPS) * chunk, chunk)
        point_scale = area[:, pl.ds(start, chunk)] * scale
        w = jnp.concatenate(
            [(point_scale * brackets[k][m].astype(F32)).astype(BF16) for m in range(local)], axis=1
        )
        weighted[k] = w
        bias = bias + lax.dot_general(ones, w, (((1,), (1,)), ((), ())), preferred_element_type=F32)
        product = jnp.dot(w, held[k].reshape(depth, features), preferred_element_type=F32)
        if k == 0:
            acc[0:rows, :] = product
        else:
            acc[0:rows, :] += product
    acc[rows:, :] = jnp.zeros((acc.shape[0] - rows, features), F32)
    half = features // 2
    total = jnp.sum(area[...], axis=1, keepdims=True)
    extra = jnp.concatenate(
        [
            bias[0:1],
            jnp.zeros((1, 128 - rows), F32),
            jnp.broadcast_to(total, (1, 128)),
            jnp.zeros((1, half - 256), F32),
        ],
        axis=1,
    )
    extra = jnp.broadcast_to(extra, (8, half))
    last = lax.broadcasted_iota(jnp.int32, (8, half), 0) == PIECE_ROWS
    for side, out in ((where[1], mine), (1 - where[1], other)):
        lanes = pl.ds(pl.multiple_of(side * half, half), half)
        for r in range(PIECES):
            out[r] = jnp.where(last, extra, acc[PIECE_ROWS * r : PIECE_ROWS * r + 8, lanes])


def grad_hidden_kernel(where, weighted, half, piece, out, *, replicas):
    inverse = 1.0 / (piece[PIECE_ROWS : PIECE_ROWS + 1, 128:129] * (1.0 / replicas))
    chunk = out.shape[1]
    for m in range(out.shape[0]):
        product = lax.dot_general(
            weighted[0, :, m * chunk : (m + 1) * chunk], half[...], (((0,), (0,)), ((), ())), preferred_element_type=F32
        )
        out[m] = (product * inverse).astype(BF16)


def update_kernel(where, step, own, partner, weight, intercept, new_weight, new_bias, *, replicas):
    variables, features = weight.shape
    half = features // 2
    first = where[1] == 0
    mean_area = own[0, PIECE_ROWS : PIECE_ROWS + 1, 128:129] * (1.0 / replicas)
    inverse = 1.0 / mean_area
    bias_grad = own[0, PIECE_ROWS : PIECE_ROWS + 1, 0:variables] * inverse
    keep = lax.broadcasted_iota(jnp.int32, (8, half), 0) < PIECE_ROWS
    squares = jnp.zeros((8, half), F32)
    for r in range(PIECES):
        for side in (own, partner):
            g = jnp.where(keep, side[r] * inverse, 0.0)
            squares = squares + g * g
    total = jnp.sum(jnp.sum(squares, axis=0, keepdims=True), axis=1, keepdims=True)
    total = total + jnp.sum(bias_grad * bias_grad, axis=1, keepdims=True)
    count = variables * features + variables
    rms = jnp.sqrt(total / count + 1e-06)
    warm = (step[0] + 1).astype(F32) / WARMUP
    scale = warm * jnp.minimum(1.0, 1.0 / rms)
    for r in range(PIECES):
        low = PIECE_ROWS * r
        n = min(PIECE_ROWS, variables - low)
        if n <= 0:
            continue
        a, b = own[r, 0:n, :], partner[r, 0:n, :]
        left, right = jnp.where(first, a, b), jnp.where(first, b, a)
        new_weight[low : low + n, :half] = weight[low : low + n, :half] - scale * (left * inverse)
        new_weight[low : low + n, half:] = weight[low : low + n, half:] - scale * (right * inverse)
    new_bias[...] = intercept[...] - scale * bias_grad


def on_device(hidden, decoder_weight, decoder_intercept, analysis_truth, var_weight, lat_weight, area_bin, train_step):
    local, points, features = hidden.shape
    variables = decoder_weight.shape[0]
    rows = -(-variables // 8) * 8
    chunk = points // GROUPS
    members = local * GROUPS
    replicas = points * lax.axis_size("z") * lax.axis_size("x") * lax.axis_size("c") * GROUPS
    me, core = lax.axis_index("y"), lax.axis_index("c")
    where = jnp.stack([me, core]).astype(jnp.int32)

    def grant(mib):
        return pltpu.CompilerParams(vmem_limit_bytes=mib * MIB)

    intercept_row = decoder_intercept.reshape(1, variables)
    var_row = var_weight.reshape(1, variables)

    def turn(value, k):
        return value if k % GROUPS == 0 else lax.ppermute(value, "y", [(i, (i + k) % GROUPS) for i in range(GROUPS)])

    with jax.named_scope("forward"):
        *residual, half_weight = pl.pallas_call(
            forward_kernel,
            out_shape=[jax.ShapeDtypeStruct((local, rows, chunk), F32)] * GROUPS
            + [jax.ShapeDtypeStruct((rows, features), BF16)],
            in_specs=[SMEM, HBM, HBM],
            out_specs=[VMEM] * (GROUPS + 1),
            scratch_shapes=[
                pltpu.VMEM((GROUPS, local, chunk, features), BF16),
                pltpu.VMEM((variables, features), F32),
                pltpu.SemaphoreType.DMA((GROUPS,)),
                pltpu.SemaphoreType.DMA(()),
            ],
            compiler_params=grant(53),
            name="forward",
        )(where, hidden, decoder_weight)
    with jax.named_scope("residual_exchange"):
        gathered = [residual[0], None, None, None]
        for k in ORDER[:-1]:
            gathered[k] = turn(residual[k], k)
    with jax.named_scope("area"):
        area, shift, held = pl.pallas_call(
            area_kernel,
            out_shape=[
                jax.ShapeDtypeStruct((1, points), F32),
                jax.ShapeDtypeStruct((rows, chunk), F32),
                jax.ShapeDtypeStruct((GROUPS, local, chunk, features), BF16),
            ],
            in_specs=[SMEM, HBM] + [VMEM] * 4,
            out_specs=[VMEM] * 3,
            scratch_shapes=[pltpu.SemaphoreType.DMA((GROUPS,))],
            compiler_params=grant(46),
            name="area",
        )(where, hidden, lat_weight.reshape(-1, 128), area_bin.reshape(1, points), intercept_row, analysis_truth)
        gathered, area, shift, held = lax.optimization_barrier((gathered, area, shift, held))
    with jax.named_scope("pairs"):
        brackets = pl.pallas_call(
            lambda *refs: pairs_kernel(members, *refs),
            out_shape=[jax.ShapeDtypeStruct((local, rows, chunk), BF16)] * GROUPS,
            in_specs=[VMEM] * (GROUPS + 1),
            out_specs=[VMEM] * GROUPS,
            scratch_shapes=[pltpu.VMEM((members, rows, chunk), F32)],
            compiler_params=grant(6),
            name="pairs",
        )(*gathered, shift)
    with jax.named_scope("bracket_exchange"):
        returned = [brackets[0], None, None, None]
        for k in ORDER[:-1]:
            returned[k] = turn(brackets[k], -k)
    with jax.named_scope("backward"):
        half = features // 2
        weighted, mine, other = pl.pallas_call(
            backward_kernel,
            out_shape=[
                jax.ShapeDtypeStruct((GROUPS, rows, local * chunk), BF16),
                jax.ShapeDtypeStruct((PIECES, 8, half), F32),
                jax.ShapeDtypeStruct((PIECES, 8, half), F32),
            ],
            in_specs=[SMEM] + [VMEM] * 7,
            out_specs=[VMEM] * 3,
            scratch_shapes=[pltpu.VMEM((PIECES * 8, features), F32)],
            compiler_params=grant(8),
            name="backward",
        )(where, held, *returned, var_row, area)
    with jax.named_scope("gradient_sum"):
        swap = [(0, 1), (1, 0)]
        part = mine + lax.ppermute(other, "c", swap)
        part = lax.all_to_all(part, ("y", "x"), 0, 0, tiled=True)
        depth = lax.axis_size("z")
        part = jnp.broadcast_to(jnp.sum(part, axis=0), (depth, 8, half))
        part = lax.all_to_all(part, "z", 0, 0, tiled=True)
        piece = jnp.sum(part, axis=0)
        own = lax.all_to_all(jnp.broadcast_to(piece, (PIECES, 8, half)), ("y", "x"), 0, 0, tiled=True)
    with jax.named_scope("grad_hidden"):
        grad_hidden = pl.pallas_call(
            lambda *refs: grad_hidden_kernel(*refs, replicas=replicas),
            out_shape=jax.ShapeDtypeStruct(hidden.shape, BF16),
            grid_spec=pltpu.PrefetchScalarGridSpec(
                num_scalar_prefetch=1,
                grid=(GROUPS,),
                in_specs=[
                    pl.BlockSpec((1, rows, local * chunk), lambda g, s: (g, 0, 0)),
                    pl.BlockSpec((rows, features), lambda g, s: (0, 0)),
                    pl.BlockSpec((8, half), lambda g, s: (0, 0)),
                ],
                out_specs=pl.BlockSpec((local, chunk, features), lambda g, s: (0, lax.rem(s[0] + g, GROUPS), 0)),
            ),
            compiler_params=grant(12),
            cost_estimate=pl.CostEstimate(
                flops=2 * rows * local * points * features, bytes_accessed=2 * hidden.size, transcendentals=0
            ),
            name="grad_hidden",
        )(where, weighted, half_weight, piece)
        own, grad_hidden = lax.optimization_barrier((own, grad_hidden))
    with jax.named_scope("last_swap"):
        partner = lax.ppermute(own, "c", swap)
    with jax.named_scope("update"):
        new_weight, new_bias = pl.pallas_call(
            lambda *refs: update_kernel(*refs, replicas=replicas),
            out_shape=[
                jax.ShapeDtypeStruct((variables, features), F32),
                jax.ShapeDtypeStruct((1, variables), F32),
            ],
            in_specs=[SMEM, SMEM] + [VMEM] * 4,
            out_specs=[VMEM] * 2,
            compiler_params=grant(6),
            name="update",
        )(where, train_step, own, partner, decoder_weight, intercept_row)
    return grad_hidden, new_weight, new_bias.reshape(variables)


def solution(mesh):
    fine = Mesh(mesh.devices.reshape(GROUPS, 8, 4, 2), ("y", "z", "x", "c"))
    space = ("z", "x", "c")
    return jax.shard_map(
        on_device,
        mesh=fine,
        in_specs=(P("y", space, None), P(), P(), P(None, space), P(), P(), P(space), P()),
        out_specs=(P("y", space, None), P(), P()),
        check_vma=False,
    )
```

```python
import jax
import jax.numpy as jnp
from jax import lax
from jax.experimental import pallas as pl
from jax.experimental.pallas import tpu as pltpu
from jax.sharding import Mesh, PartitionSpec as P

WARMUP = 1000
smooth_sq = 0.0025
fair_alpha = 0.95

GROUPS = 4
PIECES = 16
PIECE_ROWS = 7
MIB = 1024 * 1024
VMEM = pl.BlockSpec(memory_space=pltpu.VMEM)
SMEM = pl.BlockSpec(memory_space=pltpu.SMEM)
HBM = pl.BlockSpec(memory_space=pltpu.HBM)
F32 = jnp.float32
BF16 = jnp.bfloat16


def soft(d):
    return d * lax.rsqrt(d * d + smooth_sq)


def as_column(row, rows):
    n = row.shape[1]
    pick = lax.broadcasted_iota(jnp.int32, (rows, n), 0) == lax.broadcasted_iota(jnp.int32, (rows, n), 1)
    return jnp.sum(jnp.where(pick, jnp.broadcast_to(row, (rows, n)), 0.0), axis=1, keepdims=True)


def padded(value, rows):
    return jnp.concatenate([value, jnp.zeros((rows - value.shape[0], value.shape[1]), value.dtype)], axis=0)


def decode(half, features, out):
    for m in range(out.shape[0]):
        out[m] = lax.dot_general(half[...], features[m], (((1,), (1,)), ((), ())), preferred_element_type=F32)


def fetch_chunks(where, hidden, held, sem, ks):
    chunk = held.shape[2]
    copies = []
    for slot, k in enumerate(ks):
        start = pl.multiple_of(lax.rem(where[0] + k, GROUPS) * chunk, chunk)
        copies.append(pltpu.make_async_copy(hidden.at[:, pl.ds(start, chunk), :], held.at[slot], sem.at[slot]))
        copies[slot].start()
    return copies


def far_kernel(where, hidden, weight, out, half, held, w, sem, weight_sem):
    fetch = pltpu.make_async_copy(weight, w, weight_sem)
    fetch.start()
    copies = fetch_chunks(where, hidden, held, sem, (2,))
    fetch.wait()
    half[...] = padded(w[...], half.shape[0]).astype(BF16)
    copies[0].wait()
    decode(half, held.at[0], out)


def near_kernel(where, hidden, half, after, before, held, sem):
    copies = fetch_chunks(where, hidden, held, sem, (1, 3))
    for slot, out in enumerate((after, before)):
        copies[slot].wait()
        decode(half, held.at[slot], out)


def add_pair(total, i, j, s):
    total[i] = s if total[i] is None else total[i] + s
    total[j] = -s if total[j] is None else total[j] - s


def early_pairs_kernel(here, far, shift, out):
    local = here.shape[0]
    count = 2 * local

    def tile(t, carry):
        at = pl.ds(pl.multiple_of(t * 8, 8), 8)
        r = [ref[j, at, :] + shift[at, :] for ref in (here, far) for j in range(local)]
        total = [None] * count
        for i in range(count):
            for j in range(i + 1, count):
                add_pair(total, i, j, soft(r[i] - r[j]))
        for j in range(count):
            out[j, at, :] = total[j]
        return carry

    lax.fori_loop(0, here.shape[1] // 8, tile, 0)


def late_pairs_kernel(members, here, far, after, before, shift, early, *rest):
    ins, outs, scratch = (here, far, after, before), rest[:GROUPS], rest[GROUPS]
    local = here.shape[0]
    count = early.shape[0]
    eps = (1.0 - fair_alpha) / members
    normalizer = (1.0 - eps) / (members * (members - 1))

    def tile(t, carry):
        at = pl.ds(pl.multiple_of(t * 8, 8), 8)
        r = [ref[j, at, :] + shift[at, :] for ref in ins for j in range(local)]
        total = [early[j, at, :] for j in range(count)] + [None] * (members - count)
        for i in range(members):
            for j in range(max(i + 1, count), members):
                add_pair(total, i, j, soft(r[i] - r[j]))
        for j in range(members):
            scratch[j, at, :] = soft(r[j]) * (1.0 / members) - normalizer * total[j]
        return carry

    lax.fori_loop(0, here.shape[1] // 8, tile, 0)
    for j in range(members):
        outs[j // local][j % local] = scratch[j].astype(BF16)


def local_kernel(where, hidden, half, lat, area_bin, intercept, truth, out, area, shift, held, sem):
    chunk = held.shape[2]
    copies = fetch_chunks(where, hidden, held, sem, range(GROUPS))
    cells, width = lat.shape
    points = area_bin.shape[1]
    bins = jnp.broadcast_to(area_bin[...], (width, points))
    level = lax.broadcasted_iota(jnp.int32, (width, points), 0)
    total = jnp.zeros((width, points), F32)
    for q in range(cells):
        column = as_column(lat[q : q + 1, :], width)
        total = total + jnp.where(bins == level + q * width, column, 0.0)
    area[...] = jnp.sum(total, axis=0, keepdims=True)
    mine = pl.multiple_of(where[0] * chunk, chunk)
    shift[...] = as_column(intercept[...], shift.shape[0]) - padded(truth[:, pl.ds(mine, chunk)], shift.shape[0])
    copies[0].wait()
    decode(half, held.at[0], out)
    for copy in copies[1:]:
        copy.wait()


def pieces_of(acc, extra, out):
    last = lax.broadcasted_iota(jnp.int32, out.shape[1:], 0) == PIECE_ROWS
    for r in range(PIECES):
        out[r] = jnp.where(last, extra, acc[PIECE_ROWS * r : PIECE_ROWS * r + 8, :])


def gradient_half(side, weighted, held, acc):
    _, rows, depth = weighted.shape
    half = acc.shape[1]
    lanes = pl.ds(pl.multiple_of(side * half, half), half)
    total = None
    for k in range(GROUPS):
        part = jnp.dot(weighted[k], held[k, :, :, lanes].reshape(depth, half), preferred_element_type=F32)
        total = part if total is None else total + part
    acc[0:rows, :] = total
    acc[rows:, :] = jnp.zeros((acc.shape[0] - rows, half), F32)


def partner_half_kernel(where, held, b0, b1, b2, b3, var, area, weighted, extra_out, other, acc):
    brackets = (b0, b1, b2, b3)
    local, rows, chunk = b0.shape
    depth = local * chunk
    half = acc.shape[1]
    scale = as_column(var[...], rows)
    ones = jnp.ones((8, depth), BF16)
    bias = jnp.zeros((8, rows), F32)
    for k in range(GROUPS):
        start = pl.multiple_of(lax.rem(where[0] + k, GROUPS) * chunk, chunk)
        point_scale = area[:, pl.ds(start, chunk)] * scale
        w = jnp.concatenate(
            [(point_scale * brackets[k][m].astype(F32)).astype(BF16) for m in range(local)], axis=1
        )
        weighted[k] = w
        bias = bias + lax.dot_general(ones, w, (((1,), (1,)), ((), ())), preferred_element_type=F32)
    gradient_half(1 - where[1], weighted, held, acc)
    total = jnp.sum(area[...], axis=1, keepdims=True)
    extra = jnp.concatenate(
        [
            bias[0:1],
            jnp.zeros((1, 128 - rows), F32),
            jnp.broadcast_to(total, (1, 128)),
            jnp.zeros((1, half - 256), F32),
        ],
        axis=1,
    )
    extra_out[...] = jnp.broadcast_to(extra, (8, half))
    pieces_of(acc, extra_out[...], other)


def own_half_kernel(where, held, weighted, extra, mine, acc):
    gradient_half(where[1], weighted, held, acc)
    pieces_of(acc, extra[...], mine)


def grad_hidden_kernel(where, weighted, half, piece, out, *, replicas):
    inverse = 1.0 / (piece[PIECE_ROWS : PIECE_ROWS + 1, 128:129] * (1.0 / replicas))
    chunk = out.shape[1]
    for m in range(out.shape[0]):
        product = lax.dot_general(
            weighted[0, :, m * chunk : (m + 1) * chunk], half[...], (((0,), (0,)), ((), ())), preferred_element_type=F32
        )
        out[m] = (product * inverse).astype(BF16)


def squares_of(pieces, inverse):
    half = pieces.shape[2]
    keep = lax.broadcasted_iota(jnp.int32, (8, half), 0) < PIECE_ROWS
    squares = jnp.zeros((8, half), F32)
    for r in range(PIECES):
        g = jnp.where(keep, pieces[r] * inverse, 0.0)
        squares = squares + g * g
    return squares


def squares_kernel(own, out, *, replicas):
    inverse = 1.0 / (own[0, PIECE_ROWS : PIECE_ROWS + 1, 128:129] * (1.0 / replicas))
    out[...] = squares_of(own, inverse)


def update_kernel(where, step, own, partner, squares, weight, intercept, new_weight, new_bias, *, replicas):
    variables, features = weight.shape
    half = features // 2
    first = where[1] == 0
    mean_area = own[0, PIECE_ROWS : PIECE_ROWS + 1, 128:129] * (1.0 / replicas)
    inverse = 1.0 / mean_area
    bias_grad = own[0, PIECE_ROWS : PIECE_ROWS + 1, 0:variables] * inverse
    a, b = squares[...], squares_of(partner, inverse)
    both = jnp.where(first, a, b) + jnp.where(first, b, a)
    total = jnp.sum(jnp.sum(both, axis=0, keepdims=True), axis=1, keepdims=True)
    total = total + jnp.sum(bias_grad * bias_grad, axis=1, keepdims=True)
    count = variables * features + variables
    rms = jnp.sqrt(total / count + 1e-06)
    warm = (step[0] + 1).astype(F32) / WARMUP
    scale = warm * jnp.minimum(1.0, 1.0 / rms)
    for r in range(PIECES):
        low = PIECE_ROWS * r
        n = min(PIECE_ROWS, variables - low)
        if n <= 0:
            continue
        a, b = own[r, 0:n, :], partner[r, 0:n, :]
        left, right = jnp.where(first, a, b), jnp.where(first, b, a)
        new_weight[low : low + n, :half] = weight[low : low + n, :half] - scale * (left * inverse)
        new_weight[low : low + n, half:] = weight[low : low + n, half:] - scale * (right * inverse)
    new_bias[...] = intercept[...] - scale * bias_grad


def on_device(hidden, decoder_weight, decoder_intercept, analysis_truth, var_weight, lat_weight, area_bin, train_step):
    local, points, features = hidden.shape
    variables = decoder_weight.shape[0]
    rows = -(-variables // 8) * 8
    chunk = points // GROUPS
    members = local * GROUPS
    replicas = points * lax.axis_size("z") * lax.axis_size("x") * lax.axis_size("c") * GROUPS
    me, core = lax.axis_index("y"), lax.axis_index("c")
    where = jnp.stack([me, core]).astype(jnp.int32)

    def grant(mib):
        return pltpu.CompilerParams(vmem_limit_bytes=int(mib * MIB))

    intercept_row = decoder_intercept.reshape(1, variables)
    var_row = var_weight.reshape(1, variables)

    def turn(value, k):
        return value if k % GROUPS == 0 else lax.ppermute(value, "y", [(i, (i + k) % GROUPS) for i in range(GROUPS)])

    one_residual = jax.ShapeDtypeStruct((local, rows, chunk), F32)
    with jax.named_scope("forward_far"):
        far, half_weight = pl.pallas_call(
            far_kernel,
            out_shape=[one_residual, jax.ShapeDtypeStruct((rows, features), BF16)],
            in_specs=[SMEM, HBM, HBM],
            out_specs=[VMEM] * 2,
            scratch_shapes=[
                pltpu.VMEM((1, local, chunk, features), BF16),
                pltpu.VMEM((variables, features), F32),
                pltpu.SemaphoreType.DMA((1,)),
                pltpu.SemaphoreType.DMA(()),
            ],
            compiler_params=grant(53.4),
            name="forward_far",
        )(where, hidden, decoder_weight)
        far = turn(far, 2)
    with jax.named_scope("forward_near"):
        after, before = pl.pallas_call(
            near_kernel,
            out_shape=[one_residual] * 2,
            in_specs=[SMEM, HBM, VMEM],
            out_specs=[VMEM] * 2,
            scratch_shapes=[
                pltpu.VMEM((2, local, chunk, features), BF16),
                pltpu.SemaphoreType.DMA((2,)),
            ],
            compiler_params=grant(52),
            cost_estimate=pl.CostEstimate(
                flops=4 * rows * local * chunk * features, bytes_accessed=4 * local * chunk * features, transcendentals=0
            ),
            name="forward_near",
        )(where, hidden, half_weight)
        after, before = turn(after, 1), turn(before, 3)
    with jax.named_scope("forward_local"):
        here, area, shift, held = pl.pallas_call(
            local_kernel,
            out_shape=[
                one_residual,
                jax.ShapeDtypeStruct((1, points), F32),
                jax.ShapeDtypeStruct((rows, chunk), F32),
                jax.ShapeDtypeStruct((GROUPS, local, chunk, features), BF16),
            ],
            in_specs=[SMEM, HBM] + [VMEM] * 5,
            out_specs=[VMEM] * 4,
            scratch_shapes=[pltpu.SemaphoreType.DMA((GROUPS,))],
            compiler_params=grant(46),
            name="forward_local",
        )(where, hidden, half_weight, lat_weight.reshape(-1, 128), area_bin.reshape(1, points), intercept_row, analysis_truth)
    with jax.named_scope("early_pairs"):
        early = pl.pallas_call(
            early_pairs_kernel,
            out_shape=jax.ShapeDtypeStruct((2 * local, rows, chunk), F32),
            in_specs=[VMEM] * 3,
            out_specs=VMEM,
            compiler_params=grant(4),
            name="early_pairs",
        )(here, far, shift)
    after, before, early, area, held = lax.optimization_barrier((after, before, early, area, held))
    with jax.named_scope("late_pairs"):
        brackets = pl.pallas_call(
            lambda *refs: late_pairs_kernel(members, *refs),
            out_shape=[jax.ShapeDtypeStruct((local, rows, chunk), BF16)] * GROUPS,
            in_specs=[VMEM] * (GROUPS + 2),
            out_specs=[VMEM] * GROUPS,
            scratch_shapes=[pltpu.VMEM((members, rows, chunk), F32)],
            compiler_params=grant(6),
            name="late_pairs",
        )(here, far, after, before, shift, early)
    with jax.named_scope("bracket_exchange"):
        returned = [brackets[0], turn(brackets[2], -1), turn(brackets[1], -2), turn(brackets[3], -3)]
    half = features // 2
    pieces = jax.ShapeDtypeStruct((PIECES, 8, half), F32)
    sums = [pltpu.VMEM((PIECES * 8, half), F32)]
    with jax.named_scope("backward_partner_half"):
        weighted, extra, other = pl.pallas_call(
            partner_half_kernel,
            out_shape=[
                jax.ShapeDtypeStruct((GROUPS, rows, local * chunk), BF16),
                jax.ShapeDtypeStruct((8, half), F32),
                pieces,
            ],
            in_specs=[SMEM] + [VMEM] * 7,
            out_specs=[VMEM] * 3,
            scratch_shapes=sums,
            compiler_params=grant(8),
            name="backward_partner_half",
        )(where, held, *returned, var_row, area)
        swap = [(0, 1), (1, 0)]
        other = lax.ppermute(other, "c", swap)
    with jax.named_scope("backward_own_half"):
        mine = pl.pallas_call(
            own_half_kernel,
            out_shape=pieces,
            in_specs=[SMEM] + [VMEM] * 3,
            out_specs=VMEM,
            scratch_shapes=sums,
            compiler_params=grant(8),
            name="backward_own_half",
        )(where, held, weighted, extra)
    with jax.named_scope("gradient_sum"):
        part = mine + other
        part = lax.all_to_all(part, ("x", "y"), 0, 0, tiled=True)
        depth = lax.axis_size("z")
        part = jnp.broadcast_to(jnp.sum(part, axis=0), (depth, 8, half))
        part = lax.all_to_all(part, "z", 0, 0, tiled=True)
        piece = jnp.sum(part, axis=0)
        own = lax.all_to_all(jnp.broadcast_to(piece, (PIECES, 8, half)), ("x", "y"), 0, 0, tiled=True)
    with jax.named_scope("grad_hidden"):
        grad_hidden = pl.pallas_call(
            lambda *refs: grad_hidden_kernel(*refs, replicas=replicas),
            out_shape=jax.ShapeDtypeStruct(hidden.shape, BF16),
            grid_spec=pltpu.PrefetchScalarGridSpec(
                num_scalar_prefetch=1,
                grid=(GROUPS,),
                in_specs=[
                    pl.BlockSpec((1, rows, local * chunk), lambda g, s: (g, 0, 0)),
                    pl.BlockSpec((rows, features), lambda g, s: (0, 0)),
                    pl.BlockSpec((8, half), lambda g, s: (0, 0)),
                ],
                out_specs=pl.BlockSpec((local, chunk, features), lambda g, s: (0, lax.rem(s[0] + g, GROUPS), 0)),
            ),
            compiler_params=grant(12),
            cost_estimate=pl.CostEstimate(
                flops=2 * rows * local * points * features, bytes_accessed=2 * hidden.size, transcendentals=0
            ),
            name="grad_hidden",
        )(where, weighted, half_weight, piece)
        own, grad_hidden = lax.optimization_barrier((own, grad_hidden))
    with jax.named_scope("last_swap"):
        partner = lax.ppermute(own, "c", swap)
        squares = pl.pallas_call(
            lambda *refs: squares_kernel(*refs, replicas=replicas),
            out_shape=jax.ShapeDtypeStruct((8, half), F32),
            in_specs=[VMEM],
            out_specs=VMEM,
            compiler_params=grant(4),
            name="squares",
        )(own)
    with jax.named_scope("update"):
        new_weight, new_bias = pl.pallas_call(
            lambda *refs: update_kernel(*refs, replicas=replicas),
            out_shape=[
                jax.ShapeDtypeStruct((variables, features), F32),
                jax.ShapeDtypeStruct((1, variables), F32),
            ],
            in_specs=[SMEM, SMEM] + [VMEM] * 5,
            out_specs=[VMEM] * 2,
            compiler_params=grant(6),
            name="update",
        )(where, train_step, own, partner, squares, decoder_weight, intercept_row)
    return grad_hidden, new_weight, new_bias.reshape(variables)


def solution(mesh):
    fine = Mesh(mesh.devices.reshape(GROUPS, 8, 4, 2), ("y", "z", "x", "c"))
    space = ("z", "x", "c")
    return jax.shard_map(
        on_device,
        mesh=fine,
        in_specs=(P("y", space, None), P(), P(), P(None, space), P(), P(), P(space), P()),
        out_specs=(P("y", space, None), P(), P()),
        check_vma=False,
    )
```

```python
import jax
import jax.numpy as jnp
from jax import lax
from jax.experimental import pallas as pl
from jax.experimental.pallas import tpu as pltpu
from jax.sharding import Mesh, PartitionSpec as P

WARMUP = 1000
smooth_sq = 0.0025
fair_alpha = 0.95

GROUPS = 4
PIECES = 16
PIECE_ROWS = 7
MIB = 1024 * 1024
VMEM = pl.BlockSpec(memory_space=pltpu.VMEM)
SMEM = pl.BlockSpec(memory_space=pltpu.SMEM)
HBM = pl.BlockSpec(memory_space=pltpu.HBM)
F32 = jnp.float32
BF16 = jnp.bfloat16


def soft(d):
    return d * lax.rsqrt(d * d + smooth_sq)


def as_column(row, rows):
    n = row.shape[1]
    pick = lax.broadcasted_iota(jnp.int32, (rows, n), 0) == lax.broadcasted_iota(jnp.int32, (rows, n), 1)
    return jnp.sum(jnp.where(pick, jnp.broadcast_to(row, (rows, n)), 0.0), axis=1, keepdims=True)


def padded(value, rows):
    return jnp.concatenate([value, jnp.zeros((rows - value.shape[0], value.shape[1]), value.dtype)], axis=0)


def decode(half, features):
    return lax.dot_general(half[...], features, (((1,), (1,)), ((), ())), preferred_element_type=F32)


def fetch_chunks(where, hidden, held, sem, ks):
    local, chunk = held.shape[1:3]
    copies = []
    for slot, k in enumerate(ks):
        start = pl.multiple_of(lax.rem(where[0] + k, GROUPS) * chunk, chunk)
        copies.append(
            [
                pltpu.make_async_copy(hidden.at[m, pl.ds(start, chunk), :], held.at[slot, m], sem.at[slot, m])
                for m in range(local)
            ]
        )
        for copy in copies[slot]:
            copy.start()
    return copies


def far_kernel(where, hidden, weight, out, half, held, w, sem, weight_sem):
    fetch = pltpu.make_async_copy(weight, w, weight_sem)
    fetch.start()
    (copies,) = fetch_chunks(where, hidden, held, sem, (2,))
    fetch.wait()
    half[...] = padded(w[...], half.shape[0]).astype(BF16)
    for m, copy in enumerate(copies):
        copy.wait()
        out[m] = decode(half, held[0, m])


def near_kernel(where, hidden, half, after, before, held, sem):
    copies = fetch_chunks(where, hidden, held, sem, (1, 3))
    for slot, out in enumerate((after, before)):
        for m, copy in enumerate(copies[slot]):
            copy.wait()
            out[m] = decode(half, held[slot, m])


def add_pair(total, i, j, s):
    total[i] = s if total[i] is None else total[i] + s
    total[j] = -s if total[j] is None else total[j] - s


def early_pairs_kernel(here, far, shift, out):
    local = here.shape[0]
    count = 2 * local

    def tile(t, carry):
        at = pl.ds(pl.multiple_of(t * 8, 8), 8)
        r = [ref[j, at, :] + shift[at, :] for ref in (here, far) for j in range(local)]
        total = [None] * count
        for i in range(count):
            for j in range(i + 1, count):
                add_pair(total, i, j, soft(r[i] - r[j]))
        for j in range(count):
            out[j, at, :] = total[j]
        return carry

    lax.fori_loop(0, here.shape[1] // 8, tile, 0)


def late_pairs_kernel(members, here, far, after, before, shift, early, *rest):
    ins, outs, scratch = (here, far, after, before), rest[:GROUPS], rest[GROUPS]
    local = here.shape[0]
    count = early.shape[0]
    eps = (1.0 - fair_alpha) / members
    normalizer = (1.0 - eps) / (members * (members - 1))

    def tile(t, carry):
        at = pl.ds(pl.multiple_of(t * 8, 8), 8)
        r = [ref[j, at, :] + shift[at, :] for ref in ins for j in range(local)]
        total = [early[j, at, :] for j in range(count)] + [None] * (members - count)
        for i in range(members):
            for j in range(max(i + 1, count), members):
                add_pair(total, i, j, soft(r[i] - r[j]))
        for j in range(members):
            scratch[j, at, :] = soft(r[j]) * (1.0 / members) - normalizer * total[j]
        return carry

    lax.fori_loop(0, here.shape[1] // 8, tile, 0)
    for j in range(members):
        outs[j // local][j % local] = scratch[j].astype(BF16)


def local_kernel(where, hidden, half, lat, area_bin, intercept, truth, out, area, shift, held, sem):
    chunk = held.shape[2]
    copies = fetch_chunks(where, hidden, held, sem, range(GROUPS))
    cells, width = lat.shape
    points = area_bin.shape[1]
    bins = jnp.broadcast_to(area_bin[...], (width, points))
    level = lax.broadcasted_iota(jnp.int32, (width, points), 0)
    total = jnp.zeros((width, points), F32)
    for q in range(cells):
        column = as_column(lat[q : q + 1, :], width)
        total = total + jnp.where(bins == level + q * width, column, 0.0)
    area[...] = jnp.sum(total, axis=0, keepdims=True)
    mine = pl.multiple_of(where[0] * chunk, chunk)
    shift[...] = as_column(intercept[...], shift.shape[0]) - padded(truth[:, pl.ds(mine, chunk)], shift.shape[0])
    for m, copy in enumerate(copies[0]):
        copy.wait()
        out[m] = decode(half, held[0, m])
    for chunk_copies in copies[1:]:
        for copy in chunk_copies:
            copy.wait()


def pieces_of(acc, extra, out):
    last = lax.broadcasted_iota(jnp.int32, out.shape[1:], 0) == PIECE_ROWS
    for r in range(PIECES):
        out[r] = jnp.where(last, extra, acc[PIECE_ROWS * r : PIECE_ROWS * r + 8, :])


def weigh(where, k, bracket, area, scale):
    local, _, chunk = bracket.shape
    start = pl.multiple_of(lax.rem(where[0] + k, GROUPS) * chunk, chunk)
    point_scale = area[:, pl.ds(start, chunk)] * scale
    return jnp.concatenate([(point_scale * bracket[m].astype(F32)).astype(BF16) for m in range(local)], axis=1)


def bias_of(w):
    ones = jnp.ones((8, w.shape[1]), BF16)
    return lax.dot_general(ones, w, (((1,), (1,)), ((), ())), preferred_element_type=F32)


def early_backward_kernel(where, held, b0, b1, var, area, weighted, total, bias):
    local, rows, chunk = b0.shape
    depth, features = local * chunk, total.shape[1]
    scale = as_column(var[...], rows)
    w0 = weigh(where, 0, b0, area, scale)
    w1 = weigh(where, 1, b1, area, scale)
    weighted[0], weighted[1] = w0, w1
    bias[...] = bias_of(w0) + bias_of(w1)
    total[...] = jnp.dot(w0, held[0].reshape(depth, features), preferred_element_type=F32) + jnp.dot(
        w1, held[1].reshape(depth, features), preferred_element_type=F32
    )


def late_half(side, w2, w3, held, early, acc):
    rows, depth = w2.shape
    half = acc.shape[1]
    lanes = pl.ds(pl.multiple_of(side * half, half), half)
    acc[0:rows, :] = (
        early[:, lanes]
        + jnp.dot(w2, held[2, :, :, lanes].reshape(depth, half), preferred_element_type=F32)
        + jnp.dot(w3, held[3, :, :, lanes].reshape(depth, half), preferred_element_type=F32)
    )
    acc[rows:, :] = jnp.zeros((acc.shape[0] - rows, half), F32)


def partner_half_kernel(where, held, b2, b3, var, area, early, early_bias, weighted, extra_out, other, acc):
    rows, half = b2.shape[1], acc.shape[1]
    scale = as_column(var[...], rows)
    w2 = weigh(where, 2, b2, area, scale)
    w3 = weigh(where, 3, b3, area, scale)
    weighted[0], weighted[1] = w2, w3
    bias = early_bias[...] + bias_of(w2) + bias_of(w3)
    late_half(1 - where[1], w2, w3, held, early, acc)
    total = jnp.sum(area[...], axis=1, keepdims=True)
    extra = jnp.concatenate(
        [
            bias[0:1],
            jnp.zeros((1, 128 - rows), F32),
            jnp.broadcast_to(total, (1, 128)),
            jnp.zeros((1, half - 256), F32),
        ],
        axis=1,
    )
    extra_out[...] = jnp.broadcast_to(extra, (8, half))
    pieces_of(acc, extra_out[...], other)


def own_half_kernel(where, held, weighted, early, extra, mine, acc):
    late_half(where[1], weighted[0], weighted[1], held, early, acc)
    pieces_of(acc, extra[...], mine)


def grad_hidden_kernel(where, early, late, half, piece, out, *, replicas):
    first = pl.program_id(0) < GROUPS // 2
    inverse = 1.0 / (piece[PIECE_ROWS : PIECE_ROWS + 1, 128:129] * (1.0 / replicas))
    chunk = out.shape[1]
    for m in range(out.shape[0]):
        lanes = slice(m * chunk, (m + 1) * chunk)
        product = lax.dot_general(
            jnp.where(first, early[0, :, lanes], late[0, :, lanes]), half[...], (((0,), (0,)), ((), ())), preferred_element_type=F32
        )
        out[m] = (product * inverse).astype(BF16)


def squares_of(pieces, inverse):
    half = pieces.shape[2]
    keep = lax.broadcasted_iota(jnp.int32, (8, half), 0) < PIECE_ROWS
    squares = jnp.zeros((8, half), F32)
    for r in range(PIECES):
        g = jnp.where(keep, pieces[r] * inverse, 0.0)
        squares = squares + g * g
    return squares


def squares_kernel(own, out, *, replicas):
    inverse = 1.0 / (own[0, PIECE_ROWS : PIECE_ROWS + 1, 128:129] * (1.0 / replicas))
    out[...] = squares_of(own, inverse)


def update_kernel(where, step, own, partner, squares, weight, intercept, new_weight, new_bias, *, replicas):
    variables, features = weight.shape
    half = features // 2
    first = where[1] == 0
    mean_area = own[0, PIECE_ROWS : PIECE_ROWS + 1, 128:129] * (1.0 / replicas)
    inverse = 1.0 / mean_area
    bias_grad = own[0, PIECE_ROWS : PIECE_ROWS + 1, 0:variables] * inverse
    a, b = squares[...], squares_of(partner, inverse)
    both = jnp.where(first, a, b) + jnp.where(first, b, a)
    total = jnp.sum(jnp.sum(both, axis=0, keepdims=True), axis=1, keepdims=True)
    total = total + jnp.sum(bias_grad * bias_grad, axis=1, keepdims=True)
    count = variables * features + variables
    rms = jnp.sqrt(total / count + 1e-06)
    warm = (step[0] + 1).astype(F32) / WARMUP
    scale = warm * jnp.minimum(1.0, 1.0 / rms)
    for r in range(PIECES):
        low = PIECE_ROWS * r
        n = min(PIECE_ROWS, variables - low)
        if n <= 0:
            continue
        a, b = own[r, 0:n, :], partner[r, 0:n, :]
        left, right = jnp.where(first, a, b), jnp.where(first, b, a)
        new_weight[low : low + n, :half] = weight[low : low + n, :half] - scale * (left * inverse)
        new_weight[low : low + n, half:] = weight[low : low + n, half:] - scale * (right * inverse)
    new_bias[...] = intercept[...] - scale * bias_grad


def on_device(hidden, decoder_weight, decoder_intercept, analysis_truth, var_weight, lat_weight, area_bin, train_step):
    local, points, features = hidden.shape
    variables = decoder_weight.shape[0]
    rows = -(-variables // 8) * 8
    chunk = points // GROUPS
    members = local * GROUPS
    replicas = points * lax.axis_size("z") * lax.axis_size("x") * lax.axis_size("c") * GROUPS
    me, core = lax.axis_index("y"), lax.axis_index("c")
    where = jnp.stack([me, core]).astype(jnp.int32)

    def grant(mib):
        return pltpu.CompilerParams(vmem_limit_bytes=int(mib * MIB))

    intercept_row = decoder_intercept.reshape(1, variables)
    var_row = var_weight.reshape(1, variables)

    def turn(value, k):
        return value if k % GROUPS == 0 else lax.ppermute(value, "y", [(i, (i + k) % GROUPS) for i in range(GROUPS)])

    one_residual = jax.ShapeDtypeStruct((local, rows, chunk), F32)
    with jax.named_scope("forward_far"):
        far, half_weight = pl.pallas_call(
            far_kernel,
            out_shape=[one_residual, jax.ShapeDtypeStruct((rows, features), BF16)],
            in_specs=[SMEM, HBM, HBM],
            out_specs=[VMEM] * 2,
            scratch_shapes=[
                pltpu.VMEM((1, local, chunk, features), BF16),
                pltpu.VMEM((variables, features), F32),
                pltpu.SemaphoreType.DMA((1, local)),
                pltpu.SemaphoreType.DMA(()),
            ],
            compiler_params=grant(53.4),
            name="forward_far",
        )(where, hidden, decoder_weight)
        far = turn(far, 2)
    with jax.named_scope("forward_near"):
        after, before = pl.pallas_call(
            near_kernel,
            out_shape=[one_residual] * 2,
            in_specs=[SMEM, HBM, VMEM],
            out_specs=[VMEM] * 2,
            scratch_shapes=[
                pltpu.VMEM((2, local, chunk, features), BF16),
                pltpu.SemaphoreType.DMA((2, local)),
            ],
            compiler_params=grant(52),
            cost_estimate=pl.CostEstimate(
                flops=4 * rows * local * chunk * features, bytes_accessed=4 * local * chunk * features, transcendentals=0
            ),
            name="forward_near",
        )(where, hidden, half_weight)
        after, before = turn(after, 1), turn(before, 3)
    with jax.named_scope("forward_local"):
        here, area, shift, held = pl.pallas_call(
            local_kernel,
            out_shape=[
                one_residual,
                jax.ShapeDtypeStruct((1, points), F32),
                jax.ShapeDtypeStruct((rows, chunk), F32),
                jax.ShapeDtypeStruct((GROUPS, local, chunk, features), BF16),
            ],
            in_specs=[SMEM, HBM] + [VMEM] * 5,
            out_specs=[VMEM] * 4,
            scratch_shapes=[pltpu.SemaphoreType.DMA((GROUPS, local))],
            compiler_params=grant(46),
            name="forward_local",
        )(where, hidden, half_weight, lat_weight.reshape(-1, 128), area_bin.reshape(1, points), intercept_row, analysis_truth)
    with jax.named_scope("early_pairs"):
        early = pl.pallas_call(
            early_pairs_kernel,
            out_shape=jax.ShapeDtypeStruct((2 * local, rows, chunk), F32),
            in_specs=[VMEM] * 3,
            out_specs=VMEM,
            compiler_params=grant(4),
            name="early_pairs",
        )(here, far, shift)
    after, before, early, area, held = lax.optimization_barrier((after, before, early, area, held))
    with jax.named_scope("late_pairs"):
        brackets = pl.pallas_call(
            lambda *refs: late_pairs_kernel(members, *refs),
            out_shape=[jax.ShapeDtypeStruct((local, rows, chunk), BF16)] * GROUPS,
            in_specs=[VMEM] * (GROUPS + 2),
            out_specs=[VMEM] * GROUPS,
            scratch_shapes=[pltpu.VMEM((members, rows, chunk), F32)],
            compiler_params=grant(6),
            name="late_pairs",
        )(here, far, after, before, shift, early)
    with jax.named_scope("bracket_exchange"):
        returned = [brackets[0], turn(brackets[2], -1), turn(brackets[1], -2), turn(brackets[3], -3)]
    half = features // 2
    pieces = jax.ShapeDtypeStruct((PIECES, 8, half), F32)
    two_weighted = jax.ShapeDtypeStruct((GROUPS // 2, rows, local * chunk), BF16)
    sums = [pltpu.VMEM((PIECES * 8, half), F32)]
    with jax.named_scope("early_backward"):
        weighted_early, early_sum, early_bias = pl.pallas_call(
            early_backward_kernel,
            out_shape=[
                two_weighted,
                jax.ShapeDtypeStruct((rows, features), F32),
                jax.ShapeDtypeStruct((8, rows), F32),
            ],
            in_specs=[SMEM] + [VMEM] * 5,
            out_specs=[VMEM] * 3,
            compiler_params=grant(8),
            name="early_backward",
        )(where, held, returned[0], returned[1], var_row, area)
    with jax.named_scope("backward_partner_half"):
        weighted_late, extra, other = pl.pallas_call(
            partner_half_kernel,
            out_shape=[two_weighted, jax.ShapeDtypeStruct((8, half), F32), pieces],
            in_specs=[SMEM] + [VMEM] * 7,
            out_specs=[VMEM] * 3,
            scratch_shapes=sums,
            compiler_params=grant(8),
            name="backward_partner_half",
        )(where, held, returned[2], returned[3], var_row, area, early_sum, early_bias)
        swap = [(0, 1), (1, 0)]
        other = lax.ppermute(other, "c", swap)
    with jax.named_scope("backward_own_half"):
        mine = pl.pallas_call(
            own_half_kernel,
            out_shape=pieces,
            in_specs=[SMEM] + [VMEM] * 4,
            out_specs=VMEM,
            scratch_shapes=sums,
            compiler_params=grant(8),
            name="backward_own_half",
        )(where, held, weighted_late, early_sum, extra)
    with jax.named_scope("gradient_sum"):
        part = mine + other
        part = lax.all_to_all(part, ("x", "y"), 0, 0, tiled=True)
        depth = lax.axis_size("z")
        part = jnp.broadcast_to(jnp.sum(part, axis=0), (depth, 8, half))
        part = lax.all_to_all(part, "z", 0, 0, tiled=True)
        piece = jnp.sum(part, axis=0)
        own = lax.all_to_all(jnp.broadcast_to(piece, (PIECES, 8, half)), ("x", "y"), 0, 0, tiled=True)
    with jax.named_scope("grad_hidden"):
        grad_hidden = pl.pallas_call(
            lambda *refs: grad_hidden_kernel(*refs, replicas=replicas),
            out_shape=jax.ShapeDtypeStruct(hidden.shape, BF16),
            grid_spec=pltpu.PrefetchScalarGridSpec(
                num_scalar_prefetch=1,
                grid=(GROUPS,),
                in_specs=[
                    pl.BlockSpec((1, rows, local * chunk), lambda g, s: (lax.rem(g, 2), 0, 0)),
                    pl.BlockSpec((1, rows, local * chunk), lambda g, s: (lax.rem(g, 2), 0, 0)),
                    pl.BlockSpec((rows, features), lambda g, s: (0, 0)),
                    pl.BlockSpec((8, half), lambda g, s: (0, 0)),
                ],
                out_specs=pl.BlockSpec((local, chunk, features), lambda g, s: (0, lax.rem(s[0] + g, GROUPS), 0)),
            ),
            compiler_params=grant(12),
            cost_estimate=pl.CostEstimate(
                flops=2 * rows * local * points * features, bytes_accessed=2 * hidden.size, transcendentals=0
            ),
            name="grad_hidden",
        )(where, weighted_early, weighted_late, half_weight, piece)
        own, grad_hidden = lax.optimization_barrier((own, grad_hidden))
    with jax.named_scope("last_swap"):
        partner = lax.ppermute(own, "c", swap)
        squares = pl.pallas_call(
            lambda *refs: squares_kernel(*refs, replicas=replicas),
            out_shape=jax.ShapeDtypeStruct((8, half), F32),
            in_specs=[VMEM],
            out_specs=VMEM,
            compiler_params=grant(4),
            name="squares",
        )(own)
    with jax.named_scope("update"):
        new_weight, new_bias = pl.pallas_call(
            lambda *refs: update_kernel(*refs, replicas=replicas),
            out_shape=[
                jax.ShapeDtypeStruct((variables, features), F32),
                jax.ShapeDtypeStruct((1, variables), F32),
            ],
            in_specs=[SMEM, SMEM] + [VMEM] * 5,
            out_specs=[VMEM] * 2,
            compiler_params=grant(6),
            name="update",
        )(where, train_step, own, partner, squares, decoder_weight, intercept_row)
    return grad_hidden, new_weight, new_bias.reshape(variables)


def solution(mesh):
    fine = Mesh(mesh.devices.reshape(GROUPS, 8, 4, 2), ("y", "z", "x", "c"))
    space = ("z", "x", "c")
    return jax.shard_map(
        on_device,
        mesh=fine,
        in_specs=(P("y", space, None), P(), P(), P(None, space), P(), P(), P(space), P()),
        out_specs=(P("y", space, None), P(), P()),
        check_vma=False,
    )
```

```python
import jax
import jax.numpy as jnp
from jax import lax
from jax.experimental import pallas as pl
from jax.experimental.pallas import tpu as pltpu
from jax.sharding import Mesh, PartitionSpec as P

WARMUP = 1000
smooth_sq = 0.0025
fair_alpha = 0.95

GROUPS = 4
PIECES = 16
PIECE_ROWS = 7
MIB = 1024 * 1024
VMEM = pl.BlockSpec(memory_space=pltpu.VMEM)
SMEM = pl.BlockSpec(memory_space=pltpu.SMEM)
HBM = pl.BlockSpec(memory_space=pltpu.HBM)
F32 = jnp.float32
BF16 = jnp.bfloat16


def soft(d):
    return d * lax.rsqrt(d * d + smooth_sq)


def as_column(row, rows):
    n = row.shape[1]
    pick = lax.broadcasted_iota(jnp.int32, (rows, n), 0) == lax.broadcasted_iota(jnp.int32, (rows, n), 1)
    return jnp.sum(jnp.where(pick, jnp.broadcast_to(row, (rows, n)), 0.0), axis=1, keepdims=True)


def padded(value, rows):
    return jnp.concatenate([value, jnp.zeros((rows - value.shape[0], value.shape[1]), value.dtype)], axis=0)


def chunk_at(where, k, chunk):
    return pl.ds(pl.multiple_of(lax.rem(where[0] + k, GROUPS) * chunk, chunk), chunk)


def features_at(hidden, points):
    return jnp.concatenate([hidden[m, points, :] for m in range(hidden.shape[0])], axis=0)


def decode(half, features, out):
    values = lax.dot_general(half[...], features, (((1,), (1,)), ((), ())), preferred_element_type=F32)
    chunk = out.shape[2]
    for m in range(out.shape[0]):
        out[m] = values[:, m * chunk : (m + 1) * chunk]


def far_kernel(where, hidden, weight, out, half, held, w, sem):
    fetch = pltpu.make_async_copy(weight, w, sem.at[0])
    fetch.start()
    copy = pltpu.make_async_copy(hidden.at[:, chunk_at(where, 2, out.shape[2]), :], held, sem.at[1])
    copy.start()
    fetch.wait()
    half[...] = padded(w[...], half.shape[0]).astype(BF16)
    copy.wait()
    decode(half, held[...].reshape(-1, held.shape[2]), out)


def near_kernel(where, hidden, half, after, before):
    for k, out in ((1, after), (3, before)):
        decode(half, features_at(hidden, chunk_at(where, k, out.shape[2])), out)


def add_pair(total, i, j, s):
    total[i] = s if total[i] is None else total[i] + s
    total[j] = -s if total[j] is None else total[j] - s


def early_pairs_kernel(here, far, shift, out):
    local = here.shape[0]
    count = 2 * local

    def tile(t, carry):
        at = pl.ds(pl.multiple_of(t * 8, 8), 8)
        r = [ref[j, at, :] + shift[at, :] for ref in (here, far) for j in range(local)]
        total = [None] * count
        for i in range(count):
            for j in range(i + 1, count):
                add_pair(total, i, j, soft(r[i] - r[j]))
        for j in range(count):
            out[j, at, :] = total[j]
        return carry

    lax.fori_loop(0, here.shape[1] // 8, tile, 0)


def late_pairs_kernel(members, here, far, after, before, shift, early, *rest):
    ins, outs, scratch = (here, far, after, before), rest[:GROUPS], rest[GROUPS]
    local = here.shape[0]
    count = early.shape[0]
    eps = (1.0 - fair_alpha) / members
    normalizer = (1.0 - eps) / (members * (members - 1))

    def tile(t, carry):
        at = pl.ds(pl.multiple_of(t * 8, 8), 8)
        r = [ref[j, at, :] + shift[at, :] for ref in ins for j in range(local)]
        total = [early[j, at, :] for j in range(count)] + [None] * (members - count)
        for i in range(members):
            for j in range(max(i + 1, count), members):
                add_pair(total, i, j, soft(r[i] - r[j]))
        for j in range(members):
            scratch[j, at, :] = soft(r[j]) * (1.0 / members) - normalizer * total[j]
        return carry

    lax.fori_loop(0, here.shape[1] // 8, tile, 0)
    for j in range(members):
        outs[j // local][j % local] = scratch[j].astype(BF16)


def local_kernel(where, hidden, half, lat, area_bin, intercept, truth, var, out, area, weight, shift):
    rows, chunk = shift.shape
    cells, width = lat.shape
    points = area_bin.shape[1]
    bins = jnp.broadcast_to(area_bin[...], (width, points))
    level = lax.broadcasted_iota(jnp.int32, (width, points), 0)
    total = jnp.zeros((width, points), F32)
    for q in range(cells):
        column = as_column(lat[q : q + 1, :], width)
        total = total + jnp.where(bins == level + q * width, column, 0.0)
    by_point = jnp.sum(total, axis=0, keepdims=True)
    area[...] = jnp.broadcast_to(jnp.sum(by_point, axis=1, keepdims=True), area.shape)
    weight[...] = by_point * as_column(var[...], rows)
    here = chunk_at(where, 0, chunk)
    shift[...] = as_column(intercept[...], rows) - padded(truth[:, here], rows)
    decode(half, features_at(hidden, here), out)


def pieces_of(acc, extra, out):
    last = lax.broadcasted_iota(jnp.int32, out.shape[1:], 0) == PIECE_ROWS
    for r in range(PIECES):
        out[r] = jnp.where(last, extra, acc[PIECE_ROWS * r : PIECE_ROWS * r + 8, :])


def weigh(where, k, bracket, weight):
    local, _, chunk = bracket.shape
    scale = weight[:, chunk_at(where, k, chunk)]
    return jnp.concatenate([(scale * bracket[m].astype(F32)).astype(BF16) for m in range(local)], axis=1)


def bias_of(w):
    ones = jnp.ones((8, w.shape[1]), BF16)
    return lax.dot_general(ones, w, (((1,), (1,)), ((), ())), preferred_element_type=F32)


def early_backward_kernel(where, hidden, b0, b1, weight, weighted, total, bias):
    chunk = b0.shape[2]
    w0 = weigh(where, 0, b0, weight)
    w1 = weigh(where, 1, b1, weight)
    weighted[0], weighted[1] = w0, w1
    bias[...] = bias_of(w0) + bias_of(w1)
    total[...] = jnp.dot(
        w0, features_at(hidden, chunk_at(where, 0, chunk)), preferred_element_type=F32
    ) + jnp.dot(w1, features_at(hidden, chunk_at(where, 1, chunk)), preferred_element_type=F32)


def late_half(where, side, w2, w3, hidden, early, acc):
    rows, depth = w2.shape
    local = hidden.shape[0]
    half = acc.shape[1]
    lanes = pl.ds(pl.multiple_of(side * half, half), half)

    def product(w, k):
        points = chunk_at(where, k, depth // local)
        part = jnp.concatenate([hidden[m, points, lanes] for m in range(local)], axis=0)
        return jnp.dot(w, part, preferred_element_type=F32)

    acc[0:rows, :] = early[:, lanes] + product(w2, 2) + product(w3, 3)
    acc[rows:, :] = jnp.zeros((acc.shape[0] - rows, half), F32)


def extra_row(bias, area, half):
    row = jnp.concatenate([bias, area, jnp.zeros((1, half - 256), F32)], axis=1)
    return jnp.broadcast_to(row, (8, half))


def partner_half_kernel(where, hidden, b2, b3, weight, area, early, weighted, other, acc):
    w2 = weigh(where, 2, b2, weight)
    w3 = weigh(where, 3, b3, weight)
    weighted[0], weighted[1] = w2, w3
    late_half(where, 1 - where[1], w2, w3, hidden, early, acc)
    pieces_of(acc, extra_row(jnp.zeros((1, 128), F32), area[...], acc.shape[1]), other)


def own_half_kernel(where, hidden, weighted, early, early_bias, area, mine, acc):
    rows = early.shape[0]
    w2, w3 = weighted[0], weighted[1]
    late_half(where, where[1], w2, w3, hidden, early, acc)
    bias = early_bias[...] + bias_of(w2) + bias_of(w3)
    bias = jnp.concatenate([bias[0:1], jnp.zeros((1, 128 - rows), F32)], axis=1)
    pieces_of(acc, extra_row(bias, area[...], acc.shape[1]), mine)


def grad_hidden_kernel(where, early, late, half, piece, out, *, replicas):
    first = pl.program_id(0) < GROUPS // 2
    inverse = 1.0 / (piece[PIECE_ROWS : PIECE_ROWS + 1, 128:129] * (1.0 / replicas))
    chunk = out.shape[1]
    for m in range(out.shape[0]):
        lanes = slice(m * chunk, (m + 1) * chunk)
        product = lax.dot_general(
            jnp.where(first, early[0, :, lanes], late[0, :, lanes]), half[...], (((0,), (0,)), ((), ())), preferred_element_type=F32
        )
        out[m] = (product * inverse).astype(BF16)


def squares_of(pieces, inverse):
    half = pieces.shape[2]
    keep = lax.broadcasted_iota(jnp.int32, (8, half), 0) < PIECE_ROWS
    squares = jnp.zeros((8, half), F32)
    for r in range(PIECES):
        g = jnp.where(keep, pieces[r] * inverse, 0.0)
        squares = squares + g * g
    return squares


def squares_kernel(own, out, *, replicas):
    inverse = 1.0 / (own[0, PIECE_ROWS : PIECE_ROWS + 1, 128:129] * (1.0 / replicas))
    out[...] = squares_of(own, inverse)


def update_kernel(where, step, own, partner, squares, weight, intercept, new_weight, new_bias, *, replicas):
    variables, features = weight.shape
    half = features // 2
    first = where[1] == 0
    mean_area = own[0, PIECE_ROWS : PIECE_ROWS + 1, 128:129] * (1.0 / replicas)
    inverse = 1.0 / mean_area
    a, b = (side[0, PIECE_ROWS : PIECE_ROWS + 1, 0:variables] for side in (own, partner))
    bias_grad = (jnp.where(first, a, b) + jnp.where(first, b, a)) * inverse
    a, b = squares[...], squares_of(partner, inverse)
    both = jnp.where(first, a, b) + jnp.where(first, b, a)
    total = jnp.sum(jnp.sum(both, axis=0, keepdims=True), axis=1, keepdims=True)
    total = total + jnp.sum(bias_grad * bias_grad, axis=1, keepdims=True)
    count = variables * features + variables
    rms = jnp.sqrt(total / count + 1e-06)
    warm = (step[0] + 1).astype(F32) / WARMUP
    scale = warm * jnp.minimum(1.0, 1.0 / rms)
    for r in range(PIECES):
        low = PIECE_ROWS * r
        n = min(PIECE_ROWS, variables - low)
        if n <= 0:
            continue
        a, b = own[r, 0:n, :], partner[r, 0:n, :]
        left, right = jnp.where(first, a, b), jnp.where(first, b, a)
        new_weight[low : low + n, :half] = weight[low : low + n, :half] - scale * (left * inverse)
        new_weight[low : low + n, half:] = weight[low : low + n, half:] - scale * (right * inverse)
    new_bias[...] = intercept[...] - scale * bias_grad


def on_device(hidden, decoder_weight, decoder_intercept, analysis_truth, var_weight, lat_weight, area_bin, train_step):
    local, points, features = hidden.shape
    variables = decoder_weight.shape[0]
    rows = -(-variables // 8) * 8
    chunk = points // GROUPS
    members = local * GROUPS
    replicas = points * lax.axis_size("z") * lax.axis_size("x") * lax.axis_size("c") * GROUPS
    me, core = lax.axis_index("y"), lax.axis_index("c")
    where = jnp.stack([me, core]).astype(jnp.int32)

    def grant(mib):
        return pltpu.CompilerParams(vmem_limit_bytes=int(mib * MIB))

    intercept_row = decoder_intercept.reshape(1, variables)
    var_row = var_weight.reshape(1, variables)

    def turn(value, k):
        return value if k % GROUPS == 0 else lax.ppermute(value, "y", [(i, (i + k) % GROUPS) for i in range(GROUPS)])

    one_residual = jax.ShapeDtypeStruct((local, rows, chunk), F32)
    with jax.named_scope("forward_far"):
        far, half_weight = pl.pallas_call(
            far_kernel,
            out_shape=[one_residual, jax.ShapeDtypeStruct((rows, features), BF16)],
            in_specs=[SMEM, HBM, HBM],
            out_specs=[VMEM] * 2,
            scratch_shapes=[
                pltpu.VMEM((local, chunk, features), BF16),
                pltpu.VMEM((variables, features), F32),
                pltpu.SemaphoreType.DMA((2,)),
            ],
            compiler_params=grant(53.4),
            name="forward_far",
        )(where, hidden, decoder_weight)
        far = turn(far, 2)
    with jax.named_scope("forward_near"):
        after, before = pl.pallas_call(
            near_kernel,
            out_shape=[one_residual] * 2,
            in_specs=[SMEM, VMEM, VMEM],
            out_specs=[VMEM] * 2,
            compiler_params=grant(8),
            cost_estimate=pl.CostEstimate(
                flops=4 * rows * local * chunk * features, bytes_accessed=4 * local * chunk * features, transcendentals=0
            ),
            name="forward_near",
        )(where, hidden, half_weight)
        after, before = turn(after, 1), turn(before, 3)
    with jax.named_scope("forward_local"):
        here, area, point_weight, shift = pl.pallas_call(
            local_kernel,
            out_shape=[
                one_residual,
                jax.ShapeDtypeStruct((1, 128), F32),
                jax.ShapeDtypeStruct((rows, points), F32),
                jax.ShapeDtypeStruct((rows, chunk), F32),
            ],
            in_specs=[SMEM] + [VMEM] * 7,
            out_specs=[VMEM] * 4,
            compiler_params=grant(8),
            name="forward_local",
        )(where, hidden, half_weight, lat_weight.reshape(-1, 128), area_bin.reshape(1, points), intercept_row, analysis_truth, var_row)
    with jax.named_scope("early_pairs"):
        early = pl.pallas_call(
            early_pairs_kernel,
            out_shape=jax.ShapeDtypeStruct((2 * local, rows, chunk), F32),
            in_specs=[VMEM] * 3,
            out_specs=VMEM,
            compiler_params=grant(4),
            name="early_pairs",
        )(here, far, shift)
    after, before, early, point_weight = lax.optimization_barrier((after, before, early, point_weight))
    with jax.named_scope("late_pairs"):
        brackets = pl.pallas_call(
            lambda *refs: late_pairs_kernel(members, *refs),
            out_shape=[jax.ShapeDtypeStruct((local, rows, chunk), BF16)] * GROUPS,
            in_specs=[VMEM] * (GROUPS + 2),
            out_specs=[VMEM] * GROUPS,
            scratch_shapes=[pltpu.VMEM((members, rows, chunk), F32)],
            compiler_params=grant(6),
            name="late_pairs",
        )(here, far, after, before, shift, early)
    with jax.named_scope("bracket_exchange"):
        returned = [brackets[0], turn(brackets[2], -1), turn(brackets[1], -2), turn(brackets[3], -3)]
    half = features // 2
    pieces = jax.ShapeDtypeStruct((PIECES, 8, half), F32)
    two_weighted = jax.ShapeDtypeStruct((GROUPS // 2, rows, local * chunk), BF16)
    sums = [pltpu.VMEM((PIECES * 8, half), F32)]
    with jax.named_scope("early_backward"):
        weighted_early, early_sum, early_bias = pl.pallas_call(
            early_backward_kernel,
            out_shape=[
                two_weighted,
                jax.ShapeDtypeStruct((rows, features), F32),
                jax.ShapeDtypeStruct((8, rows), F32),
            ],
            in_specs=[SMEM] + [VMEM] * 4,
            out_specs=[VMEM] * 3,
            compiler_params=grant(10),
            name="early_backward",
        )(where, hidden, returned[0], returned[1], point_weight)
    with jax.named_scope("backward_partner_half"):
        weighted_late, other = pl.pallas_call(
            partner_half_kernel,
            out_shape=[two_weighted, pieces],
            in_specs=[SMEM] + [VMEM] * 6,
            out_specs=[VMEM] * 2,
            scratch_shapes=sums,
            compiler_params=grant(10),
            name="backward_partner_half",
        )(where, hidden, returned[2], returned[3], point_weight, area, early_sum)
        swap = [(0, 1), (1, 0)]
        other = lax.ppermute(other, "c", swap)
    with jax.named_scope("backward_own_half"):
        mine = pl.pallas_call(
            own_half_kernel,
            out_shape=pieces,
            in_specs=[SMEM] + [VMEM] * 5,
            out_specs=VMEM,
            scratch_shapes=sums,
            compiler_params=grant(10),
            name="backward_own_half",
        )(where, hidden, weighted_late, early_sum, early_bias, area)
    with jax.named_scope("gradient_sum"):
        part = mine + other
        part = lax.all_to_all(part, ("x", "y"), 0, 0, tiled=True)
        depth = lax.axis_size("z")
        part = jnp.broadcast_to(jnp.sum(part, axis=0), (depth, 8, half))
        part = lax.all_to_all(part, "z", 0, 0, tiled=True)
        piece = jnp.sum(part, axis=0)
        own = lax.all_to_all(jnp.broadcast_to(piece, (PIECES, 8, half)), ("x", "y"), 0, 0, tiled=True)
    with jax.named_scope("grad_hidden"):
        grad_hidden = pl.pallas_call(
            lambda *refs: grad_hidden_kernel(*refs, replicas=replicas),
            out_shape=jax.ShapeDtypeStruct(hidden.shape, BF16),
            grid_spec=pltpu.PrefetchScalarGridSpec(
                num_scalar_prefetch=1,
                grid=(GROUPS,),
                in_specs=[
                    pl.BlockSpec((1, rows, local * chunk), lambda g, s: (lax.rem(g, 2), 0, 0)),
                    pl.BlockSpec((1, rows, local * chunk), lambda g, s: (lax.rem(g, 2), 0, 0)),
                    pl.BlockSpec((rows, features), lambda g, s: (0, 0)),
                    pl.BlockSpec((8, half), lambda g, s: (0, 0)),
                ],
                out_specs=pl.BlockSpec((local, chunk, features), lambda g, s: (0, lax.rem(s[0] + g, GROUPS), 0)),
            ),
            compiler_params=grant(12),
            cost_estimate=pl.CostEstimate(
                flops=2 * rows * local * points * features, bytes_accessed=2 * hidden.size, transcendentals=0
            ),
            name="grad_hidden",
        )(where, weighted_early, weighted_late, half_weight, piece)
        own, grad_hidden = lax.optimization_barrier((own, grad_hidden))
    with jax.named_scope("last_swap"):
        partner = lax.ppermute(own, "c", swap)
        squares = pl.pallas_call(
            lambda *refs: squares_kernel(*refs, replicas=replicas),
            out_shape=jax.ShapeDtypeStruct((8, half), F32),
            in_specs=[VMEM],
            out_specs=VMEM,
            compiler_params=grant(4),
            name="squares",
        )(own)
    with jax.named_scope("update"):
        new_weight, new_bias = pl.pallas_call(
            lambda *refs: update_kernel(*refs, replicas=replicas),
            out_shape=[
                jax.ShapeDtypeStruct((variables, features), F32),
                jax.ShapeDtypeStruct((1, variables), F32),
            ],
            in_specs=[SMEM, SMEM] + [VMEM] * 5,
            out_specs=[VMEM] * 2,
            compiler_params=grant(6),
            name="update",
        )(where, train_step, own, partner, squares, decoder_weight, intercept_row)
    return grad_hidden, new_weight, new_bias.reshape(variables)


def solution(mesh):
    fine = Mesh(mesh.devices.reshape(GROUPS, 8, 4, 2), ("y", "z", "x", "c"))
    space = ("z", "x", "c")
    return jax.shard_map(
        on_device,
        mesh=fine,
        in_specs=(P("y", space, None), P(), P(), P(None, space), P(), P(), P(space), P()),
        out_specs=(P("y", space, None), P(), P()),
        check_vma=False,
    )
```

```python
import jax
import jax.numpy as jnp
from jax import lax
from jax.experimental import pallas as pl
from jax.experimental.pallas import tpu as pltpu
from jax.sharding import Mesh, PartitionSpec as P

WARMUP = 1000
smooth_sq = 0.0025
fair_alpha = 0.95

GROUPS = 4
PIECES = 16
PIECE_ROWS = 7
MIB = 1024 * 1024
VMEM = pl.BlockSpec(memory_space=pltpu.VMEM)
SMEM = pl.BlockSpec(memory_space=pltpu.SMEM)
HBM = pl.BlockSpec(memory_space=pltpu.HBM)
F32 = jnp.float32
BF16 = jnp.bfloat16


def soft(d):
    return d * lax.rsqrt(d * d + smooth_sq)


def as_column(row, rows):
    n = row.shape[1]
    pick = lax.broadcasted_iota(jnp.int32, (rows, n), 0) == lax.broadcasted_iota(jnp.int32, (rows, n), 1)
    return jnp.sum(jnp.where(pick, jnp.broadcast_to(row, (rows, n)), 0.0), axis=1, keepdims=True)


def padded(value, rows):
    return jnp.concatenate([value, jnp.zeros((rows - value.shape[0], value.shape[1]), value.dtype)], axis=0)


def chunk_at(where, k, chunk):
    return pl.ds(pl.multiple_of(lax.rem(where[0] + k, GROUPS) * chunk, chunk), chunk)


def fetch_chunks(where, hidden, held, sem, ks):
    local, chunk = held.shape[1:3]
    copies = []
    for slot, k in enumerate(ks):
        points = chunk_at(where, k, chunk)
        copies.append(
            [pltpu.make_async_copy(hidden.at[m, points, :], held.at[slot, m], sem.at[slot, m]) for m in range(local)]
        )
        for copy in copies[slot]:
            copy.start()
    return copies


def decode_chunk(copies, held, half, out):
    for copy in copies:
        copy.wait()
    values = lax.dot_general(
        half[...], held[...].reshape(-1, held.shape[2]), (((1,), (1,)), ((), ())), preferred_element_type=F32
    )
    chunk = out.shape[2]
    for m in range(out.shape[0]):
        out[m] = values[:, m * chunk : (m + 1) * chunk]


def far_kernel(where, hidden, weight, out, half, held, w, sem, weight_sem):
    fetch = pltpu.make_async_copy(weight, w, weight_sem)
    fetch.start()
    (copies,) = fetch_chunks(where, hidden, held, sem, (2,))
    fetch.wait()
    half[...] = padded(w[...], half.shape[0]).astype(BF16)
    decode_chunk(copies, held.at[0], half, out)


def near_kernel(where, hidden, half, after, before, held, sem):
    copies = fetch_chunks(where, hidden, held, sem, (1, 3))
    for slot, out in enumerate((after, before)):
        decode_chunk(copies[slot], held.at[slot], half, out)


def add_pair(total, i, j, s):
    total[i] = s if total[i] is None else total[i] + s
    total[j] = -s if total[j] is None else total[j] - s


def early_pairs_kernel(here, far, shift, out):
    local = here.shape[0]
    count = 2 * local

    def tile(t, carry):
        at = pl.ds(pl.multiple_of(t * 8, 8), 8)
        r = [ref[j, at, :] + shift[at, :] for ref in (here, far) for j in range(local)]
        total = [None] * count
        for i in range(count):
            for j in range(i + 1, count):
                add_pair(total, i, j, soft(r[i] - r[j]))
        for j in range(count):
            out[j, at, :] = total[j]
        return carry

    lax.fori_loop(0, here.shape[1] // 8, tile, 0)


def late_pairs_kernel(members, here, far, after, before, shift, early, *rest):
    ins, outs, scratch = (here, far, after, before), rest[:GROUPS], rest[GROUPS]
    local = here.shape[0]
    count = early.shape[0]
    eps = (1.0 - fair_alpha) / members
    normalizer = (1.0 - eps) / (members * (members - 1))

    def tile(t, carry):
        at = pl.ds(pl.multiple_of(t * 8, 8), 8)
        r = [ref[j, at, :] + shift[at, :] for ref in ins for j in range(local)]
        total = [early[j, at, :] for j in range(count)] + [None] * (members - count)
        for i in range(members):
            for j in range(max(i + 1, count), members):
                add_pair(total, i, j, soft(r[i] - r[j]))
        for j in range(members):
            scratch[j, at, :] = soft(r[j]) * (1.0 / members) - normalizer * total[j]
        return carry

    lax.fori_loop(0, here.shape[1] // 8, tile, 0)
    for j in range(members):
        outs[j // local][j % local] = scratch[j].astype(BF16)


def local_kernel(where, hidden, half, lat, area_bin, intercept, truth, var, out, area, weight, shift, held, sem):
    copies = fetch_chunks(where, hidden, held, sem, range(GROUPS))
    rows, chunk = shift.shape
    cells, width = lat.shape
    points = area_bin.shape[1]
    bins = jnp.broadcast_to(area_bin[...], (width, points))
    level = lax.broadcasted_iota(jnp.int32, (width, points), 0)
    total = jnp.zeros((width, points), F32)
    for q in range(cells):
        column = as_column(lat[q : q + 1, :], width)
        total = total + jnp.where(bins == level + q * width, column, 0.0)
    by_point = jnp.sum(total, axis=0, keepdims=True)
    area[...] = jnp.broadcast_to(jnp.sum(by_point, axis=1, keepdims=True), area.shape)
    weight[...] = by_point * as_column(var[...], rows)
    here = chunk_at(where, 0, chunk)
    shift[...] = as_column(intercept[...], rows) - padded(truth[:, here], rows)
    decode_chunk(copies[0], held.at[0], half, out)
    for chunk_copies in copies[1:]:
        for copy in chunk_copies:
            copy.wait()


def pieces_of(acc, extra, out):
    last = lax.broadcasted_iota(jnp.int32, out.shape[1:], 0) == PIECE_ROWS
    for r in range(PIECES):
        out[r] = jnp.where(last, extra, acc[PIECE_ROWS * r : PIECE_ROWS * r + 8, :])


def weigh(where, k, bracket, weight):
    local, _, chunk = bracket.shape
    scale = weight[:, chunk_at(where, k, chunk)]
    return jnp.concatenate([(scale * bracket[m].astype(F32)).astype(BF16) for m in range(local)], axis=1)


def bias_of(w):
    ones = jnp.ones((8, w.shape[1]), BF16)
    return lax.dot_general(ones, w, (((1,), (1,)), ((), ())), preferred_element_type=F32)


def early_backward_kernel(where, held, b0, b1, weight, weighted, total, bias):
    features = held.shape[3]
    w0 = weigh(where, 0, b0, weight)
    w1 = weigh(where, 1, b1, weight)
    weighted[0], weighted[1] = w0, w1
    bias[...] = bias_of(w0) + bias_of(w1)
    total[...] = jnp.dot(
        w0, held[0].reshape(-1, features), preferred_element_type=F32
    ) + jnp.dot(w1, held[1].reshape(-1, features), preferred_element_type=F32)


def late_half(side, w2, w3, held, early, acc):
    rows = w2.shape[0]
    half = acc.shape[1]
    lanes = pl.ds(pl.multiple_of(side * half, half), half)
    acc[0:rows, :] = (
        early[:, lanes]
        + jnp.dot(w2, held[2, :, :, lanes].reshape(-1, half), preferred_element_type=F32)
        + jnp.dot(w3, held[3, :, :, lanes].reshape(-1, half), preferred_element_type=F32)
    )
    acc[rows:, :] = jnp.zeros((acc.shape[0] - rows, half), F32)


def extra_row(bias, area, half):
    row = jnp.concatenate([bias, area, jnp.zeros((1, half - 256), F32)], axis=1)
    return jnp.broadcast_to(row, (8, half))


def partner_half_kernel(where, held, b2, b3, weight, area, early, weighted, other, acc):
    w2 = weigh(where, 2, b2, weight)
    w3 = weigh(where, 3, b3, weight)
    weighted[0], weighted[1] = w2, w3
    late_half(1 - where[1], w2, w3, held, early, acc)
    pieces_of(acc, extra_row(jnp.zeros((1, 128), F32), area[...], acc.shape[1]), other)


def own_half_kernel(where, held, weighted, early, early_bias, area, mine, acc):
    rows = early.shape[0]
    w2, w3 = weighted[0], weighted[1]
    late_half(where[1], w2, w3, held, early, acc)
    bias = early_bias[...] + bias_of(w2) + bias_of(w3)
    bias = jnp.concatenate([bias[0:1], jnp.zeros((1, 128 - rows), F32)], axis=1)
    pieces_of(acc, extra_row(bias, area[...], acc.shape[1]), mine)


def grad_hidden_kernel(where, early, late, half, piece, out, *, replicas):
    first = pl.program_id(0) < GROUPS // 2
    inverse = 1.0 / (piece[PIECE_ROWS : PIECE_ROWS + 1, 128:129] * (1.0 / replicas))
    chunk = out.shape[1]
    for m in range(out.shape[0]):
        lanes = slice(m * chunk, (m + 1) * chunk)
        product = lax.dot_general(
            jnp.where(first, early[0, :, lanes], late[0, :, lanes]), half[...], (((0,), (0,)), ((), ())), preferred_element_type=F32
        )
        out[m] = (product * inverse).astype(BF16)


def squares_of(pieces, inverse):
    half = pieces.shape[2]
    keep = lax.broadcasted_iota(jnp.int32, (8, half), 0) < PIECE_ROWS
    squares = jnp.zeros((8, half), F32)
    for r in range(PIECES):
        g = jnp.where(keep, pieces[r] * inverse, 0.0)
        squares = squares + g * g
    return squares


def squares_kernel(own, out, *, replicas):
    inverse = 1.0 / (own[0, PIECE_ROWS : PIECE_ROWS + 1, 128:129] * (1.0 / replicas))
    out[...] = squares_of(own, inverse)


def update_kernel(where, step, own, partner, squares, weight, intercept, new_weight, new_bias, result, sem, *, replicas):
    variables, features = weight.shape
    half = features // 2
    first = where[1] == 0
    mean_area = own[0, PIECE_ROWS : PIECE_ROWS + 1, 128:129] * (1.0 / replicas)
    inverse = 1.0 / mean_area
    a, b = (side[0, PIECE_ROWS : PIECE_ROWS + 1, 0:variables] for side in (own, partner))
    bias_grad = (jnp.where(first, a, b) + jnp.where(first, b, a)) * inverse
    a, b = squares[...], squares_of(partner, inverse)
    both = jnp.where(first, a, b) + jnp.where(first, b, a)
    total = jnp.sum(jnp.sum(both, axis=0, keepdims=True), axis=1, keepdims=True)
    total = total + jnp.sum(bias_grad * bias_grad, axis=1, keepdims=True)
    count = variables * features + variables
    rms = jnp.sqrt(total / count + 1e-06)
    warm = (step[0] + 1).astype(F32) / WARMUP
    scale = warm * jnp.minimum(1.0, 1.0 / rms)
    copies = []
    for side in range(2):
        lanes = slice(side * half, (side + 1) * half)
        this_core = where[1] == side
        for r in range(PIECES):
            low = PIECE_ROWS * r
            n = min(PIECE_ROWS, variables - low)
            if n <= 0:
                continue
            g = jnp.where(this_core, own[r, 0:n, :], partner[r, 0:n, :])
            result[low : low + n, lanes] = weight[low : low + n, lanes] - scale * (g * inverse)
        copies.append(pltpu.make_async_copy(result.at[:, lanes], new_weight.at[:, lanes], sem.at[side]))
        copies[side].start()
    new_bias[...] = intercept[...] - scale * bias_grad
    for copy in copies:
        copy.wait()


def on_device(hidden, decoder_weight, decoder_intercept, analysis_truth, var_weight, lat_weight, area_bin, train_step):
    local, points, features = hidden.shape
    variables = decoder_weight.shape[0]
    rows = -(-variables // 8) * 8
    chunk = points // GROUPS
    members = local * GROUPS
    replicas = points * lax.axis_size("z") * lax.axis_size("x") * lax.axis_size("c") * GROUPS
    me, core = lax.axis_index("y"), lax.axis_index("c")
    where = jnp.stack([me, core]).astype(jnp.int32)

    def grant(mib):
        return pltpu.CompilerParams(vmem_limit_bytes=int(mib * MIB))

    intercept_row = decoder_intercept.reshape(1, variables)
    var_row = var_weight.reshape(1, variables)

    def turn(value, k):
        return value if k % GROUPS == 0 else lax.ppermute(value, "y", [(i, (i + k) % GROUPS) for i in range(GROUPS)])

    one_residual = jax.ShapeDtypeStruct((local, rows, chunk), F32)
    with jax.named_scope("forward_far"):
        far, half_weight = pl.pallas_call(
            far_kernel,
            out_shape=[one_residual, jax.ShapeDtypeStruct((rows, features), BF16)],
            in_specs=[SMEM, HBM, HBM],
            out_specs=[VMEM] * 2,
            scratch_shapes=[
                pltpu.VMEM((1, local, chunk, features), BF16),
                pltpu.VMEM((variables, features), F32),
                pltpu.SemaphoreType.DMA((1, local)),
                pltpu.SemaphoreType.DMA(()),
            ],
            compiler_params=grant(53.4),
            name="forward_far",
        )(where, hidden, decoder_weight)
        far = turn(far, 2)
    with jax.named_scope("forward_near"):
        after, before = pl.pallas_call(
            near_kernel,
            out_shape=[one_residual] * 2,
            in_specs=[SMEM, HBM, VMEM],
            out_specs=[VMEM] * 2,
            scratch_shapes=[
                pltpu.VMEM((2, local, chunk, features), BF16),
                pltpu.SemaphoreType.DMA((2, local)),
            ],
            compiler_params=grant(52),
            cost_estimate=pl.CostEstimate(
                flops=4 * rows * local * chunk * features, bytes_accessed=4 * local * chunk * features, transcendentals=0
            ),
            name="forward_near",
        )(where, hidden, half_weight)
        after, before = turn(after, 1), turn(before, 3)
    with jax.named_scope("forward_local"):
        here, area, point_weight, shift, held = pl.pallas_call(
            local_kernel,
            out_shape=[
                one_residual,
                jax.ShapeDtypeStruct((1, 128), F32),
                jax.ShapeDtypeStruct((rows, points), F32),
                jax.ShapeDtypeStruct((rows, chunk), F32),
                jax.ShapeDtypeStruct((GROUPS, local, chunk, features), BF16),
            ],
            in_specs=[SMEM, HBM] + [VMEM] * 6,
            out_specs=[VMEM] * 5,
            scratch_shapes=[pltpu.SemaphoreType.DMA((GROUPS, local))],
            compiler_params=grant(46),
            name="forward_local",
        )(where, hidden, half_weight, lat_weight.reshape(-1, 128), area_bin.reshape(1, points), intercept_row, analysis_truth, var_row)
    with jax.named_scope("early_pairs"):
        early = pl.pallas_call(
            early_pairs_kernel,
            out_shape=jax.ShapeDtypeStruct((2 * local, rows, chunk), F32),
            in_specs=[VMEM] * 3,
            out_specs=VMEM,
            compiler_params=grant(4),
            name="early_pairs",
        )(here, far, shift)
    after, before, early, point_weight, held = lax.optimization_barrier((after, before, early, point_weight, held))
    with jax.named_scope("late_pairs"):
        brackets = pl.pallas_call(
            lambda *refs: late_pairs_kernel(members, *refs),
            out_shape=[jax.ShapeDtypeStruct((local, rows, chunk), BF16)] * GROUPS,
            in_specs=[VMEM] * (GROUPS + 2),
            out_specs=[VMEM] * GROUPS,
            scratch_shapes=[pltpu.VMEM((members, rows, chunk), F32)],
            compiler_params=grant(6),
            name="late_pairs",
        )(here, far, after, before, shift, early)
    with jax.named_scope("bracket_exchange"):
        returned = [brackets[0], turn(brackets[2], -1), turn(brackets[1], -2), turn(brackets[3], -3)]
    half = features // 2
    pieces = jax.ShapeDtypeStruct((PIECES, 8, half), F32)
    two_weighted = jax.ShapeDtypeStruct((GROUPS // 2, rows, local * chunk), BF16)
    sums = [pltpu.VMEM((PIECES * 8, half), F32)]
    with jax.named_scope("early_backward"):
        weighted_early, early_sum, early_bias = pl.pallas_call(
            early_backward_kernel,
            out_shape=[
                two_weighted,
                jax.ShapeDtypeStruct((rows, features), F32),
                jax.ShapeDtypeStruct((8, rows), F32),
            ],
            in_specs=[SMEM] + [VMEM] * 4,
            out_specs=[VMEM] * 3,
            compiler_params=grant(10),
            name="early_backward",
        )(where, held, returned[0], returned[1], point_weight)
    with jax.named_scope("backward_partner_half"):
        weighted_late, other = pl.pallas_call(
            partner_half_kernel,
            out_shape=[two_weighted, pieces],
            in_specs=[SMEM] + [VMEM] * 6,
            out_specs=[VMEM] * 2,
            scratch_shapes=sums,
            compiler_params=grant(10),
            name="backward_partner_half",
        )(where, held, returned[2], returned[3], point_weight, area, early_sum)
        swap = [(0, 1), (1, 0)]
        other = lax.ppermute(other, "c", swap)
    with jax.named_scope("backward_own_half"):
        mine = pl.pallas_call(
            own_half_kernel,
            out_shape=pieces,
            in_specs=[SMEM] + [VMEM] * 5,
            out_specs=VMEM,
            scratch_shapes=sums,
            compiler_params=grant(10),
            name="backward_own_half",
        )(where, held, weighted_late, early_sum, early_bias, area)
    with jax.named_scope("gradient_sum"):
        part = mine + other
        part = lax.all_to_all(part, ("x", "y"), 0, 0, tiled=True)
        depth = lax.axis_size("z")
        part = jnp.broadcast_to(jnp.sum(part, axis=0), (depth, 8, half))
        part = lax.all_to_all(part, "z", 0, 0, tiled=True)
        piece = jnp.sum(part, axis=0)
        own = lax.all_to_all(jnp.broadcast_to(piece, (PIECES, 8, half)), ("x", "y"), 0, 0, tiled=True)
    with jax.named_scope("grad_hidden"):
        grad_hidden = pl.pallas_call(
            lambda *refs: grad_hidden_kernel(*refs, replicas=replicas),
            out_shape=jax.ShapeDtypeStruct(hidden.shape, BF16),
            grid_spec=pltpu.PrefetchScalarGridSpec(
                num_scalar_prefetch=1,
                grid=(GROUPS,),
                in_specs=[
                    pl.BlockSpec((1, rows, local * chunk), lambda g, s: (lax.rem(g, 2), 0, 0)),
                    pl.BlockSpec((1, rows, local * chunk), lambda g, s: (lax.rem(g, 2), 0, 0)),
                    pl.BlockSpec((rows, features), lambda g, s: (0, 0)),
                    pl.BlockSpec((8, half), lambda g, s: (0, 0)),
                ],
                out_specs=pl.BlockSpec((local, chunk, features), lambda g, s: (0, lax.rem(s[0] + g, GROUPS), 0)),
            ),
            compiler_params=grant(12),
            cost_estimate=pl.CostEstimate(
                flops=2 * rows * local * points * features, bytes_accessed=2 * hidden.size, transcendentals=0
            ),
            name="grad_hidden",
        )(where, weighted_early, weighted_late, half_weight, piece)
        own, grad_hidden = lax.optimization_barrier((own, grad_hidden))
    with jax.named_scope("last_swap"):
        partner = lax.ppermute(own, "c", swap)
        squares = pl.pallas_call(
            lambda *refs: squares_kernel(*refs, replicas=replicas),
            out_shape=jax.ShapeDtypeStruct((8, half), F32),
            in_specs=[VMEM],
            out_specs=VMEM,
            compiler_params=grant(4),
            name="squares",
        )(own)
    with jax.named_scope("update"):
        new_weight, new_bias = pl.pallas_call(
            lambda *refs: update_kernel(*refs, replicas=replicas),
            out_shape=[
                jax.ShapeDtypeStruct((variables, features), F32),
                jax.ShapeDtypeStruct((1, variables), F32),
            ],
            in_specs=[SMEM, SMEM] + [VMEM] * 5,
            out_specs=[HBM, VMEM],
            scratch_shapes=[pltpu.VMEM((variables, features), F32), pltpu.SemaphoreType.DMA((2,))],
            compiler_params=grant(6),
            name="update",
        )(where, train_step, own, partner, squares, decoder_weight, intercept_row)
    return grad_hidden, new_weight, new_bias.reshape(variables)


def solution(mesh):
    fine = Mesh(mesh.devices.reshape(GROUPS, 8, 4, 2), ("y", "z", "x", "c"))
    space = ("z", "x", "c")
    return jax.shard_map(
        on_device,
        mesh=fine,
        in_specs=(P("y", space, None), P(), P(), P(None, space), P(), P(), P(space), P()),
        out_specs=(P("y", space, None), P(), P()),
        check_vma=False,
    )
```

```python
import jax
import jax.numpy as jnp
from jax import lax
from jax.experimental import pallas as pl
from jax.experimental.pallas import tpu as pltpu
from jax.sharding import Mesh, PartitionSpec as P

WARMUP = 1000
smooth_sq = 0.0025
fair_alpha = 0.95

GROUPS = 4
PIECES = 16
PIECE_ROWS = 7
MIB = 1024 * 1024
VMEM = pl.BlockSpec(memory_space=pltpu.VMEM)
SMEM = pl.BlockSpec(memory_space=pltpu.SMEM)
HBM = pl.BlockSpec(memory_space=pltpu.HBM)
F32 = jnp.float32
BF16 = jnp.bfloat16


def soft(d):
    return d * lax.rsqrt(d * d + smooth_sq)


def as_column(row, rows):
    n = row.shape[1]
    pick = lax.broadcasted_iota(jnp.int32, (rows, n), 0) == lax.broadcasted_iota(jnp.int32, (rows, n), 1)
    return jnp.sum(jnp.where(pick, jnp.broadcast_to(row, (rows, n)), 0.0), axis=1, keepdims=True)


def padded(value, rows):
    return jnp.concatenate([value, jnp.zeros((rows - value.shape[0], value.shape[1]), value.dtype)], axis=0)


def chunk_at(where, k, chunk):
    return pl.ds(pl.multiple_of(lax.rem(where[0] + k, GROUPS) * chunk, chunk), chunk)


def fetch_chunks(where, hidden, held, sem, ks):
    local, chunk = held.shape[1:3]
    copies = []
    for slot, k in enumerate(ks):
        points = chunk_at(where, k, chunk)
        copies.append(
            [pltpu.make_async_copy(hidden.at[m, points, :], held.at[slot, m], sem.at[slot, m]) for m in range(local)]
        )
        for copy in copies[slot]:
            copy.start()
    return copies


def decode_chunk(copies, held, half, out):
    for copy in copies:
        copy.wait()
    values = lax.dot_general(
        half[...], held[...].reshape(-1, held.shape[2]), (((1,), (1,)), ((), ())), preferred_element_type=F32
    )
    chunk = out.shape[2]
    for m in range(out.shape[0]):
        out[m] = values[:, m * chunk : (m + 1) * chunk]


def far_kernel(where, hidden, weight, out, half, held, w, sem, weight_sem):
    fetch = pltpu.make_async_copy(weight, w, weight_sem)
    fetch.start()
    (copies,) = fetch_chunks(where, hidden, held, sem, (2,))
    fetch.wait()
    half[...] = padded(w[...], half.shape[0]).astype(BF16)
    decode_chunk(copies, held.at[0], half, out)


def near_kernel(where, hidden, half, after, before, held, sem):
    copies = fetch_chunks(where, hidden, held, sem, (1, 3))
    for slot, out in enumerate((after, before)):
        decode_chunk(copies[slot], held.at[slot], half, out)


def add_pair(total, i, j, s):
    total[i] = s if total[i] is None else total[i] + s
    total[j] = -s if total[j] is None else total[j] - s


def early_pairs_kernel(here, far, shift, out):
    local = here.shape[0]
    count = 2 * local

    def tile(t, carry):
        at = pl.ds(pl.multiple_of(t * 8, 8), 8)
        r = [ref[j, at, :] + shift[at, :] for ref in (here, far) for j in range(local)]
        total = [None] * count
        for i in range(count):
            for j in range(i + 1, count):
                add_pair(total, i, j, soft(r[i] - r[j]))
        for j in range(count):
            out[j, at, :] = total[j]
        return carry

    lax.fori_loop(0, here.shape[1] // 8, tile, 0)


def late_pairs_kernel(members, here, far, after, before, shift, early, *rest):
    ins, outs, scratch = (here, far, after, before), rest[:GROUPS], rest[GROUPS]
    local = here.shape[0]
    count = early.shape[0]
    eps = (1.0 - fair_alpha) / members
    normalizer = (1.0 - eps) / (members * (members - 1))

    def tile(t, carry):
        at = pl.ds(pl.multiple_of(t * 8, 8), 8)
        r = [ref[j, at, :] + shift[at, :] for ref in ins for j in range(local)]
        total = [early[j, at, :] for j in range(count)] + [None] * (members - count)
        for i in range(members):
            for j in range(max(i + 1, count), members):
                add_pair(total, i, j, soft(r[i] - r[j]))
        for j in range(members):
            scratch[j, at, :] = soft(r[j]) * (1.0 / members) - normalizer * total[j]
        return carry

    lax.fori_loop(0, here.shape[1] // 8, tile, 0)
    for j in range(members):
        outs[j // local][j % local] = scratch[j].astype(BF16)


def local_kernel(where, hidden, half, lat, area_bin, intercept, truth, var, out, area, weight, shift, held, sem):
    copies = fetch_chunks(where, hidden, held, sem, range(GROUPS))
    rows, chunk = shift.shape
    cells, width = lat.shape
    points = area_bin.shape[1]
    bins = jnp.broadcast_to(area_bin[...], (width, points))
    level = lax.broadcasted_iota(jnp.int32, (width, points), 0)
    total = jnp.zeros((width, points), F32)
    for q in range(cells):
        column = as_column(lat[q : q + 1, :], width)
        total = total + jnp.where(bins == level + q * width, column, 0.0)
    by_point = jnp.sum(total, axis=0, keepdims=True)
    area[...] = jnp.broadcast_to(jnp.sum(by_point, axis=1, keepdims=True), area.shape)
    weight[...] = by_point * as_column(var[...], rows)
    here = chunk_at(where, 0, chunk)
    shift[...] = as_column(intercept[...], rows) - padded(truth[:, here], rows)
    decode_chunk(copies[0], held.at[0], half, out)
    for chunk_copies in copies[1:]:
        for copy in chunk_copies:
            copy.wait()


def pieces_of(acc, extra, out):
    last = lax.broadcasted_iota(jnp.int32, out.shape[1:], 0) == PIECE_ROWS
    for r in range(PIECES):
        out[r] = jnp.where(last, extra, acc[PIECE_ROWS * r : PIECE_ROWS * r + 8, :])


def weigh(where, k, bracket, weight):
    local, _, chunk = bracket.shape
    scale = weight[:, chunk_at(where, k, chunk)]
    return jnp.concatenate([(scale * bracket[m].astype(F32)).astype(BF16) for m in range(local)], axis=1)


def bias_of(w):
    ones = jnp.ones((8, w.shape[1]), BF16)
    return lax.dot_general(ones, w, (((1,), (1,)), ((), ())), preferred_element_type=F32)


def early_backward_kernel(where, held, b0, b2, weight, weighted, total, bias):
    features = held.shape[3]
    w0 = weigh(where, 0, b0, weight)
    w2 = weigh(where, 2, b2, weight)
    weighted[0], weighted[1] = w0, w2
    bias[...] = bias_of(w0) + bias_of(w2)
    total[...] = jnp.dot(
        w0, held[0].reshape(-1, features), preferred_element_type=F32
    ) + jnp.dot(w2, held[2].reshape(-1, features), preferred_element_type=F32)


def late_half(side, w1, w3, held, early, acc):
    rows = w1.shape[0]
    half = acc.shape[1]
    lanes = pl.ds(pl.multiple_of(side * half, half), half)
    acc[0:rows, :] = (
        early[:, lanes]
        + jnp.dot(w1, held[1, :, :, lanes].reshape(-1, half), preferred_element_type=F32)
        + jnp.dot(w3, held[3, :, :, lanes].reshape(-1, half), preferred_element_type=F32)
    )
    acc[rows:, :] = jnp.zeros((acc.shape[0] - rows, half), F32)


def extra_row(bias, area, half):
    row = jnp.concatenate([bias, area, jnp.zeros((1, half - 256), F32)], axis=1)
    return jnp.broadcast_to(row, (8, half))


def partner_half_kernel(where, held, b1, b3, weight, area, early, weighted, other, acc):
    w1 = weigh(where, 1, b1, weight)
    w3 = weigh(where, 3, b3, weight)
    weighted[0], weighted[1] = w1, w3
    late_half(1 - where[1], w1, w3, held, early, acc)
    pieces_of(acc, extra_row(jnp.zeros((1, 128), F32), area[...], acc.shape[1]), other)


def own_half_kernel(where, held, weighted, early, early_bias, area, mine, acc):
    rows = early.shape[0]
    w1, w3 = weighted[0], weighted[1]
    late_half(where[1], w1, w3, held, early, acc)
    bias = early_bias[...] + bias_of(w1) + bias_of(w3)
    bias = jnp.concatenate([bias[0:1], jnp.zeros((1, 128 - rows), F32)], axis=1)
    pieces_of(acc, extra_row(bias, area[...], acc.shape[1]), mine)


def grad_hidden_kernel(where, early, late, half, piece, out, *, replicas):
    first = lax.rem(pl.program_id(0), 2) == 0
    inverse = 1.0 / (piece[PIECE_ROWS : PIECE_ROWS + 1, 128:129] * (1.0 / replicas))
    chunk = out.shape[1]
    for m in range(out.shape[0]):
        lanes = slice(m * chunk, (m + 1) * chunk)
        product = lax.dot_general(
            jnp.where(first, early[0, :, lanes], late[0, :, lanes]), half[...], (((0,), (0,)), ((), ())), preferred_element_type=F32
        )
        out[m] = (product * inverse).astype(BF16)


def squares_of(pieces, inverse):
    half = pieces.shape[2]
    keep = lax.broadcasted_iota(jnp.int32, (8, half), 0) < PIECE_ROWS
    squares = jnp.zeros((8, half), F32)
    for r in range(PIECES):
        g = jnp.where(keep, pieces[r] * inverse, 0.0)
        squares = squares + g * g
    return squares


def in_order(pieces, inverse, out):
    for r in range(PIECES):
        low = PIECE_ROWS * r
        n = min(PIECE_ROWS, out.shape[0] - low)
        if n > 0:
            out[low : low + n, :] = pieces[r, 0:n, :] * inverse


def own_gradient_kernel(own, gradient, squares, *, replicas):
    inverse = 1.0 / (own[0, PIECE_ROWS : PIECE_ROWS + 1, 128:129] * (1.0 / replicas))
    squares[...] = squares_of(own, inverse)
    in_order(own, inverse, gradient)


def update_kernel(
    where, step, own, gradient, partner, squares, weight, intercept, new_weight, new_bias, other, *, replicas
):
    variables, features = weight.shape
    half = features // 2
    first = where[1] == 0
    inverse = 1.0 / (own[0, PIECE_ROWS : PIECE_ROWS + 1, 128:129] * (1.0 / replicas))
    a, b = (side[0, PIECE_ROWS : PIECE_ROWS + 1, 0:variables] for side in (own, partner))
    bias_grad = (jnp.where(first, a, b) + jnp.where(first, b, a)) * inverse
    in_order(partner, inverse, other)
    a, b = squares[...], squares_of(partner, inverse)
    both = jnp.where(first, a, b) + jnp.where(first, b, a)
    total = jnp.sum(jnp.sum(both, axis=0, keepdims=True), axis=1, keepdims=True)
    total = total + jnp.sum(bias_grad * bias_grad, axis=1, keepdims=True)
    count = variables * features + variables
    rms = jnp.sqrt(total / count + 1e-06)
    warm = (step[0] + 1).astype(F32) / WARMUP
    scale = warm * jnp.minimum(1.0, 1.0 / rms)
    a, b = gradient[...], other[...]
    new_weight[:, :half] = weight[:, :half] - scale * jnp.where(first, a, b)
    new_weight[:, half:] = weight[:, half:] - scale * jnp.where(first, b, a)
    new_bias[...] = intercept[...] - scale * bias_grad


def on_device(hidden, decoder_weight, decoder_intercept, analysis_truth, var_weight, lat_weight, area_bin, train_step):
    local, points, features = hidden.shape
    variables = decoder_weight.shape[0]
    rows = -(-variables // 8) * 8
    chunk = points // GROUPS
    members = local * GROUPS
    replicas = points * lax.axis_size("z") * lax.axis_size("x") * lax.axis_size("c") * GROUPS
    me, core = lax.axis_index("y"), lax.axis_index("c")
    where = jnp.stack([me, core]).astype(jnp.int32)

    def grant(mib):
        return pltpu.CompilerParams(vmem_limit_bytes=int(mib * MIB))

    intercept_row = decoder_intercept.reshape(1, variables)
    var_row = var_weight.reshape(1, variables)

    def turn(value, k):
        return value if k % GROUPS == 0 else lax.ppermute(value, "y", [(i, (i + k) % GROUPS) for i in range(GROUPS)])

    one_residual = jax.ShapeDtypeStruct((local, rows, chunk), F32)
    with jax.named_scope("forward_far"):
        far, half_weight = pl.pallas_call(
            far_kernel,
            out_shape=[one_residual, jax.ShapeDtypeStruct((rows, features), BF16)],
            in_specs=[SMEM, HBM, HBM],
            out_specs=[VMEM] * 2,
            scratch_shapes=[
                pltpu.VMEM((1, local, chunk, features), BF16),
                pltpu.VMEM((variables, features), F32),
                pltpu.SemaphoreType.DMA((1, local)),
                pltpu.SemaphoreType.DMA(()),
            ],
            compiler_params=grant(53.4),
            name="forward_far",
        )(where, hidden, decoder_weight)
        far = turn(far, 2)
    with jax.named_scope("forward_near"):
        after, before = pl.pallas_call(
            near_kernel,
            out_shape=[one_residual] * 2,
            in_specs=[SMEM, HBM, VMEM],
            out_specs=[VMEM] * 2,
            scratch_shapes=[
                pltpu.VMEM((2, local, chunk, features), BF16),
                pltpu.SemaphoreType.DMA((2, local)),
            ],
            compiler_params=grant(52),
            cost_estimate=pl.CostEstimate(
                flops=4 * rows * local * chunk * features, bytes_accessed=4 * local * chunk * features, transcendentals=0
            ),
            name="forward_near",
        )(where, hidden, half_weight)
        after, before = turn(after, 1), turn(before, 3)
    with jax.named_scope("forward_local"):
        here, area, point_weight, shift, held = pl.pallas_call(
            local_kernel,
            out_shape=[
                one_residual,
                jax.ShapeDtypeStruct((1, 128), F32),
                jax.ShapeDtypeStruct((rows, points), F32),
                jax.ShapeDtypeStruct((rows, chunk), F32),
                jax.ShapeDtypeStruct((GROUPS, local, chunk, features), BF16),
            ],
            in_specs=[SMEM, HBM] + [VMEM] * 6,
            out_specs=[VMEM] * 5,
            scratch_shapes=[pltpu.SemaphoreType.DMA((GROUPS, local))],
            compiler_params=grant(46),
            name="forward_local",
        )(where, hidden, half_weight, lat_weight.reshape(-1, 128), area_bin.reshape(1, points), intercept_row, analysis_truth, var_row)
    with jax.named_scope("early_pairs"):
        early = pl.pallas_call(
            early_pairs_kernel,
            out_shape=jax.ShapeDtypeStruct((2 * local, rows, chunk), F32),
            in_specs=[VMEM] * 3,
            out_specs=VMEM,
            compiler_params=grant(4),
            name="early_pairs",
        )(here, far, shift)
    after, before, early, point_weight, held = lax.optimization_barrier((after, before, early, point_weight, held))
    with jax.named_scope("late_pairs"):
        brackets = pl.pallas_call(
            lambda *refs: late_pairs_kernel(members, *refs),
            out_shape=[jax.ShapeDtypeStruct((local, rows, chunk), BF16)] * GROUPS,
            in_specs=[VMEM] * (GROUPS + 2),
            out_specs=[VMEM] * GROUPS,
            scratch_shapes=[pltpu.VMEM((members, rows, chunk), F32)],
            compiler_params=grant(6),
            name="late_pairs",
        )(here, far, after, before, shift, early)
    with jax.named_scope("bracket_exchange"):
        returned = [brackets[0], turn(brackets[2], -1), turn(brackets[1], -2), turn(brackets[3], -3)]
    half = features // 2
    pieces = jax.ShapeDtypeStruct((PIECES, 8, half), F32)
    two_weighted = jax.ShapeDtypeStruct((GROUPS // 2, rows, local * chunk), BF16)
    sums = [pltpu.VMEM((PIECES * 8, half), F32)]
    with jax.named_scope("early_backward"):
        weighted_early, early_sum, early_bias = pl.pallas_call(
            early_backward_kernel,
            out_shape=[
                two_weighted,
                jax.ShapeDtypeStruct((rows, features), F32),
                jax.ShapeDtypeStruct((8, rows), F32),
            ],
            in_specs=[SMEM] + [VMEM] * 4,
            out_specs=[VMEM] * 3,
            compiler_params=grant(10),
            name="early_backward",
        )(where, held, returned[0], returned[2], point_weight)
    with jax.named_scope("backward_partner_half"):
        weighted_late, other = pl.pallas_call(
            partner_half_kernel,
            out_shape=[two_weighted, pieces],
            in_specs=[SMEM] + [VMEM] * 6,
            out_specs=[VMEM] * 2,
            scratch_shapes=sums,
            compiler_params=grant(10),
            name="backward_partner_half",
        )(where, held, returned[1], returned[3], point_weight, area, early_sum)
        swap = [(0, 1), (1, 0)]
        other = lax.ppermute(other, "c", swap)
    with jax.named_scope("backward_own_half"):
        mine = pl.pallas_call(
            own_half_kernel,
            out_shape=pieces,
            in_specs=[SMEM] + [VMEM] * 5,
            out_specs=VMEM,
            scratch_shapes=sums,
            compiler_params=grant(10),
            name="backward_own_half",
        )(where, held, weighted_late, early_sum, early_bias, area)
    with jax.named_scope("gradient_sum"):
        part = mine + other
        part = lax.all_to_all(part, ("x", "y"), 0, 0, tiled=True)
        depth = lax.axis_size("z")
        part = jnp.broadcast_to(jnp.sum(part, axis=0), (depth, 8, half))
        part = lax.all_to_all(part, "z", 0, 0, tiled=True)
        piece = jnp.sum(part, axis=0)
        own = lax.all_to_all(jnp.broadcast_to(piece, (PIECES, 8, half)), ("x", "y"), 0, 0, tiled=True)
    with jax.named_scope("grad_hidden"):
        grad_hidden = pl.pallas_call(
            lambda *refs: grad_hidden_kernel(*refs, replicas=replicas),
            out_shape=jax.ShapeDtypeStruct(hidden.shape, BF16),
            grid_spec=pltpu.PrefetchScalarGridSpec(
                num_scalar_prefetch=1,
                grid=(GROUPS,),
                in_specs=[
                    pl.BlockSpec((1, rows, local * chunk), lambda g, s: (lax.div(g, 2), 0, 0)),
                    pl.BlockSpec((1, rows, local * chunk), lambda g, s: (lax.div(g, 2), 0, 0)),
                    pl.BlockSpec((rows, features), lambda g, s: (0, 0)),
                    pl.BlockSpec((8, half), lambda g, s: (0, 0)),
                ],
                out_specs=pl.BlockSpec((local, chunk, features), lambda g, s: (0, lax.rem(s[0] + g, GROUPS), 0)),
            ),
            compiler_params=grant(12),
            cost_estimate=pl.CostEstimate(
                flops=2 * rows * local * points * features, bytes_accessed=2 * hidden.size, transcendentals=0
            ),
            name="grad_hidden",
        )(where, weighted_early, weighted_late, half_weight, piece)
        own, grad_hidden = lax.optimization_barrier((own, grad_hidden))
    with jax.named_scope("last_swap"):
        partner = lax.ppermute(own, "c", swap)
        gradient, squares = pl.pallas_call(
            lambda *refs: own_gradient_kernel(*refs, replicas=replicas),
            out_shape=[jax.ShapeDtypeStruct((variables, half), F32), jax.ShapeDtypeStruct((8, half), F32)],
            in_specs=[VMEM],
            out_specs=[VMEM] * 2,
            compiler_params=grant(4),
            name="own_gradient",
        )(own)
    with jax.named_scope("update"):
        new_weight, new_bias = pl.pallas_call(
            lambda *refs: update_kernel(*refs, replicas=replicas),
            out_shape=[
                jax.ShapeDtypeStruct((variables, features), F32),
                jax.ShapeDtypeStruct((1, variables), F32),
            ],
            in_specs=[SMEM, SMEM] + [VMEM] * 6,
            out_specs=[VMEM] * 2,
            scratch_shapes=[pltpu.VMEM((variables, half), F32)],
            compiler_params=grant(6),
            name="update",
        )(where, train_step, own, gradient, partner, squares, decoder_weight, intercept_row)
    return grad_hidden, new_weight, new_bias.reshape(variables)


def solution(mesh):
    fine = Mesh(mesh.devices.reshape(GROUPS, 8, 4, 2), ("y", "z", "x", "c"))
    space = ("z", "x", "c")
    return jax.shard_map(
        on_device,
        mesh=fine,
        in_specs=(P("y", space, None), P(), P(), P(None, space), P(), P(), P(space), P()),
        out_specs=(P("y", space, None), P(), P()),
        check_vma=False,
    )
```

```python
import jax
import jax.numpy as jnp
from jax import lax
from jax.experimental import pallas as pl
from jax.experimental.pallas import tpu as pltpu
from jax.sharding import Mesh, PartitionSpec as P

WARMUP = 1000
smooth_sq = 0.0025
fair_alpha = 0.95

GROUPS = 4
PIECES = 16
PIECE_ROWS = 7
MIB = 1024 * 1024
VMEM = pl.BlockSpec(memory_space=pltpu.VMEM)
SMEM = pl.BlockSpec(memory_space=pltpu.SMEM)
HBM = pl.BlockSpec(memory_space=pltpu.HBM)
F32 = jnp.float32
BF16 = jnp.bfloat16


def soft(d):
    return d * lax.rsqrt(d * d + smooth_sq)


def as_column(row, rows):
    n = row.shape[1]
    pick = lax.broadcasted_iota(jnp.int32, (rows, n), 0) == lax.broadcasted_iota(jnp.int32, (rows, n), 1)
    return jnp.sum(jnp.where(pick, jnp.broadcast_to(row, (rows, n)), 0.0), axis=1, keepdims=True)


def padded(value, rows):
    return jnp.concatenate([value, jnp.zeros((rows - value.shape[0], value.shape[1]), value.dtype)], axis=0)


def chunk_at(where, k, chunk):
    return pl.ds(pl.multiple_of(lax.rem(where[0] + k, GROUPS) * chunk, chunk), chunk)


def fetch_chunks(where, hidden, held, sem, ks):
    local, chunk = held.shape[1:3]
    copies = []
    for slot, k in enumerate(ks):
        points = chunk_at(where, k, chunk)
        copies.append(
            [pltpu.make_async_copy(hidden.at[m, points, :], held.at[slot, m], sem.at[slot, m]) for m in range(local)]
        )
        for copy in copies[slot]:
            copy.start()
    return copies


def decode_chunk(copies, held, half, out):
    for copy in copies:
        copy.wait()
    values = lax.dot_general(
        half[...], held[...].reshape(-1, held.shape[2]), (((1,), (1,)), ((), ())), preferred_element_type=F32
    )
    chunk = out.shape[2]
    for m in range(out.shape[0]):
        out[m] = values[:, m * chunk : (m + 1) * chunk]


def far_kernel(where, hidden, weight, out, half, held, w, sem, weight_sem):
    fetch = pltpu.make_async_copy(weight, w, weight_sem)
    fetch.start()
    (copies,) = fetch_chunks(where, hidden, held, sem, (2,))
    fetch.wait()
    half[...] = padded(w[...], half.shape[0]).astype(BF16)
    decode_chunk(copies, held.at[0], half, out)


def near_kernel(where, hidden, half, after, before, held, sem):
    copies = fetch_chunks(where, hidden, held, sem, (1, 3))
    for slot, out in enumerate((after, before)):
        decode_chunk(copies[slot], held.at[slot], half, out)


def add_pair(total, i, j, s):
    total[i] = s if total[i] is None else total[i] + s
    total[j] = -s if total[j] is None else total[j] - s


def pair_normalizer(members):
    eps = (1.0 - fair_alpha) / members
    return (1.0 - eps) / (members * (members - 1))


def early_pairs_kernel(members, here, far, shift, out):
    normalizer = pair_normalizer(members)
    local = here.shape[0]
    count = 2 * local

    def tile(t, carry):
        at = pl.ds(pl.multiple_of(t * 8, 8), 8)
        r = [ref[j, at, :] + shift[at, :] for ref in (here, far) for j in range(local)]
        total = [None] * count
        for i in range(count):
            for j in range(i + 1, count):
                add_pair(total, i, j, soft(r[i] - r[j]))
        for j in range(count):
            out[j, at, :] = soft(r[j]) * (1.0 / members) - normalizer * total[j]
        return carry

    lax.fori_loop(0, here.shape[1] // 8, tile, 0)


def late_pairs_kernel(members, here, far, after, before, shift, early, *rest):
    ins, outs, scratch = (here, far, after, before), rest[:GROUPS], rest[GROUPS]
    local = here.shape[0]
    count = early.shape[0]
    normalizer = pair_normalizer(members)

    def tile(t, carry):
        at = pl.ds(pl.multiple_of(t * 8, 8), 8)
        r = [ref[j, at, :] + shift[at, :] for ref in ins for j in range(local)]
        total = [None] * members
        for i in range(members):
            for j in range(max(i + 1, count), members):
                add_pair(total, i, j, soft(r[i] - r[j]))
        for j in range(members):
            base = early[j, at, :] if j < count else soft(r[j]) * (1.0 / members)
            scratch[j, at, :] = base - normalizer * total[j]
        return carry

    lax.fori_loop(0, here.shape[1] // 8, tile, 0)
    for j in range(members):
        outs[j // local][j % local] = scratch[j].astype(BF16)


def local_kernel(where, hidden, half, lat, area_bin, intercept, truth, var, out, area, weight, shift, held, sem):
    copies = fetch_chunks(where, hidden, held, sem, range(GROUPS))
    rows, chunk = shift.shape
    cells, width = lat.shape
    points = area_bin.shape[1]
    bins = jnp.broadcast_to(area_bin[...], (width, points))
    level = lax.broadcasted_iota(jnp.int32, (width, points), 0)
    total = jnp.zeros((width, points), F32)
    for q in range(cells):
        column = as_column(lat[q : q + 1, :], width)
        total = total + jnp.where(bins == level + q * width, column, 0.0)
    by_point = jnp.sum(total, axis=0, keepdims=True)
    area[...] = jnp.broadcast_to(jnp.sum(by_point, axis=1, keepdims=True), area.shape)
    weight[...] = by_point * as_column(var[...], rows)
    here = chunk_at(where, 0, chunk)
    shift[...] = as_column(intercept[...], rows) - padded(truth[:, here], rows)
    decode_chunk(copies[0], held.at[0], half, out)
    for chunk_copies in copies[1:]:
        for copy in chunk_copies:
            copy.wait()


def pieces_of(acc, extra, out):
    last = lax.broadcasted_iota(jnp.int32, out.shape[1:], 0) == PIECE_ROWS
    for r in range(PIECES):
        out[r] = jnp.where(last, extra, acc[PIECE_ROWS * r : PIECE_ROWS * r + 8, :])


def weigh(where, k, bracket, weight):
    local, _, chunk = bracket.shape
    scale = weight[:, chunk_at(where, k, chunk)]
    return jnp.concatenate([(scale * bracket[m].astype(F32)).astype(BF16) for m in range(local)], axis=1)


def bias_of(w):
    ones = jnp.ones((8, w.shape[1]), BF16)
    return lax.dot_general(ones, w, (((1,), (1,)), ((), ())), preferred_element_type=F32)


def early_backward_kernel(where, held, b0, b2, weight, weighted, total, bias):
    features = held.shape[3]
    w0 = weigh(where, 0, b0, weight)
    w2 = weigh(where, 2, b2, weight)
    weighted[0], weighted[1] = w0, w2
    bias[...] = bias_of(w0) + bias_of(w2)
    total[...] = jnp.dot(
        w0, held[0].reshape(-1, features), preferred_element_type=F32
    ) + jnp.dot(w2, held[2].reshape(-1, features), preferred_element_type=F32)


def late_half(side, w1, w3, held, early, acc):
    rows = w1.shape[0]
    half = acc.shape[1]
    lanes = pl.ds(pl.multiple_of(side * half, half), half)
    acc[0:rows, :] = (
        early[:, lanes]
        + jnp.dot(w1, held[1, :, :, lanes].reshape(-1, half), preferred_element_type=F32)
        + jnp.dot(w3, held[3, :, :, lanes].reshape(-1, half), preferred_element_type=F32)
    )
    acc[rows:, :] = jnp.zeros((acc.shape[0] - rows, half), F32)


def extra_row(bias, area, half):
    row = jnp.concatenate([bias, area, jnp.zeros((1, half - 256), F32)], axis=1)
    return jnp.broadcast_to(row, (8, half))


def partner_half_kernel(where, held, b1, b3, weight, area, early, weighted, other, acc):
    w1 = weigh(where, 1, b1, weight)
    w3 = weigh(where, 3, b3, weight)
    weighted[0], weighted[1] = w1, w3
    late_half(1 - where[1], w1, w3, held, early, acc)
    pieces_of(acc, extra_row(jnp.zeros((1, 128), F32), area[...], acc.shape[1]), other)


def own_half_kernel(where, held, weighted, early, early_bias, area, mine, acc):
    rows = early.shape[0]
    w1, w3 = weighted[0], weighted[1]
    late_half(where[1], w1, w3, held, early, acc)
    bias = early_bias[...] + bias_of(w1) + bias_of(w3)
    bias = jnp.concatenate([bias[0:1], jnp.zeros((1, 128 - rows), F32)], axis=1)
    pieces_of(acc, extra_row(bias, area[...], acc.shape[1]), mine)


def sum_kernel(parts, piece, copies_out, sem):
    total = parts[0]
    for k in range(1, parts.shape[0]):
        total = total + parts[k]
    piece[...] = total
    copies = [pltpu.make_async_copy(piece, copies_out.at[r], sem.at[r]) for r in range(PIECES)]
    for copy in copies:
        copy.start()
    for copy in copies:
        copy.wait()


def grad_hidden_kernel(where, early, late, half, piece, out, *, replicas):
    first = lax.rem(pl.program_id(0), 2) == 0
    inverse = 1.0 / (piece[PIECE_ROWS : PIECE_ROWS + 1, 128:129] * (1.0 / replicas))
    chunk = out.shape[1]
    for m in range(out.shape[0]):
        lanes = slice(m * chunk, (m + 1) * chunk)
        product = lax.dot_general(
            jnp.where(first, early[0, :, lanes], late[0, :, lanes]), half[...], (((0,), (0,)), ((), ())), preferred_element_type=F32
        )
        out[m] = (product * inverse).astype(BF16)


def squares_of(pieces, inverse):
    half = pieces.shape[2]
    keep = lax.broadcasted_iota(jnp.int32, (8, half), 0) < PIECE_ROWS
    squares = jnp.zeros((8, half), F32)
    for r in range(PIECES):
        g = jnp.where(keep, pieces[r] * inverse, 0.0)
        squares = squares + g * g
    return squares


def in_order(pieces, inverse, out):
    for r in range(PIECES):
        low = PIECE_ROWS * r
        n = min(PIECE_ROWS, out.shape[0] - low)
        if n > 0:
            out[low : low + n, :] = pieces[r, 0:n, :] * inverse


def own_gradient_kernel(own, gradient, squares, *, replicas):
    inverse = 1.0 / (own[0, PIECE_ROWS : PIECE_ROWS + 1, 128:129] * (1.0 / replicas))
    squares[...] = squares_of(own, inverse)
    in_order(own, inverse, gradient)


def update_kernel(
    where, step, own, gradient, partner, squares, weight, intercept, new_weight, new_bias, other, *, replicas
):
    variables, features = weight.shape
    half = features // 2
    first = where[1] == 0
    inverse = 1.0 / (own[0, PIECE_ROWS : PIECE_ROWS + 1, 128:129] * (1.0 / replicas))
    a, b = (side[0, PIECE_ROWS : PIECE_ROWS + 1, 0:variables] for side in (own, partner))
    bias_grad = (jnp.where(first, a, b) + jnp.where(first, b, a)) * inverse
    in_order(partner, inverse, other)
    a, b = squares[...], squares_of(partner, inverse)
    both = jnp.where(first, a, b) + jnp.where(first, b, a)
    total = jnp.sum(jnp.sum(both, axis=0, keepdims=True), axis=1, keepdims=True)
    total = total + jnp.sum(bias_grad * bias_grad, axis=1, keepdims=True)
    count = variables * features + variables
    rms = jnp.sqrt(total / count + 1e-06)
    warm = (step[0] + 1).astype(F32) / WARMUP
    scale = warm * jnp.minimum(1.0, 1.0 / rms)
    a, b = gradient[...], other[...]
    new_weight[:, :half] = weight[:, :half] - scale * jnp.where(first, a, b)
    new_weight[:, half:] = weight[:, half:] - scale * jnp.where(first, b, a)
    new_bias[...] = intercept[...] - scale * bias_grad


def on_device(hidden, decoder_weight, decoder_intercept, analysis_truth, var_weight, lat_weight, area_bin, train_step):
    local, points, features = hidden.shape
    variables = decoder_weight.shape[0]
    rows = -(-variables // 8) * 8
    chunk = points // GROUPS
    members = local * GROUPS
    replicas = points * lax.axis_size("z") * lax.axis_size("x") * lax.axis_size("c") * GROUPS
    me, core = lax.axis_index("y"), lax.axis_index("c")
    where = jnp.stack([me, core]).astype(jnp.int32)

    def grant(mib):
        return pltpu.CompilerParams(vmem_limit_bytes=int(mib * MIB))

    intercept_row = decoder_intercept.reshape(1, variables)
    var_row = var_weight.reshape(1, variables)

    def turn(value, k):
        return value if k % GROUPS == 0 else lax.ppermute(value, "y", [(i, (i + k) % GROUPS) for i in range(GROUPS)])

    one_residual = jax.ShapeDtypeStruct((local, rows, chunk), F32)
    with jax.named_scope("forward_far"):
        far, half_weight = pl.pallas_call(
            far_kernel,
            out_shape=[one_residual, jax.ShapeDtypeStruct((rows, features), BF16)],
            in_specs=[SMEM, HBM, HBM],
            out_specs=[VMEM] * 2,
            scratch_shapes=[
                pltpu.VMEM((1, local, chunk, features), BF16),
                pltpu.VMEM((variables, features), F32),
                pltpu.SemaphoreType.DMA((1, local)),
                pltpu.SemaphoreType.DMA(()),
            ],
            compiler_params=grant(53.4),
            name="forward_far",
        )(where, hidden, decoder_weight)
        far = turn(far, 2)
    with jax.named_scope("forward_near"):
        after, before = pl.pallas_call(
            near_kernel,
            out_shape=[one_residual] * 2,
            in_specs=[SMEM, HBM, VMEM],
            out_specs=[VMEM] * 2,
            scratch_shapes=[
                pltpu.VMEM((2, local, chunk, features), BF16),
                pltpu.SemaphoreType.DMA((2, local)),
            ],
            compiler_params=grant(52),
            cost_estimate=pl.CostEstimate(
                flops=4 * rows * local * chunk * features, bytes_accessed=4 * local * chunk * features, transcendentals=0
            ),
            name="forward_near",
        )(where, hidden, half_weight)
        after, before = turn(after, 1), turn(before, 3)
    with jax.named_scope("forward_local"):
        here, area, point_weight, shift, held = pl.pallas_call(
            local_kernel,
            out_shape=[
                one_residual,
                jax.ShapeDtypeStruct((1, 128), F32),
                jax.ShapeDtypeStruct((rows, points), F32),
                jax.ShapeDtypeStruct((rows, chunk), F32),
                jax.ShapeDtypeStruct((GROUPS, local, chunk, features), BF16),
            ],
            in_specs=[SMEM, HBM] + [VMEM] * 6,
            out_specs=[VMEM] * 5,
            scratch_shapes=[pltpu.SemaphoreType.DMA((GROUPS, local))],
            compiler_params=grant(46),
            name="forward_local",
        )(where, hidden, half_weight, lat_weight.reshape(-1, 128), area_bin.reshape(1, points), intercept_row, analysis_truth, var_row)
    with jax.named_scope("early_pairs"):
        early = pl.pallas_call(
            lambda *refs: early_pairs_kernel(members, *refs),
            out_shape=jax.ShapeDtypeStruct((2 * local, rows, chunk), F32),
            in_specs=[VMEM] * 3,
            out_specs=VMEM,
            compiler_params=grant(4),
            name="early_pairs",
        )(here, far, shift)
    after, before, early, point_weight, held = lax.optimization_barrier((after, before, early, point_weight, held))
    with jax.named_scope("late_pairs"):
        brackets = pl.pallas_call(
            lambda *refs: late_pairs_kernel(members, *refs),
            out_shape=[jax.ShapeDtypeStruct((local, rows, chunk), BF16)] * GROUPS,
            in_specs=[VMEM] * (GROUPS + 2),
            out_specs=[VMEM] * GROUPS,
            scratch_shapes=[pltpu.VMEM((members, rows, chunk), F32)],
            compiler_params=grant(6),
            name="late_pairs",
        )(here, far, after, before, shift, early)
    with jax.named_scope("bracket_exchange"):
        returned = [brackets[0], turn(brackets[2], -1), turn(brackets[1], -2), turn(brackets[3], -3)]
    half = features // 2
    pieces = jax.ShapeDtypeStruct((PIECES, 8, half), F32)
    two_weighted = jax.ShapeDtypeStruct((GROUPS // 2, rows, local * chunk), BF16)
    sums = [pltpu.VMEM((PIECES * 8, half), F32)]
    with jax.named_scope("early_backward"):
        weighted_early, early_sum, early_bias = pl.pallas_call(
            early_backward_kernel,
            out_shape=[
                two_weighted,
                jax.ShapeDtypeStruct((rows, features), F32),
                jax.ShapeDtypeStruct((8, rows), F32),
            ],
            in_specs=[SMEM] + [VMEM] * 4,
            out_specs=[VMEM] * 3,
            compiler_params=grant(10),
            name="early_backward",
        )(where, held, returned[0], returned[2], point_weight)
    with jax.named_scope("backward_partner_half"):
        weighted_late, other = pl.pallas_call(
            partner_half_kernel,
            out_shape=[two_weighted, pieces],
            in_specs=[SMEM] + [VMEM] * 6,
            out_specs=[VMEM] * 2,
            scratch_shapes=sums,
            compiler_params=grant(10),
            name="backward_partner_half",
        )(where, held, returned[1], returned[3], point_weight, area, early_sum)
        swap = [(0, 1), (1, 0)]
        other = lax.ppermute(other, "c", swap)
    with jax.named_scope("backward_own_half"):
        mine = pl.pallas_call(
            own_half_kernel,
            out_shape=pieces,
            in_specs=[SMEM] + [VMEM] * 5,
            out_specs=VMEM,
            scratch_shapes=sums,
            compiler_params=grant(10),
            name="backward_own_half",
        )(where, held, weighted_late, early_sum, early_bias, area)
    with jax.named_scope("gradient_sum"):
        part = mine + other
        part = lax.all_to_all(part, ("x", "y"), 0, 0, tiled=True)
        depth = lax.axis_size("z")
        part = jnp.broadcast_to(jnp.sum(part, axis=0), (depth, 8, half))
        part = lax.all_to_all(part, "z", 0, 0, tiled=True)
        piece, outgoing = pl.pallas_call(
            sum_kernel,
            out_shape=[jax.ShapeDtypeStruct((8, half), F32), pieces],
            in_specs=[VMEM],
            out_specs=[VMEM, HBM],
            scratch_shapes=[pltpu.SemaphoreType.DMA((PIECES,))],
            compiler_params=grant(4),
            name="sum_pieces",
        )(part)
        own = lax.all_to_all(outgoing, ("x", "y"), 0, 0, tiled=True)
    with jax.named_scope("grad_hidden"):
        grad_hidden = pl.pallas_call(
            lambda *refs: grad_hidden_kernel(*refs, replicas=replicas),
            out_shape=jax.ShapeDtypeStruct(hidden.shape, BF16),
            grid_spec=pltpu.PrefetchScalarGridSpec(
                num_scalar_prefetch=1,
                grid=(GROUPS,),
                in_specs=[
                    pl.BlockSpec((1, rows, local * chunk), lambda g, s: (lax.div(g, 2), 0, 0)),
                    pl.BlockSpec((1, rows, local * chunk), lambda g, s: (lax.div(g, 2), 0, 0)),
                    pl.BlockSpec((rows, features), lambda g, s: (0, 0)),
                    pl.BlockSpec((8, half), lambda g, s: (0, 0)),
                ],
                out_specs=pl.BlockSpec((local, chunk, features), lambda g, s: (0, lax.rem(s[0] + g, GROUPS), 0)),
            ),
            compiler_params=grant(12),
            cost_estimate=pl.CostEstimate(
                flops=2 * rows * local * points * features, bytes_accessed=2 * hidden.size, transcendentals=0
            ),
            name="grad_hidden",
        )(where, weighted_early, weighted_late, half_weight, piece)
        own, grad_hidden = lax.optimization_barrier((own, grad_hidden))
    with jax.named_scope("last_swap"):
        partner = lax.ppermute(own, "c", swap)
        gradient, squares = pl.pallas_call(
            lambda *refs: own_gradient_kernel(*refs, replicas=replicas),
            out_shape=[jax.ShapeDtypeStruct((variables, half), F32), jax.ShapeDtypeStruct((8, half), F32)],
            in_specs=[VMEM],
            out_specs=[VMEM] * 2,
            compiler_params=grant(4),
            name="own_gradient",
        )(own)
    with jax.named_scope("update"):
        new_weight, new_bias = pl.pallas_call(
            lambda *refs: update_kernel(*refs, replicas=replicas),
            out_shape=[
                jax.ShapeDtypeStruct((variables, features), F32),
                jax.ShapeDtypeStruct((1, variables), F32),
            ],
            in_specs=[SMEM, SMEM] + [VMEM] * 6,
            out_specs=[VMEM] * 2,
            scratch_shapes=[pltpu.VMEM((variables, half), F32)],
            compiler_params=grant(6),
            name="update",
        )(where, train_step, own, gradient, partner, squares, decoder_weight, intercept_row)
    return grad_hidden, new_weight, new_bias.reshape(variables)


def solution(mesh):
    fine = Mesh(mesh.devices.reshape(GROUPS, 8, 4, 2), ("y", "z", "x", "c"))
    space = ("z", "x", "c")
    return jax.shard_map(
        on_device,
        mesh=fine,
        in_specs=(P("y", space, None), P(), P(), P(None, space), P(), P(), P(space), P()),
        out_specs=(P("y", space, None), P(), P()),
        check_vma=False,
    )
```

```python
import jax
import jax.numpy as jnp
from jax import lax
from jax.experimental import pallas as pl
from jax.experimental.pallas import tpu as pltpu
from jax.sharding import Mesh, PartitionSpec as P

WARMUP = 1000
smooth_sq = 0.0025
fair_alpha = 0.95

GROUPS = 4
PIECES = 16
PIECE_ROWS = 7
MIB = 1024 * 1024
VMEM = pl.BlockSpec(memory_space=pltpu.VMEM)
SMEM = pl.BlockSpec(memory_space=pltpu.SMEM)
HBM = pl.BlockSpec(memory_space=pltpu.HBM)
F32 = jnp.float32
BF16 = jnp.bfloat16


def soft(d):
    return d * lax.rsqrt(d * d + smooth_sq)


def as_column(row, rows):
    n = row.shape[1]
    pick = lax.broadcasted_iota(jnp.int32, (rows, n), 0) == lax.broadcasted_iota(jnp.int32, (rows, n), 1)
    return jnp.sum(jnp.where(pick, jnp.broadcast_to(row, (rows, n)), 0.0), axis=1, keepdims=True)


def padded(value, rows):
    return jnp.concatenate([value, jnp.zeros((rows - value.shape[0], value.shape[1]), value.dtype)], axis=0)


def chunk_at(where, k, chunk):
    return pl.ds(pl.multiple_of(lax.rem(where[0] + k, GROUPS) * chunk, chunk), chunk)


def fetch_chunks(where, hidden, held, sem, ks):
    local, chunk = held.shape[1:3]
    copies = []
    for slot, k in enumerate(ks):
        points = chunk_at(where, k, chunk)
        copies.append(
            [pltpu.make_async_copy(hidden.at[m, points, :], held.at[slot, m], sem.at[slot, m]) for m in range(local)]
        )
        for copy in copies[slot]:
            copy.start()
    return copies


def decode_chunk(copies, held, half, out):
    for copy in copies:
        copy.wait()
    values = lax.dot_general(
        half[...], held[...].reshape(-1, held.shape[2]), (((1,), (1,)), ((), ())), preferred_element_type=F32
    )
    chunk = out.shape[2]
    for m in range(out.shape[0]):
        out[m] = values[:, m * chunk : (m + 1) * chunk]


def far_kernel(where, hidden, weight, out, half, held, w, sem, weight_sem):
    fetch = pltpu.make_async_copy(weight, w, weight_sem)
    fetch.start()
    (copies,) = fetch_chunks(where, hidden, held, sem, (2,))
    fetch.wait()
    half[...] = padded(w[...], half.shape[0]).astype(BF16)
    decode_chunk(copies, held.at[0], half, out)


def near_kernel(where, hidden, half, after, before, held, sem):
    copies = fetch_chunks(where, hidden, held, sem, (1, 3))
    for slot, out in enumerate((after, before)):
        decode_chunk(copies[slot], held.at[slot], half, out)


def add_pair(total, i, j, s):
    total[i] = s if total[i] is None else total[i] + s
    total[j] = -s if total[j] is None else total[j] - s


def pair_normalizer(members):
    eps = (1.0 - fair_alpha) / members
    return (1.0 - eps) / (members * (members - 1))


def early_pairs_kernel(members, here, far, shift, out):
    normalizer = pair_normalizer(members)
    local = here.shape[0]
    count = 2 * local

    def tile(t, carry):
        at = pl.ds(pl.multiple_of(t * 8, 8), 8)
        r = [ref[j, at, :] + shift[at, :] for ref in (here, far) for j in range(local)]
        total = [None] * count
        for i in range(count):
            for j in range(i + 1, count):
                add_pair(total, i, j, soft(r[i] - r[j]))
        for j in range(count):
            out[j, at, :] = soft(r[j]) * (1.0 / members) - normalizer * total[j]
        return carry

    lax.fori_loop(0, here.shape[1] // 8, tile, 0)


def late_pairs_kernel(members, here, far, after, before, shift, early, *rest):
    ins, outs, scratch = (here, far, after, before), rest[:GROUPS], rest[GROUPS]
    local = here.shape[0]
    count = early.shape[0]
    normalizer = pair_normalizer(members)

    def tile(t, carry):
        at = pl.ds(pl.multiple_of(t * 8, 8), 8)
        r = [ref[j, at, :] + shift[at, :] for ref in ins for j in range(local)]
        total = [None] * members
        for i in range(members):
            for j in range(max(i + 1, count), members):
                add_pair(total, i, j, soft(r[i] - r[j]))
        for j in range(members):
            base = early[j, at, :] if j < count else soft(r[j]) * (1.0 / members)
            scratch[j, at, :] = base - normalizer * total[j]
        return carry

    lax.fori_loop(0, here.shape[1] // 8, tile, 0)
    for j in range(members):
        outs[j // local][j % local] = scratch[j].astype(BF16)


def local_kernel(where, hidden, half, lat, area_bin, intercept, truth, var, out, area, weight, shift, held, sem):
    copies = fetch_chunks(where, hidden, held, sem, range(GROUPS))
    rows, chunk = shift.shape
    cells, width = lat.shape
    points = area_bin.shape[1]
    bins = jnp.broadcast_to(area_bin[...], (width, points))
    level = lax.broadcasted_iota(jnp.int32, (width, points), 0)
    total = jnp.zeros((width, points), F32)
    for q in range(cells):
        column = as_column(lat[q : q + 1, :], width)
        total = total + jnp.where(bins == level + q * width, column, 0.0)
    by_point = jnp.sum(total, axis=0, keepdims=True)
    area[...] = jnp.broadcast_to(jnp.sum(by_point, axis=1, keepdims=True), area.shape)
    weight[...] = by_point * as_column(var[...], rows)
    here = chunk_at(where, 0, chunk)
    shift[...] = as_column(intercept[...], rows) - padded(truth[:, here], rows)
    decode_chunk(copies[0], held.at[0], half, out)
    for chunk_copies in copies[1:]:
        for copy in chunk_copies:
            copy.wait()


def pieces_of(acc, extra, out):
    last = lax.broadcasted_iota(jnp.int32, out.shape[1:], 0) == PIECE_ROWS
    for r in range(PIECES):
        out[r] = jnp.where(last, extra, acc[PIECE_ROWS * r : PIECE_ROWS * r + 8, :])


def weigh(where, k, bracket, weight):
    local, _, chunk = bracket.shape
    scale = weight[:, chunk_at(where, k, chunk)]
    return jnp.concatenate([(scale * bracket[m].astype(F32)).astype(BF16) for m in range(local)], axis=1)


def bias_of(w):
    ones = jnp.ones((8, w.shape[1]), BF16)
    return lax.dot_general(ones, w, (((1,), (1,)), ((), ())), preferred_element_type=F32)


def early_backward_kernel(where, held, b0, weight, weighted, total, bias):
    w = weigh(where, 0, b0, weight)
    weighted[0] = w
    bias[...] = bias_of(w)
    total[...] = jnp.dot(w, held[0].reshape(-1, held.shape[3]), preferred_element_type=F32)


def late_half(side, ws, held, early, acc):
    rows = early.shape[0]
    half = acc.shape[1]
    lanes = pl.ds(pl.multiple_of(side * half, half), half)
    total = early[:, lanes]
    for k, w in enumerate(ws, 1):
        total = total + jnp.dot(w, held[k, :, :, lanes].reshape(-1, half), preferred_element_type=F32)
    acc[0:rows, :] = total
    acc[rows:, :] = jnp.zeros((acc.shape[0] - rows, half), F32)


def extra_row(bias, area, half):
    row = jnp.concatenate([bias, area, jnp.zeros((1, half - 256), F32)], axis=1)
    return jnp.broadcast_to(row, (8, half))


def partner_half_kernel(where, held, b1, b2, b3, weight, area, early, weighted, other, acc):
    ws = [weigh(where, k, bracket, weight) for k, bracket in enumerate((b1, b2, b3), 1)]
    for k, w in enumerate(ws):
        weighted[k] = w
    late_half(1 - where[1], ws, held, early, acc)
    pieces_of(acc, extra_row(jnp.zeros((1, 128), F32), area[...], acc.shape[1]), other)


def own_half_kernel(where, held, weighted, early, early_bias, area, mine, acc):
    rows = early.shape[0]
    ws = [weighted[k] for k in range(GROUPS - 1)]
    late_half(where[1], ws, held, early, acc)
    bias = early_bias[...]
    for w in ws:
        bias = bias + bias_of(w)
    bias = jnp.concatenate([bias[0:1], jnp.zeros((1, 128 - rows), F32)], axis=1)
    pieces_of(acc, extra_row(bias, area[...], acc.shape[1]), mine)


def grad_hidden_kernel(where, early, late, half, piece, out, *, replicas):
    first = pl.program_id(0) == 0
    inverse = 1.0 / (piece[PIECE_ROWS : PIECE_ROWS + 1, 128:129] * (1.0 / replicas))
    chunk = out.shape[1]
    for m in range(out.shape[0]):
        lanes = slice(m * chunk, (m + 1) * chunk)
        product = lax.dot_general(
            jnp.where(first, early[0, :, lanes], late[0, :, lanes]), half[...], (((0,), (0,)), ((), ())), preferred_element_type=F32
        )
        out[m] = (product * inverse).astype(BF16)


def squares_of(pieces, inverse):
    half = pieces.shape[2]
    keep = lax.broadcasted_iota(jnp.int32, (8, half), 0) < PIECE_ROWS
    squares = jnp.zeros((8, half), F32)
    for r in range(PIECES):
        g = jnp.where(keep, pieces[r] * inverse, 0.0)
        squares = squares + g * g
    return squares


def in_order(pieces, inverse, out):
    for r in range(PIECES):
        low = PIECE_ROWS * r
        n = min(PIECE_ROWS, out.shape[0] - low)
        if n > 0:
            out[low : low + n, :] = pieces[r, 0:n, :] * inverse


def own_gradient_kernel(own, gradient, squares, *, replicas):
    inverse = 1.0 / (own[0, PIECE_ROWS : PIECE_ROWS + 1, 128:129] * (1.0 / replicas))
    squares[...] = squares_of(own, inverse)
    in_order(own, inverse, gradient)


def update_kernel(
    where, step, own, gradient, partner, squares, weight, intercept, new_weight, new_bias, other, *, replicas
):
    variables, features = weight.shape
    half = features // 2
    first = where[1] == 0
    inverse = 1.0 / (own[0, PIECE_ROWS : PIECE_ROWS + 1, 128:129] * (1.0 / replicas))
    a, b = (side[0, PIECE_ROWS : PIECE_ROWS + 1, 0:variables] for side in (own, partner))
    bias_grad = (jnp.where(first, a, b) + jnp.where(first, b, a)) * inverse
    in_order(partner, inverse, other)
    a, b = squares[...], squares_of(partner, inverse)
    both = jnp.where(first, a, b) + jnp.where(first, b, a)
    total = jnp.sum(jnp.sum(both, axis=0, keepdims=True), axis=1, keepdims=True)
    total = total + jnp.sum(bias_grad * bias_grad, axis=1, keepdims=True)
    count = variables * features + variables
    rms = jnp.sqrt(total / count + 1e-06)
    warm = (step[0] + 1).astype(F32) / WARMUP
    scale = warm * jnp.minimum(1.0, 1.0 / rms)
    a, b = gradient[...], other[...]
    new_weight[:, :half] = weight[:, :half] - scale * jnp.where(first, a, b)
    new_weight[:, half:] = weight[:, half:] - scale * jnp.where(first, b, a)
    new_bias[...] = intercept[...] - scale * bias_grad


def on_device(hidden, decoder_weight, decoder_intercept, analysis_truth, var_weight, lat_weight, area_bin, train_step):
    local, points, features = hidden.shape
    variables = decoder_weight.shape[0]
    rows = -(-variables // 8) * 8
    chunk = points // GROUPS
    members = local * GROUPS
    replicas = points * lax.axis_size("z") * lax.axis_size("x") * lax.axis_size("c") * GROUPS
    me, core = lax.axis_index("y"), lax.axis_index("c")
    where = jnp.stack([me, core]).astype(jnp.int32)

    def grant(mib):
        return pltpu.CompilerParams(vmem_limit_bytes=int(mib * MIB))

    intercept_row = decoder_intercept.reshape(1, variables)
    var_row = var_weight.reshape(1, variables)

    def turn(value, k):
        return value if k % GROUPS == 0 else lax.ppermute(value, "y", [(i, (i + k) % GROUPS) for i in range(GROUPS)])

    one_residual = jax.ShapeDtypeStruct((local, rows, chunk), F32)
    with jax.named_scope("forward_far"):
        far, half_weight = pl.pallas_call(
            far_kernel,
            out_shape=[one_residual, jax.ShapeDtypeStruct((rows, features), BF16)],
            in_specs=[SMEM, HBM, HBM],
            out_specs=[VMEM] * 2,
            scratch_shapes=[
                pltpu.VMEM((1, local, chunk, features), BF16),
                pltpu.VMEM((variables, features), F32),
                pltpu.SemaphoreType.DMA((1, local)),
                pltpu.SemaphoreType.DMA(()),
            ],
            compiler_params=grant(53.4),
            name="forward_far",
        )(where, hidden, decoder_weight)
        far = turn(far, 2)
    with jax.named_scope("forward_near"):
        after, before = pl.pallas_call(
            near_kernel,
            out_shape=[one_residual] * 2,
            in_specs=[SMEM, HBM, VMEM],
            out_specs=[VMEM] * 2,
            scratch_shapes=[
                pltpu.VMEM((2, local, chunk, features), BF16),
                pltpu.SemaphoreType.DMA((2, local)),
            ],
            compiler_params=grant(52),
            cost_estimate=pl.CostEstimate(
                flops=4 * rows * local * chunk * features, bytes_accessed=4 * local * chunk * features, transcendentals=0
            ),
            name="forward_near",
        )(where, hidden, half_weight)
        after, before = turn(after, 1), turn(before, 3)
    with jax.named_scope("forward_local"):
        here, area, point_weight, shift, held = pl.pallas_call(
            local_kernel,
            out_shape=[
                one_residual,
                jax.ShapeDtypeStruct((1, 128), F32),
                jax.ShapeDtypeStruct((rows, points), F32),
                jax.ShapeDtypeStruct((rows, chunk), F32),
                jax.ShapeDtypeStruct((GROUPS, local, chunk, features), BF16),
            ],
            in_specs=[SMEM, HBM] + [VMEM] * 6,
            out_specs=[VMEM] * 5,
            scratch_shapes=[pltpu.SemaphoreType.DMA((GROUPS, local))],
            compiler_params=grant(46),
            name="forward_local",
        )(where, hidden, half_weight, lat_weight.reshape(-1, 128), area_bin.reshape(1, points), intercept_row, analysis_truth, var_row)
    with jax.named_scope("early_pairs"):
        early = pl.pallas_call(
            lambda *refs: early_pairs_kernel(members, *refs),
            out_shape=jax.ShapeDtypeStruct((2 * local, rows, chunk), F32),
            in_specs=[VMEM] * 3,
            out_specs=VMEM,
            compiler_params=grant(4),
            name="early_pairs",
        )(here, far, shift)
    after, before, early, point_weight, held = lax.optimization_barrier((after, before, early, point_weight, held))
    with jax.named_scope("late_pairs"):
        brackets = pl.pallas_call(
            lambda *refs: late_pairs_kernel(members, *refs),
            out_shape=[jax.ShapeDtypeStruct((local, rows, chunk), BF16)] * GROUPS,
            in_specs=[VMEM] * (GROUPS + 2),
            out_specs=[VMEM] * GROUPS,
            scratch_shapes=[pltpu.VMEM((members, rows, chunk), F32)],
            compiler_params=grant(6),
            name="late_pairs",
        )(here, far, after, before, shift, early)
    with jax.named_scope("bracket_exchange"):
        returned = [brackets[0], turn(brackets[2], -1), turn(brackets[1], -2), turn(brackets[3], -3)]
    half = features // 2
    pieces = jax.ShapeDtypeStruct((PIECES, 8, half), F32)
    sums = [pltpu.VMEM((PIECES * 8, half), F32)]
    with jax.named_scope("early_backward"):
        weighted_early, early_sum, early_bias = pl.pallas_call(
            early_backward_kernel,
            out_shape=[
                jax.ShapeDtypeStruct((1, rows, local * chunk), BF16),
                jax.ShapeDtypeStruct((rows, features), F32),
                jax.ShapeDtypeStruct((8, rows), F32),
            ],
            in_specs=[SMEM] + [VMEM] * 3,
            out_specs=[VMEM] * 3,
            compiler_params=grant(10),
            name="early_backward",
        )(where, held, returned[0], point_weight)
    with jax.named_scope("backward_partner_half"):
        weighted_late, other = pl.pallas_call(
            partner_half_kernel,
            out_shape=[jax.ShapeDtypeStruct((GROUPS - 1, rows, local * chunk), BF16), pieces],
            in_specs=[SMEM] + [VMEM] * 7,
            out_specs=[VMEM] * 2,
            scratch_shapes=sums,
            compiler_params=grant(10),
            name="backward_partner_half",
        )(where, held, *returned[1:], point_weight, area, early_sum)
        swap = [(0, 1), (1, 0)]
        other = lax.ppermute(other, "c", swap)
    with jax.named_scope("backward_own_half"):
        mine = pl.pallas_call(
            own_half_kernel,
            out_shape=pieces,
            in_specs=[SMEM] + [VMEM] * 5,
            out_specs=VMEM,
            scratch_shapes=sums,
            compiler_params=grant(10),
            name="backward_own_half",
        )(where, held, weighted_late, early_sum, early_bias, area)
    with jax.named_scope("gradient_sum"):
        part = mine + other
        part = lax.all_to_all(part, ("x", "y"), 0, 0, tiled=True)
        depth = lax.axis_size("z")
        part = jnp.broadcast_to(jnp.sum(part, axis=0), (depth, 8, half))
        part = lax.all_to_all(part, "z", 0, 0, tiled=True)
        piece = jnp.sum(part, axis=0)
        own = lax.all_to_all(jnp.broadcast_to(piece, (PIECES, 8, half)), ("x", "y"), 0, 0, tiled=True)
    with jax.named_scope("grad_hidden"):
        grad_hidden = pl.pallas_call(
            lambda *refs: grad_hidden_kernel(*refs, replicas=replicas),
            out_shape=jax.ShapeDtypeStruct(hidden.shape, BF16),
            grid_spec=pltpu.PrefetchScalarGridSpec(
                num_scalar_prefetch=1,
                grid=(GROUPS,),
                in_specs=[
                    pl.BlockSpec((1, rows, local * chunk), lambda g, s: (0, 0, 0)),
                    pl.BlockSpec((1, rows, local * chunk), lambda g, s: (lax.max(g - 1, 0), 0, 0)),
                    pl.BlockSpec((rows, features), lambda g, s: (0, 0)),
                    pl.BlockSpec((8, half), lambda g, s: (0, 0)),
                ],
                out_specs=pl.BlockSpec((local, chunk, features), lambda g, s: (0, lax.rem(s[0] + g, GROUPS), 0)),
            ),
            compiler_params=grant(12),
            cost_estimate=pl.CostEstimate(
                flops=2 * rows * local * points * features, bytes_accessed=2 * hidden.size, transcendentals=0
            ),
            name="grad_hidden",
        )(where, weighted_early, weighted_late, half_weight, piece)
        own, grad_hidden = lax.optimization_barrier((own, grad_hidden))
    with jax.named_scope("last_swap"):
        partner = lax.ppermute(own, "c", swap)
        gradient, squares = pl.pallas_call(
            lambda *refs: own_gradient_kernel(*refs, replicas=replicas),
            out_shape=[jax.ShapeDtypeStruct((variables, half), F32), jax.ShapeDtypeStruct((8, half), F32)],
            in_specs=[VMEM],
            out_specs=[VMEM] * 2,
            compiler_params=grant(4),
            name="own_gradient",
        )(own)
    with jax.named_scope("update"):
        new_weight, new_bias = pl.pallas_call(
            lambda *refs: update_kernel(*refs, replicas=replicas),
            out_shape=[
                jax.ShapeDtypeStruct((variables, features), F32),
                jax.ShapeDtypeStruct((1, variables), F32),
            ],
            in_specs=[SMEM, SMEM] + [VMEM] * 6,
            out_specs=[VMEM] * 2,
            scratch_shapes=[pltpu.VMEM((variables, half), F32)],
            compiler_params=grant(6),
            name="update",
        )(where, train_step, own, gradient, partner, squares, decoder_weight, intercept_row)
    return grad_hidden, new_weight, new_bias.reshape(variables)


def solution(mesh):
    fine = Mesh(mesh.devices.reshape(GROUPS, 8, 4, 2), ("y", "z", "x", "c"))
    space = ("z", "x", "c")
    return jax.shard_map(
        on_device,
        mesh=fine,
        in_specs=(P("y", space, None), P(), P(), P(None, space), P(), P(), P(space), P()),
        out_specs=(P("y", space, None), P(), P()),
        check_vma=False,
    )
```

```python
import jax
import jax.numpy as jnp
from jax import lax
from jax.experimental import pallas as pl
from jax.experimental.pallas import tpu as pltpu
from jax.sharding import Mesh, PartitionSpec as P

WARMUP = 1000
smooth_sq = 0.0025
fair_alpha = 0.95

GROUPS = 4
PIECES = 16
PIECE_ROWS = 7
MIB = 1024 * 1024
VMEM = pl.BlockSpec(memory_space=pltpu.VMEM)
SMEM = pl.BlockSpec(memory_space=pltpu.SMEM)
HBM = pl.BlockSpec(memory_space=pltpu.HBM)
F32 = jnp.float32
BF16 = jnp.bfloat16


def soft(d):
    return d * lax.rsqrt(d * d + smooth_sq)


def as_column(row, rows):
    n = row.shape[1]
    pick = lax.broadcasted_iota(jnp.int32, (rows, n), 0) == lax.broadcasted_iota(jnp.int32, (rows, n), 1)
    return jnp.sum(jnp.where(pick, jnp.broadcast_to(row, (rows, n)), 0.0), axis=1, keepdims=True)


def padded(value, rows):
    return jnp.concatenate([value, jnp.zeros((rows - value.shape[0], value.shape[1]), value.dtype)], axis=0)


def chunk_at(where, k, chunk):
    return pl.ds(pl.multiple_of(lax.rem(where[0] + k, GROUPS) * chunk, chunk), chunk)


def fetch_chunks(where, hidden, held, sem, ks):
    local, chunk = held.shape[1:3]
    copies = []
    for slot, k in enumerate(ks):
        points = chunk_at(where, k, chunk)
        copies.append(
            [pltpu.make_async_copy(hidden.at[m, points, :], held.at[slot, m], sem.at[slot, m]) for m in range(local)]
        )
        for copy in copies[slot]:
            copy.start()
    return copies


def decode_chunk(copies, held, half, out):
    for copy in copies:
        copy.wait()
    values = lax.dot_general(
        half[...], held[...].reshape(-1, held.shape[2]), (((1,), (1,)), ((), ())), preferred_element_type=F32
    )
    chunk = out.shape[2]
    for m in range(out.shape[0]):
        out[m] = values[:, m * chunk : (m + 1) * chunk]


def far_kernel(where, hidden, weight, out, half, held, w, sem, weight_sem):
    fetch = pltpu.make_async_copy(weight, w, weight_sem)
    fetch.start()
    (copies,) = fetch_chunks(where, hidden, held, sem, (2,))
    fetch.wait()
    half[...] = padded(w[...], half.shape[0]).astype(BF16)
    decode_chunk(copies, held.at[0], half, out)


def near_kernel(where, hidden, half, after, before, held, sem):
    copies = fetch_chunks(where, hidden, held, sem, (1, 3))
    for slot, out in enumerate((after, before)):
        decode_chunk(copies[slot], held.at[slot], half, out)


def add_pair(total, i, j, s):
    total[i] = s if total[i] is None else total[i] + s
    total[j] = -s if total[j] is None else total[j] - s


def pair_normalizer(members):
    eps = (1.0 - fair_alpha) / members
    return (1.0 - eps) / (members * (members - 1))


def row_tiles(rows, body):
    def tile(t, carry):
        body(pl.ds(pl.multiple_of(t * 8, 8), 8))
        return carry

    lax.fori_loop(0, rows // 8, tile, 0)


def early_pairs_kernel(members, here, far, shift, out):
    local = here.shape[0]
    count = 2 * local
    normalizer = pair_normalizer(members)

    def body(at):
        r = [ref[j, at, :] + shift[at, :] for ref in (here, far) for j in range(local)]
        total = [None] * count
        for i in range(count):
            for j in range(i + 1, count):
                add_pair(total, i, j, soft(r[i] - r[j]))
        for j in range(count):
            out[j, at, :] = soft(r[j]) * (1.0 / members) - normalizer * total[j]

    row_tiles(here.shape[1], body)


def far_pairs_kernel(members, far, after, before, shift, early, bracket, near, scratch):
    local = far.shape[0]
    normalizer = pair_normalizer(members)

    def body(at):
        r = [ref[j, at, :] + shift[at, :] for ref in (far, after, before) for j in range(local)]
        total = [None] * (3 * local)
        for i in range(local):
            for j in range(local, 3 * local):
                add_pair(total, i, j, soft(r[i] - r[j]))
        for j in range(local):
            scratch[j, at, :] = early[local + j, at, :] - normalizer * total[j]
        for j in range(2 * local):
            near[j, at, :] = total[local + j]

    row_tiles(far.shape[1], body)
    for j in range(local):
        bracket[j] = scratch[j].astype(BF16)


def near_pairs_kernel(members, here, after, before, shift, early, near, *rest):
    outs, scratch = rest[:3], rest[3]
    local = here.shape[0]
    normalizer = pair_normalizer(members)

    def body(at):
        r = [ref[j, at, :] + shift[at, :] for ref in (here, after, before) for j in range(local)]
        total = [None] * local + [near[j, at, :] for j in range(2 * local)]
        for i in range(3 * local):
            for j in range(max(i + 1, local), 3 * local):
                add_pair(total, i, j, soft(r[i] - r[j]))
        for j in range(3 * local):
            base = early[j, at, :] if j < local else soft(r[j]) * (1.0 / members)
            scratch[j, at, :] = base - normalizer * total[j]

    row_tiles(here.shape[1], body)
    for j in range(3 * local):
        outs[j // local][j % local] = scratch[j].astype(BF16)


def local_kernel(where, hidden, half, lat, area_bin, intercept, truth, var, out, area, weight, shift, held, sem):
    copies = fetch_chunks(where, hidden, held, sem, range(GROUPS))
    rows, chunk = shift.shape
    cells, width = lat.shape
    points = area_bin.shape[1]
    bins = jnp.broadcast_to(area_bin[...], (width, points))
    level = lax.broadcasted_iota(jnp.int32, (width, points), 0)
    total = jnp.zeros((width, points), F32)
    for q in range(cells):
        column = as_column(lat[q : q + 1, :], width)
        total = total + jnp.where(bins == level + q * width, column, 0.0)
    by_point = jnp.sum(total, axis=0, keepdims=True)
    area[...] = jnp.broadcast_to(jnp.sum(by_point, axis=1, keepdims=True), area.shape)
    weight[...] = by_point * as_column(var[...], rows)
    here = chunk_at(where, 0, chunk)
    shift[...] = as_column(intercept[...], rows) - padded(truth[:, here], rows)
    decode_chunk(copies[0], held.at[0], half, out)
    for chunk_copies in copies[1:]:
        for copy in chunk_copies:
            copy.wait()


def pieces_of(acc, extra, out):
    last = lax.broadcasted_iota(jnp.int32, out.shape[1:], 0) == PIECE_ROWS
    for r in range(PIECES):
        out[r] = jnp.where(last, extra, acc[PIECE_ROWS * r : PIECE_ROWS * r + 8, :])


def weigh(where, k, bracket, weight):
    local, _, chunk = bracket.shape
    scale = weight[:, chunk_at(where, k, chunk)]
    return jnp.concatenate([(scale * bracket[m].astype(F32)).astype(BF16) for m in range(local)], axis=1)


def bias_of(w):
    ones = jnp.ones((8, w.shape[1]), BF16)
    return lax.dot_general(ones, w, (((1,), (1,)), ((), ())), preferred_element_type=F32)


def early_backward_kernel(where, held, b0, b2, weight, weighted, total, bias):
    features = held.shape[3]
    w0 = weigh(where, 0, b0, weight)
    w2 = weigh(where, 2, b2, weight)
    weighted[0], weighted[1] = w0, w2
    bias[...] = bias_of(w0) + bias_of(w2)
    total[...] = jnp.dot(
        w0, held[0].reshape(-1, features), preferred_element_type=F32
    ) + jnp.dot(w2, held[2].reshape(-1, features), preferred_element_type=F32)


def late_half(side, w1, w3, held, early, acc):
    rows = w1.shape[0]
    half = acc.shape[1]
    lanes = pl.ds(pl.multiple_of(side * half, half), half)
    acc[0:rows, :] = (
        early[:, lanes]
        + jnp.dot(w1, held[1, :, :, lanes].reshape(-1, half), preferred_element_type=F32)
        + jnp.dot(w3, held[3, :, :, lanes].reshape(-1, half), preferred_element_type=F32)
    )
    acc[rows:, :] = jnp.zeros((acc.shape[0] - rows, half), F32)


def extra_row(bias, area, half):
    row = jnp.concatenate([bias, area, jnp.zeros((1, half - 256), F32)], axis=1)
    return jnp.broadcast_to(row, (8, half))


def partner_half_kernel(where, held, b1, b3, weight, area, early, weighted, other, acc):
    w1 = weigh(where, 1, b1, weight)
    w3 = weigh(where, 3, b3, weight)
    weighted[0], weighted[1] = w1, w3
    late_half(1 - where[1], w1, w3, held, early, acc)
    pieces_of(acc, extra_row(jnp.zeros((1, 128), F32), area[...], acc.shape[1]), other)


def own_half_kernel(where, held, weighted, early, early_bias, area, mine, acc):
    rows = early.shape[0]
    w1, w3 = weighted[0], weighted[1]
    late_half(where[1], w1, w3, held, early, acc)
    bias = early_bias[...] + bias_of(w1) + bias_of(w3)
    bias = jnp.concatenate([bias[0:1], jnp.zeros((1, 128 - rows), F32)], axis=1)
    pieces_of(acc, extra_row(bias, area[...], acc.shape[1]), mine)


def grad_hidden_kernel(where, early, late, half, piece, out, *, replicas):
    first = lax.rem(pl.program_id(0), 2) == 0
    inverse = 1.0 / (piece[PIECE_ROWS : PIECE_ROWS + 1, 128:129] * (1.0 / replicas))
    chunk = out.shape[1]
    for m in range(out.shape[0]):
        lanes = slice(m * chunk, (m + 1) * chunk)
        product = lax.dot_general(
            jnp.where(first, early[0, :, lanes], late[0, :, lanes]), half[...], (((0,), (0,)), ((), ())), preferred_element_type=F32
        )
        out[m] = (product * inverse).astype(BF16)


def squares_of(pieces, inverse):
    half = pieces.shape[2]
    keep = lax.broadcasted_iota(jnp.int32, (8, half), 0) < PIECE_ROWS
    squares = jnp.zeros((8, half), F32)
    for r in range(PIECES):
        g = jnp.where(keep, pieces[r] * inverse, 0.0)
        squares = squares + g * g
    return squares


def in_order(pieces, inverse, out):
    for r in range(PIECES):
        low = PIECE_ROWS * r
        n = min(PIECE_ROWS, out.shape[0] - low)
        if n > 0:
            out[low : low + n, :] = pieces[r, 0:n, :] * inverse


def own_gradient_kernel(own, gradient, squares, *, replicas):
    inverse = 1.0 / (own[0, PIECE_ROWS : PIECE_ROWS + 1, 128:129] * (1.0 / replicas))
    squares[...] = squares_of(own, inverse)
    in_order(own, inverse, gradient)


def update_kernel(
    where, step, own, gradient, partner, squares, weight, intercept, new_weight, new_bias, other, *, replicas
):
    variables, features = weight.shape
    half = features // 2
    first = where[1] == 0
    inverse = 1.0 / (own[0, PIECE_ROWS : PIECE_ROWS + 1, 128:129] * (1.0 / replicas))
    a, b = (side[0, PIECE_ROWS : PIECE_ROWS + 1, 0:variables] for side in (own, partner))
    bias_grad = (jnp.where(first, a, b) + jnp.where(first, b, a)) * inverse
    in_order(partner, inverse, other)
    a, b = squares[...], squares_of(partner, inverse)
    both = jnp.where(first, a, b) + jnp.where(first, b, a)
    total = jnp.sum(jnp.sum(both, axis=0, keepdims=True), axis=1, keepdims=True)
    total = total + jnp.sum(bias_grad * bias_grad, axis=1, keepdims=True)
    count = variables * features + variables
    rms = jnp.sqrt(total / count + 1e-06)
    warm = (step[0] + 1).astype(F32) / WARMUP
    scale = warm * jnp.minimum(1.0, 1.0 / rms)
    a, b = gradient[...], other[...]
    new_weight[:, :half] = weight[:, :half] - scale * jnp.where(first, a, b)
    new_weight[:, half:] = weight[:, half:] - scale * jnp.where(first, b, a)
    new_bias[...] = intercept[...] - scale * bias_grad


def on_device(hidden, decoder_weight, decoder_intercept, analysis_truth, var_weight, lat_weight, area_bin, train_step):
    local, points, features = hidden.shape
    variables = decoder_weight.shape[0]
    rows = -(-variables // 8) * 8
    chunk = points // GROUPS
    members = local * GROUPS
    replicas = points * lax.axis_size("z") * lax.axis_size("x") * lax.axis_size("c") * GROUPS
    me, core = lax.axis_index("y"), lax.axis_index("c")
    where = jnp.stack([me, core]).astype(jnp.int32)

    def grant(mib):
        return pltpu.CompilerParams(vmem_limit_bytes=int(mib * MIB))

    intercept_row = decoder_intercept.reshape(1, variables)
    var_row = var_weight.reshape(1, variables)

    def turn(value, k):
        return value if k % GROUPS == 0 else lax.ppermute(value, "y", [(i, (i + k) % GROUPS) for i in range(GROUPS)])

    one_residual = jax.ShapeDtypeStruct((local, rows, chunk), F32)
    with jax.named_scope("forward_far"):
        far, half_weight = pl.pallas_call(
            far_kernel,
            out_shape=[one_residual, jax.ShapeDtypeStruct((rows, features), BF16)],
            in_specs=[SMEM, HBM, HBM],
            out_specs=[VMEM] * 2,
            scratch_shapes=[
                pltpu.VMEM((1, local, chunk, features), BF16),
                pltpu.VMEM((variables, features), F32),
                pltpu.SemaphoreType.DMA((1, local)),
                pltpu.SemaphoreType.DMA(()),
            ],
            compiler_params=grant(53.4),
            name="forward_far",
        )(where, hidden, decoder_weight)
        far = turn(far, 2)
    with jax.named_scope("forward_near"):
        after, before = pl.pallas_call(
            near_kernel,
            out_shape=[one_residual] * 2,
            in_specs=[SMEM, HBM, VMEM],
            out_specs=[VMEM] * 2,
            scratch_shapes=[
                pltpu.VMEM((2, local, chunk, features), BF16),
                pltpu.SemaphoreType.DMA((2, local)),
            ],
            compiler_params=grant(52),
            cost_estimate=pl.CostEstimate(
                flops=4 * rows * local * chunk * features, bytes_accessed=4 * local * chunk * features, transcendentals=0
            ),
            name="forward_near",
        )(where, hidden, half_weight)
        after, before = turn(after, 1), turn(before, 3)
    with jax.named_scope("forward_local"):
        here, area, point_weight, shift, held = pl.pallas_call(
            local_kernel,
            out_shape=[
                one_residual,
                jax.ShapeDtypeStruct((1, 128), F32),
                jax.ShapeDtypeStruct((rows, points), F32),
                jax.ShapeDtypeStruct((rows, chunk), F32),
                jax.ShapeDtypeStruct((GROUPS, local, chunk, features), BF16),
            ],
            in_specs=[SMEM, HBM] + [VMEM] * 6,
            out_specs=[VMEM] * 5,
            scratch_shapes=[pltpu.SemaphoreType.DMA((GROUPS, local))],
            compiler_params=grant(46),
            name="forward_local",
        )(where, hidden, half_weight, lat_weight.reshape(-1, 128), area_bin.reshape(1, points), intercept_row, analysis_truth, var_row)
    with jax.named_scope("early_pairs"):
        early = pl.pallas_call(
            lambda *refs: early_pairs_kernel(members, *refs),
            out_shape=jax.ShapeDtypeStruct((2 * local, rows, chunk), F32),
            in_specs=[VMEM] * 3,
            out_specs=VMEM,
            compiler_params=grant(4),
            name="early_pairs",
        )(here, far, shift)
    after, before, early, point_weight, held = lax.optimization_barrier((after, before, early, point_weight, held))
    one_bracket = jax.ShapeDtypeStruct((local, rows, chunk), BF16)
    with jax.named_scope("far_pairs"):
        far_bracket, near_sums = pl.pallas_call(
            lambda *refs: far_pairs_kernel(members, *refs),
            out_shape=[one_bracket, jax.ShapeDtypeStruct((2 * local, rows, chunk), F32)],
            in_specs=[VMEM] * 5,
            out_specs=[VMEM] * 2,
            scratch_shapes=[pltpu.VMEM((local, rows, chunk), F32)],
            compiler_params=grant(6),
            name="far_pairs",
        )(far, after, before, shift, early)
        far_bracket = turn(far_bracket, -2)
    with jax.named_scope("near_pairs"):
        here_bracket, after_bracket, before_bracket = pl.pallas_call(
            lambda *refs: near_pairs_kernel(members, *refs),
            out_shape=[one_bracket] * 3,
            in_specs=[VMEM] * 6,
            out_specs=[VMEM] * 3,
            scratch_shapes=[pltpu.VMEM((3 * local, rows, chunk), F32)],
            compiler_params=grant(6),
            cost_estimate=pl.CostEstimate(flops=600 * rows * chunk, bytes_accessed=64 * rows * chunk, transcendentals=60 * rows * chunk),
            name="near_pairs",
        )(here, after, before, shift, early, near_sums)
        returned = [here_bracket, turn(after_bracket, -1), far_bracket, turn(before_bracket, -3)]
    half = features // 2
    pieces = jax.ShapeDtypeStruct((PIECES, 8, half), F32)
    two_weighted = jax.ShapeDtypeStruct((GROUPS // 2, rows, local * chunk), BF16)
    sums = [pltpu.VMEM((PIECES * 8, half), F32)]
    with jax.named_scope("early_backward"):
        weighted_early, early_sum, early_bias = pl.pallas_call(
            early_backward_kernel,
            out_shape=[
                two_weighted,
                jax.ShapeDtypeStruct((rows, features), F32),
                jax.ShapeDtypeStruct((8, rows), F32),
            ],
            in_specs=[SMEM] + [VMEM] * 4,
            out_specs=[VMEM] * 3,
            compiler_params=grant(10),
            name="early_backward",
        )(where, held, returned[0], returned[2], point_weight)
    with jax.named_scope("backward_partner_half"):
        weighted_late, other = pl.pallas_call(
            partner_half_kernel,
            out_shape=[two_weighted, pieces],
            in_specs=[SMEM] + [VMEM] * 6,
            out_specs=[VMEM] * 2,
            scratch_shapes=sums,
            compiler_params=grant(10),
            name="backward_partner_half",
        )(where, held, returned[1], returned[3], point_weight, area, early_sum)
        swap = [(0, 1), (1, 0)]
        other = lax.ppermute(other, "c", swap)
    with jax.named_scope("backward_own_half"):
        mine = pl.pallas_call(
            own_half_kernel,
            out_shape=pieces,
            in_specs=[SMEM] + [VMEM] * 5,
            out_specs=VMEM,
            scratch_shapes=sums,
            compiler_params=grant(10),
            name="backward_own_half",
        )(where, held, weighted_late, early_sum, early_bias, area)
    with jax.named_scope("gradient_sum"):
        part = mine + other
        part = lax.all_to_all(part, ("x", "y"), 0, 0, tiled=True)
        depth = lax.axis_size("z")
        part = jnp.broadcast_to(jnp.sum(part, axis=0), (depth, 8, half))
        part = lax.all_to_all(part, "z", 0, 0, tiled=True)
        piece = jnp.sum(part, axis=0)
        own = lax.all_to_all(jnp.broadcast_to(piece, (PIECES, 8, half)), ("x", "y"), 0, 0, tiled=True)
    with jax.named_scope("grad_hidden"):
        grad_hidden = pl.pallas_call(
            lambda *refs: grad_hidden_kernel(*refs, replicas=replicas),
            out_shape=jax.ShapeDtypeStruct(hidden.shape, BF16),
            grid_spec=pltpu.PrefetchScalarGridSpec(
                num_scalar_prefetch=1,
                grid=(GROUPS,),
                in_specs=[
                    pl.BlockSpec((1, rows, local * chunk), lambda g, s: (lax.div(g, 2), 0, 0)),
                    pl.BlockSpec((1, rows, local * chunk), lambda g, s: (lax.div(g, 2), 0, 0)),
                    pl.BlockSpec((rows, features), lambda g, s: (0, 0)),
                    pl.BlockSpec((8, half), lambda g, s: (0, 0)),
                ],
                out_specs=pl.BlockSpec((local, chunk, features), lambda g, s: (0, lax.rem(s[0] + g, GROUPS), 0)),
            ),
            compiler_params=grant(12),
            cost_estimate=pl.CostEstimate(
                flops=2 * rows * local * points * features, bytes_accessed=2 * hidden.size, transcendentals=0
            ),
            name="grad_hidden",
        )(where, weighted_early, weighted_late, half_weight, piece)
        own, grad_hidden = lax.optimization_barrier((own, grad_hidden))
    with jax.named_scope("last_swap"):
        partner = lax.ppermute(own, "c", swap)
        gradient, squares = pl.pallas_call(
            lambda *refs: own_gradient_kernel(*refs, replicas=replicas),
            out_shape=[jax.ShapeDtypeStruct((variables, half), F32), jax.ShapeDtypeStruct((8, half), F32)],
            in_specs=[VMEM],
            out_specs=[VMEM] * 2,
            compiler_params=grant(4),
            name="own_gradient",
        )(own)
    with jax.named_scope("update"):
        new_weight, new_bias = pl.pallas_call(
            lambda *refs: update_kernel(*refs, replicas=replicas),
            out_shape=[
                jax.ShapeDtypeStruct((variables, features), F32),
                jax.ShapeDtypeStruct((1, variables), F32),
            ],
            in_specs=[SMEM, SMEM] + [VMEM] * 6,
            out_specs=[VMEM] * 2,
            scratch_shapes=[pltpu.VMEM((variables, half), F32)],
            compiler_params=grant(6),
            name="update",
        )(where, train_step, own, gradient, partner, squares, decoder_weight, intercept_row)
    return grad_hidden, new_weight, new_bias.reshape(variables)


def solution(mesh):
    fine = Mesh(mesh.devices.reshape(GROUPS, 8, 4, 2), ("y", "z", "x", "c"))
    space = ("z", "x", "c")
    return jax.shard_map(
        on_device,
        mesh=fine,
        in_specs=(P("y", space, None), P(), P(), P(None, space), P(), P(), P(space), P()),
        out_specs=(P("y", space, None), P(), P()),
        check_vma=False,
    )
```

```python
import jax
import jax.numpy as jnp
from jax import lax
from jax.experimental import pallas as pl
from jax.experimental.pallas import tpu as pltpu
from jax.sharding import Mesh, PartitionSpec as P

WARMUP = 1000
smooth_sq = 0.0025
fair_alpha = 0.95

GROUPS = 4
PIECES = 16
PIECE_ROWS = 7
MIB = 1024 * 1024
VMEM = pl.BlockSpec(memory_space=pltpu.VMEM)
SMEM = pl.BlockSpec(memory_space=pltpu.SMEM)
HBM = pl.BlockSpec(memory_space=pltpu.HBM)
F32 = jnp.float32
BF16 = jnp.bfloat16


def soft(d):
    return d * lax.rsqrt(d * d + smooth_sq)


def as_column(row, rows):
    n = row.shape[1]
    pick = lax.broadcasted_iota(jnp.int32, (rows, n), 0) == lax.broadcasted_iota(jnp.int32, (rows, n), 1)
    return jnp.sum(jnp.where(pick, jnp.broadcast_to(row, (rows, n)), 0.0), axis=1, keepdims=True)


def padded(value, rows):
    return jnp.concatenate([value, jnp.zeros((rows - value.shape[0], value.shape[1]), value.dtype)], axis=0)


def chunk_at(where, k, chunk):
    return pl.ds(pl.multiple_of(lax.rem(where[0] + k, GROUPS) * chunk, chunk), chunk)


def fetch_chunks(where, hidden, held, sem, ks):
    local, chunk = held.shape[1:3]
    copies = []
    for slot, k in enumerate(ks):
        points = chunk_at(where, k, chunk)
        copies.append(
            [pltpu.make_async_copy(hidden.at[m, points, :], held.at[slot, m], sem.at[slot, m]) for m in range(local)]
        )
        for copy in copies[slot]:
            copy.start()
    return copies


def decode_chunk(copies, held, half, out):
    for copy in copies:
        copy.wait()
    for m in range(out.shape[0]):
        out[m] = lax.dot_general(half[...], held[m], (((1,), (1,)), ((), ())), preferred_element_type=F32)


def far_kernel(where, hidden, weight, out, half, held, w, sem, weight_sem):
    fetch = pltpu.make_async_copy(weight, w, weight_sem)
    fetch.start()
    (copies,) = fetch_chunks(where, hidden, held, sem, (2,))
    fetch.wait()
    half[...] = padded(w[...], half.shape[0]).astype(BF16)
    decode_chunk(copies, held.at[0], half, out)


def near_kernel(where, hidden, half, after, before, held, sem):
    copies = fetch_chunks(where, hidden, held, sem, (1, 3))
    for slot, out in enumerate((after, before)):
        decode_chunk(copies[slot], held.at[slot], half, out)


def add_pair(total, i, j, s):
    total[i] = s if total[i] is None else total[i] + s
    total[j] = -s if total[j] is None else total[j] - s


def pair_normalizer(members):
    eps = (1.0 - fair_alpha) / members
    return (1.0 - eps) / (members * (members - 1))


def row_tiles(rows, body):
    def tile(t, carry):
        body(pl.ds(pl.multiple_of(t * 8, 8), 8))
        return carry

    lax.fori_loop(0, rows // 8, tile, 0)


def early_pairs_kernel(members, here, far, shift, out):
    local = here.shape[0]
    count = 2 * local
    normalizer = pair_normalizer(members)

    def body(at):
        r = [ref[j, at, :] + shift[at, :] for ref in (here, far) for j in range(local)]
        total = [None] * count
        for i in range(count):
            for j in range(i + 1, count):
                add_pair(total, i, j, soft(r[i] - r[j]))
        for j in range(count):
            out[j, at, :] = soft(r[j]) * (1.0 / members) - normalizer * total[j]

    row_tiles(here.shape[1], body)


def far_pairs_kernel(members, far, after, before, shift, early, bracket, near, scratch):
    local = far.shape[0]
    normalizer = pair_normalizer(members)

    def body(at):
        r = [ref[j, at, :] + shift[at, :] for ref in (far, after, before) for j in range(local)]
        total = [None] * (3 * local)
        for i in range(local):
            for j in range(local, 3 * local):
                add_pair(total, i, j, soft(r[i] - r[j]))
        for j in range(local):
            scratch[j, at, :] = early[local + j, at, :] - normalizer * total[j]
        for j in range(2 * local):
            near[j, at, :] = total[local + j]

    row_tiles(far.shape[1], body)
    for j in range(local):
        bracket[j] = scratch[j].astype(BF16)


def near_pairs_kernel(members, here, after, before, shift, early, near, *rest):
    outs, scratch = rest[:3], rest[3]
    local = here.shape[0]
    normalizer = pair_normalizer(members)

    def body(at):
        r = [ref[j, at, :] + shift[at, :] for ref in (here, after, before) for j in range(local)]
        total = [None] * local + [near[j, at, :] for j in range(2 * local)]
        for i in range(3 * local):
            for j in range(max(i + 1, local), 3 * local):
                add_pair(total, i, j, soft(r[i] - r[j]))
        for j in range(3 * local):
            base = early[j, at, :] if j < local else soft(r[j]) * (1.0 / members)
            scratch[j, at, :] = base - normalizer * total[j]

    row_tiles(here.shape[1], body)
    for j in range(3 * local):
        outs[j // local][j % local] = scratch[j].astype(BF16)


def local_kernel(where, hidden, half, lat, area_bin, intercept, truth, var, out, area, weight, shift, held, sem):
    copies = fetch_chunks(where, hidden, held, sem, range(GROUPS))
    rows, chunk = shift.shape
    cells, width = lat.shape
    points = area_bin.shape[1]
    bins = jnp.broadcast_to(area_bin[...], (width, points))
    level = lax.broadcasted_iota(jnp.int32, (width, points), 0)
    total = jnp.zeros((width, points), F32)
    for q in range(cells):
        column = as_column(lat[q : q + 1, :], width)
        total = total + jnp.where(bins == level + q * width, column, 0.0)
    by_point = jnp.sum(total, axis=0, keepdims=True)
    area[...] = jnp.broadcast_to(jnp.sum(by_point, axis=1, keepdims=True), area.shape)
    weight[...] = by_point * as_column(var[...], rows)
    here = chunk_at(where, 0, chunk)
    shift[...] = as_column(intercept[...], rows) - padded(truth[:, here], rows)
    decode_chunk(copies[0], held.at[0], half, out)
    for chunk_copies in copies[1:]:
        for copy in chunk_copies:
            copy.wait()


def pieces_of(acc, extra, out):
    last = lax.broadcasted_iota(jnp.int32, out.shape[1:], 0) == PIECE_ROWS
    for r in range(PIECES):
        out[r] = jnp.where(last, extra, acc[PIECE_ROWS * r : PIECE_ROWS * r + 8, :])


def weigh(where, k, bracket, weight):
    local, _, chunk = bracket.shape
    scale = weight[:, chunk_at(where, k, chunk)]
    return jnp.concatenate([(scale * bracket[m].astype(F32)).astype(BF16) for m in range(local)], axis=1)


def bias_of(w):
    ones = jnp.ones((8, w.shape[1]), BF16)
    return lax.dot_general(ones, w, (((1,), (1,)), ((), ())), preferred_element_type=F32)


def early_backward_kernel(where, held, b0, b2, weight, weighted, total, bias):
    features = held.shape[3]
    w0 = weigh(where, 0, b0, weight)
    w2 = weigh(where, 2, b2, weight)
    weighted[0], weighted[1] = w0, w2
    bias[...] = bias_of(w0) + bias_of(w2)
    total[...] = jnp.dot(
        w0, held[0].reshape(-1, features), preferred_element_type=F32
    ) + jnp.dot(w2, held[2].reshape(-1, features), preferred_element_type=F32)


def late_half(side, w1, w3, held, early, acc):
    rows = w1.shape[0]
    half = acc.shape[1]
    lanes = pl.ds(pl.multiple_of(side * half, half), half)
    acc[0:rows, :] = (
        early[:, lanes]
        + jnp.dot(w1, held[1, :, :, lanes].reshape(-1, half), preferred_element_type=F32)
        + jnp.dot(w3, held[3, :, :, lanes].reshape(-1, half), preferred_element_type=F32)
    )
    acc[rows:, :] = jnp.zeros((acc.shape[0] - rows, half), F32)


def extra_row(bias, area, half):
    row = jnp.concatenate([bias, area, jnp.zeros((1, half - 256), F32)], axis=1)
    return jnp.broadcast_to(row, (8, half))


def partner_half_kernel(where, held, b1, b3, weight, area, early, weighted, other, acc):
    w1 = weigh(where, 1, b1, weight)
    w3 = weigh(where, 3, b3, weight)
    weighted[0], weighted[1] = w1, w3
    late_half(1 - where[1], w1, w3, held, early, acc)
    pieces_of(acc, extra_row(jnp.zeros((1, 128), F32), area[...], acc.shape[1]), other)


def own_half_kernel(where, held, weighted, early, early_bias, area, mine, acc):
    rows = early.shape[0]
    w1, w3 = weighted[0], weighted[1]
    late_half(where[1], w1, w3, held, early, acc)
    bias = early_bias[...] + bias_of(w1) + bias_of(w3)
    bias = jnp.concatenate([bias[0:1], jnp.zeros((1, 128 - rows), F32)], axis=1)
    pieces_of(acc, extra_row(bias, area[...], acc.shape[1]), mine)


def grad_hidden_kernel(where, early, late, half, piece, out, *, replicas):
    first = lax.rem(pl.program_id(0), 2) == 0
    inverse = 1.0 / (piece[PIECE_ROWS : PIECE_ROWS + 1, 128:129] * (1.0 / replicas))
    chunk = out.shape[1]
    for m in range(out.shape[0]):
        lanes = slice(m * chunk, (m + 1) * chunk)
        product = lax.dot_general(
            jnp.where(first, early[0, :, lanes], late[0, :, lanes]), half[...], (((0,), (0,)), ((), ())), preferred_element_type=F32
        )
        out[m] = (product * inverse).astype(BF16)


def squares_of(pieces, inverse):
    half = pieces.shape[2]
    keep = lax.broadcasted_iota(jnp.int32, (8, half), 0) < PIECE_ROWS
    squares = jnp.zeros((8, half), F32)
    for r in range(PIECES):
        g = jnp.where(keep, pieces[r] * inverse, 0.0)
        squares = squares + g * g
    return squares


def in_order(pieces, inverse, out):
    for r in range(PIECES):
        low = PIECE_ROWS * r
        n = min(PIECE_ROWS, out.shape[0] - low)
        if n > 0:
            out[low : low + n, :] = pieces[r, 0:n, :] * inverse


def own_gradient_kernel(own, gradient, squares, *, replicas):
    inverse = 1.0 / (own[0, PIECE_ROWS : PIECE_ROWS + 1, 128:129] * (1.0 / replicas))
    squares[...] = squares_of(own, inverse)
    in_order(own, inverse, gradient)


def update_kernel(
    where, step, own, gradient, partner, squares, weight, intercept, new_weight, new_bias, other, *, replicas
):
    variables, features = weight.shape
    half = features // 2
    first = where[1] == 0
    inverse = 1.0 / (own[0, PIECE_ROWS : PIECE_ROWS + 1, 128:129] * (1.0 / replicas))
    a, b = (side[0, PIECE_ROWS : PIECE_ROWS + 1, 0:variables] for side in (own, partner))
    bias_grad = (jnp.where(first, a, b) + jnp.where(first, b, a)) * inverse
    in_order(partner, inverse, other)
    a, b = squares[...], squares_of(partner, inverse)
    both = jnp.where(first, a, b) + jnp.where(first, b, a)
    total = jnp.sum(jnp.sum(both, axis=0, keepdims=True), axis=1, keepdims=True)
    total = total + jnp.sum(bias_grad * bias_grad, axis=1, keepdims=True)
    count = variables * features + variables
    rms = jnp.sqrt(total / count + 1e-06)
    warm = (step[0] + 1).astype(F32) / WARMUP
    scale = warm * jnp.minimum(1.0, 1.0 / rms)
    a, b = gradient[...], other[...]
    new_weight[:, :half] = weight[:, :half] - scale * jnp.where(first, a, b)
    new_weight[:, half:] = weight[:, half:] - scale * jnp.where(first, b, a)
    new_bias[...] = intercept[...] - scale * bias_grad


def on_device(hidden, decoder_weight, decoder_intercept, analysis_truth, var_weight, lat_weight, area_bin, train_step):
    local, points, features = hidden.shape
    variables = decoder_weight.shape[0]
    rows = -(-variables // 8) * 8
    chunk = points // GROUPS
    members = local * GROUPS
    replicas = points * lax.axis_size("z") * lax.axis_size("x") * lax.axis_size("c") * GROUPS
    me, core = lax.axis_index("y"), lax.axis_index("c")
    where = jnp.stack([me, core]).astype(jnp.int32)

    def grant(mib):
        return pltpu.CompilerParams(vmem_limit_bytes=int(mib * MIB))

    intercept_row = decoder_intercept.reshape(1, variables)
    var_row = var_weight.reshape(1, variables)

    def turn(value, k):
        return value if k % GROUPS == 0 else lax.ppermute(value, "y", [(i, (i + k) % GROUPS) for i in range(GROUPS)])

    one_residual = jax.ShapeDtypeStruct((local, rows, chunk), F32)
    with jax.named_scope("forward_far"):
        far, half_weight = pl.pallas_call(
            far_kernel,
            out_shape=[one_residual, jax.ShapeDtypeStruct((rows, features), BF16)],
            in_specs=[SMEM, HBM, HBM],
            out_specs=[VMEM] * 2,
            scratch_shapes=[
                pltpu.VMEM((1, local, chunk, features), BF16),
                pltpu.VMEM((variables, features), F32),
                pltpu.SemaphoreType.DMA((1, local)),
                pltpu.SemaphoreType.DMA(()),
            ],
            compiler_params=grant(53.4),
            name="forward_far",
        )(where, hidden, decoder_weight)
        far = turn(far, 2)
    with jax.named_scope("forward_near"):
        after, before = pl.pallas_call(
            near_kernel,
            out_shape=[one_residual] * 2,
            in_specs=[SMEM, HBM, VMEM],
            out_specs=[VMEM] * 2,
            scratch_shapes=[
                pltpu.VMEM((2, local, chunk, features), BF16),
                pltpu.SemaphoreType.DMA((2, local)),
            ],
            compiler_params=grant(52),
            cost_estimate=pl.CostEstimate(
                flops=4 * rows * local * chunk * features, bytes_accessed=4 * local * chunk * features, transcendentals=0
            ),
            name="forward_near",
        )(where, hidden, half_weight)
        after, before = turn(after, 1), turn(before, 3)
    with jax.named_scope("forward_local"):
        here, area, point_weight, shift, held = pl.pallas_call(
            local_kernel,
            out_shape=[
                one_residual,
                jax.ShapeDtypeStruct((1, 128), F32),
                jax.ShapeDtypeStruct((rows, points), F32),
                jax.ShapeDtypeStruct((rows, chunk), F32),
                jax.ShapeDtypeStruct((GROUPS, local, chunk, features), BF16),
            ],
            in_specs=[SMEM, HBM] + [VMEM] * 6,
            out_specs=[VMEM] * 5,
            scratch_shapes=[pltpu.SemaphoreType.DMA((GROUPS, local))],
            compiler_params=grant(46),
            name="forward_local",
        )(where, hidden, half_weight, lat_weight.reshape(-1, 128), area_bin.reshape(1, points), intercept_row, analysis_truth, var_row)
    with jax.named_scope("early_pairs"):
        early = pl.pallas_call(
            lambda *refs: early_pairs_kernel(members, *refs),
            out_shape=jax.ShapeDtypeStruct((2 * local, rows, chunk), F32),
            in_specs=[VMEM] * 3,
            out_specs=VMEM,
            compiler_params=grant(4),
            name="early_pairs",
        )(here, far, shift)
    after, before, early, point_weight, held = lax.optimization_barrier((after, before, early, point_weight, held))
    one_bracket = jax.ShapeDtypeStruct((local, rows, chunk), BF16)
    with jax.named_scope("far_pairs"):
        far_bracket, near_sums = pl.pallas_call(
            lambda *refs: far_pairs_kernel(members, *refs),
            out_shape=[one_bracket, jax.ShapeDtypeStruct((2 * local, rows, chunk), F32)],
            in_specs=[VMEM] * 5,
            out_specs=[VMEM] * 2,
            scratch_shapes=[pltpu.VMEM((local, rows, chunk), F32)],
            compiler_params=grant(6),
            name="far_pairs",
        )(far, after, before, shift, early)
        far_bracket = turn(far_bracket, -2)
    with jax.named_scope("near_pairs"):
        here_bracket, after_bracket, before_bracket = pl.pallas_call(
            lambda *refs: near_pairs_kernel(members, *refs),
            out_shape=[one_bracket] * 3,
            in_specs=[VMEM] * 6,
            out_specs=[VMEM] * 3,
            scratch_shapes=[pltpu.VMEM((3 * local, rows, chunk), F32)],
            compiler_params=grant(6),
            cost_estimate=pl.CostEstimate(flops=600 * rows * chunk, bytes_accessed=64 * rows * chunk, transcendentals=60 * rows * chunk),
            name="near_pairs",
        )(here, after, before, shift, early, near_sums)
        returned = [here_bracket, turn(after_bracket, -1), far_bracket, turn(before_bracket, -3)]
    half = features // 2
    pieces = jax.ShapeDtypeStruct((PIECES, 8, half), F32)
    two_weighted = jax.ShapeDtypeStruct((GROUPS // 2, rows, local * chunk), BF16)
    sums = [pltpu.VMEM((PIECES * 8, half), F32)]
    with jax.named_scope("early_backward"):
        weighted_early, early_sum, early_bias = pl.pallas_call(
            early_backward_kernel,
            out_shape=[
                two_weighted,
                jax.ShapeDtypeStruct((rows, features), F32),
                jax.ShapeDtypeStruct((8, rows), F32),
            ],
            in_specs=[SMEM] + [VMEM] * 4,
            out_specs=[VMEM] * 3,
            compiler_params=grant(10),
            name="early_backward",
        )(where, held, returned[0], returned[2], point_weight)
    with jax.named_scope("backward_partner_half"):
        weighted_late, other = pl.pallas_call(
            partner_half_kernel,
            out_shape=[two_weighted, pieces],
            in_specs=[SMEM] + [VMEM] * 6,
            out_specs=[VMEM] * 2,
            scratch_shapes=sums,
            compiler_params=grant(10),
            name="backward_partner_half",
        )(where, held, returned[1], returned[3], point_weight, area, early_sum)
        swap = [(0, 1), (1, 0)]
        other = lax.ppermute(other, "c", swap)
    with jax.named_scope("backward_own_half"):
        mine = pl.pallas_call(
            own_half_kernel,
            out_shape=pieces,
            in_specs=[SMEM] + [VMEM] * 5,
            out_specs=VMEM,
            scratch_shapes=sums,
            compiler_params=grant(10),
            name="backward_own_half",
        )(where, held, weighted_late, early_sum, early_bias, area)
    with jax.named_scope("gradient_sum"):
        part = mine + other
        part = lax.all_to_all(part, ("x", "y"), 0, 0, tiled=True)
        depth = lax.axis_size("z")
        part = jnp.broadcast_to(jnp.sum(part, axis=0), (depth, 8, half))
        part = lax.all_to_all(part, "z", 0, 0, tiled=True)
        piece = jnp.sum(part, axis=0)
        own = lax.all_to_all(jnp.broadcast_to(piece, (PIECES, 8, half)), ("x", "y"), 0, 0, tiled=True)
    with jax.named_scope("grad_hidden"):
        grad_hidden = pl.pallas_call(
            lambda *refs: grad_hidden_kernel(*refs, replicas=replicas),
            out_shape=jax.ShapeDtypeStruct(hidden.shape, BF16),
            grid_spec=pltpu.PrefetchScalarGridSpec(
                num_scalar_prefetch=1,
                grid=(GROUPS,),
                in_specs=[
                    pl.BlockSpec((1, rows, local * chunk), lambda g, s: (lax.div(g, 2), 0, 0)),
                    pl.BlockSpec((1, rows, local * chunk), lambda g, s: (lax.div(g, 2), 0, 0)),
                    pl.BlockSpec((rows, features), lambda g, s: (0, 0)),
                    pl.BlockSpec((8, half), lambda g, s: (0, 0)),
                ],
                out_specs=pl.BlockSpec((local, chunk, features), lambda g, s: (0, lax.rem(s[0] + g, GROUPS), 0)),
            ),
            compiler_params=grant(12),
            cost_estimate=pl.CostEstimate(
                flops=2 * rows * local * points * features, bytes_accessed=2 * hidden.size, transcendentals=0
            ),
            name="grad_hidden",
        )(where, weighted_early, weighted_late, half_weight, piece)
        own, grad_hidden = lax.optimization_barrier((own, grad_hidden))
    with jax.named_scope("last_swap"):
        partner = lax.ppermute(own, "c", swap)
        gradient, squares = pl.pallas_call(
            lambda *refs: own_gradient_kernel(*refs, replicas=replicas),
            out_shape=[jax.ShapeDtypeStruct((variables, half), F32), jax.ShapeDtypeStruct((8, half), F32)],
            in_specs=[VMEM],
            out_specs=[VMEM] * 2,
            compiler_params=grant(4),
            name="own_gradient",
        )(own)
    with jax.named_scope("update"):
        new_weight, new_bias = pl.pallas_call(
            lambda *refs: update_kernel(*refs, replicas=replicas),
            out_shape=[
                jax.ShapeDtypeStruct((variables, features), F32),
                jax.ShapeDtypeStruct((1, variables), F32),
            ],
            in_specs=[SMEM, SMEM] + [VMEM] * 6,
            out_specs=[VMEM] * 2,
            scratch_shapes=[pltpu.VMEM((variables, half), F32)],
            compiler_params=grant(6),
            name="update",
        )(where, train_step, own, gradient, partner, squares, decoder_weight, intercept_row)
    return grad_hidden, new_weight, new_bias.reshape(variables)


def solution(mesh):
    fine = Mesh(mesh.devices.reshape(GROUPS, 8, 4, 2), ("y", "z", "x", "c"))
    space = ("z", "x", "c")
    return jax.shard_map(
        on_device,
        mesh=fine,
        in_specs=(P("y", space, None), P(), P(), P(None, space), P(), P(), P(space), P()),
        out_specs=(P("y", space, None), P(), P()),
        check_vma=False,
    )
```

```python
import jax
import jax.numpy as jnp
from jax import lax
from jax.experimental import pallas as pl
from jax.experimental.pallas import tpu as pltpu
from jax.sharding import Mesh, PartitionSpec as P

WARMUP = 1000
smooth_sq = 0.0025
fair_alpha = 0.95

GROUPS = 4
PIECES = 16
PIECE_ROWS = 7
MIB = 1024 * 1024
VMEM = pl.BlockSpec(memory_space=pltpu.VMEM)
SMEM = pl.BlockSpec(memory_space=pltpu.SMEM)
HBM = pl.BlockSpec(memory_space=pltpu.HBM)
F32 = jnp.float32
BF16 = jnp.bfloat16


def soft(d):
    return d * lax.rsqrt(d * d + smooth_sq)


def as_column(row, rows):
    n = row.shape[1]
    pick = lax.broadcasted_iota(jnp.int32, (rows, n), 0) == lax.broadcasted_iota(jnp.int32, (rows, n), 1)
    return jnp.sum(jnp.where(pick, jnp.broadcast_to(row, (rows, n)), 0.0), axis=1, keepdims=True)


def padded(value, rows):
    return jnp.concatenate([value, jnp.zeros((rows - value.shape[0], value.shape[1]), value.dtype)], axis=0)


def chunk_at(where, k, chunk):
    return pl.ds(pl.multiple_of(lax.rem(where[0] + k, GROUPS) * chunk, chunk), chunk)


def fetch_chunks(where, hidden, held, sem, ks):
    local, chunk = held.shape[1:3]
    copies = []
    for slot, k in enumerate(ks):
        points = chunk_at(where, k, chunk)
        copies.append(
            [pltpu.make_async_copy(hidden.at[m, points, :], held.at[slot, m], sem.at[slot, m]) for m in range(local)]
        )
        for copy in copies[slot]:
            copy.start()
    return copies


def decode_chunk(copies, held, half, out):
    for copy in copies:
        copy.wait()
    values = lax.dot_general(
        half[...], held[...].reshape(-1, held.shape[2]), (((1,), (1,)), ((), ())), preferred_element_type=F32
    )
    chunk = out.shape[2]
    for m in range(out.shape[0]):
        out[m] = values[:, m * chunk : (m + 1) * chunk]


def far_kernel(where, hidden, weight, out, half, held, w, sem, weight_sem):
    fetch = pltpu.make_async_copy(weight, w, weight_sem)
    fetch.start()
    (copies,) = fetch_chunks(where, hidden, held, sem, (2,))
    fetch.wait()
    half[...] = padded(w[...], half.shape[0]).astype(BF16)
    decode_chunk(copies, held.at[0], half, out)


def near_kernel(where, hidden, half, after, before, held, sem):
    copies = fetch_chunks(where, hidden, held, sem, (1, 3))
    for slot, out in enumerate((after, before)):
        decode_chunk(copies[slot], held.at[slot], half, out)


def add_pair(total, i, j, s):
    total[i] = s if total[i] is None else total[i] + s
    total[j] = -s if total[j] is None else total[j] - s


def pair_normalizer(members):
    eps = (1.0 - fair_alpha) / members
    return (1.0 - eps) / (members * (members - 1))


def row_tiles(rows, body):
    def tile(t, carry):
        body(pl.ds(pl.multiple_of(t * 8, 8), 8))
        return carry

    lax.fori_loop(0, rows // 8, tile, 0)


def early_pairs_kernel(members, here, far, shift, out):
    local = here.shape[0]
    count = 2 * local
    normalizer = pair_normalizer(members)

    def body(at):
        r = [ref[j, at, :] + shift[at, :] for ref in (here, far) for j in range(local)]
        total = [None] * count
        for i in range(count):
            for j in range(i + 1, count):
                add_pair(total, i, j, soft(r[i] - r[j]))
        for j in range(count):
            out[j, at, :] = soft(r[j]) * (1.0 / members) - normalizer * total[j]

    row_tiles(here.shape[1], body)


def far_pairs_kernel(members, far, after, before, shift, early, bracket, near, scratch):
    local = far.shape[0]
    normalizer = pair_normalizer(members)

    def body(at):
        r = [ref[j, at, :] + shift[at, :] for ref in (far, after, before) for j in range(local)]
        total = [None] * (3 * local)
        for i in range(local):
            for j in range(local, 3 * local):
                add_pair(total, i, j, soft(r[i] - r[j]))
        for j in range(local):
            scratch[j, at, :] = early[local + j, at, :] - normalizer * total[j]
        for j in range(2 * local):
            near[j, at, :] = total[local + j]

    row_tiles(far.shape[1], body)
    for j in range(local):
        bracket[j] = scratch[j].astype(BF16)


def near_pairs_kernel(members, here, after, before, shift, early, near, *rest):
    outs, scratch = rest[:3], rest[3]
    local = here.shape[0]
    normalizer = pair_normalizer(members)

    def body(at):
        r = [ref[j, at, :] + shift[at, :] for ref in (here, after, before) for j in range(local)]
        total = [None] * local + [near[j, at, :] for j in range(2 * local)]
        for i in range(3 * local):
            for j in range(max(i + 1, local), 3 * local):
                add_pair(total, i, j, soft(r[i] - r[j]))
        for j in range(3 * local):
            base = early[j, at, :] if j < local else soft(r[j]) * (1.0 / members)
            scratch[j, at, :] = base - normalizer * total[j]

    row_tiles(here.shape[1], body)
    for j in range(3 * local):
        outs[j // local][j % local] = scratch[j].astype(BF16)


def local_kernel(where, hidden, half, lat, area_bin, intercept, truth, var, out, area, weight, shift, held, sem):
    copies = fetch_chunks(where, hidden, held, sem, range(GROUPS))
    rows, chunk = shift.shape
    cells, width = lat.shape
    points = area_bin.shape[1]
    bins = jnp.broadcast_to(area_bin[...], (width, points))
    level = lax.broadcasted_iota(jnp.int32, (width, points), 0)
    total = jnp.zeros((width, points), F32)
    for q in range(cells):
        column = as_column(lat[q : q + 1, :], width)
        total = total + jnp.where(bins == level + q * width, column, 0.0)
    by_point = jnp.sum(total, axis=0, keepdims=True)
    area[...] = jnp.broadcast_to(jnp.sum(by_point, axis=1, keepdims=True), area.shape)
    weight[...] = by_point * as_column(var[...], rows)
    here = chunk_at(where, 0, chunk)
    shift[...] = as_column(intercept[...], rows) - padded(truth[:, here], rows)
    decode_chunk(copies[0], held.at[0], half, out)
    for chunk_copies in copies[1:]:
        for copy in chunk_copies:
            copy.wait()


def pieces_of(acc, extra, out):
    last = lax.broadcasted_iota(jnp.int32, out.shape[1:], 0) == PIECE_ROWS
    for r in range(PIECES):
        out[r] = jnp.where(last, extra, acc[PIECE_ROWS * r : PIECE_ROWS * r + 8, :])


def weigh(where, k, bracket, weight):
    local, _, chunk = bracket.shape
    scale = weight[:, chunk_at(where, k, chunk)]
    return jnp.concatenate([(scale * bracket[m].astype(F32)).astype(BF16) for m in range(local)], axis=1)


def bias_of(w):
    ones = jnp.ones((8, w.shape[1]), BF16)
    return lax.dot_general(ones, w, (((1,), (1,)), ((), ())), preferred_element_type=F32)


def early_backward_kernel(where, held, b0, b2, weight, weighted, total, bias):
    features = held.shape[3]
    w0 = weigh(where, 0, b0, weight)
    w2 = weigh(where, 2, b2, weight)
    weighted[0], weighted[1] = w0, w2
    bias[...] = bias_of(w0) + bias_of(w2)
    total[...] = jnp.dot(
        w0, held[0].reshape(-1, features), preferred_element_type=F32
    ) + jnp.dot(w2, held[2].reshape(-1, features), preferred_element_type=F32)


def next_backward_kernel(where, held, b1, weight, early, early_bias, weighted, total, bias):
    w1 = weigh(where, 1, b1, weight)
    weighted[0] = w1
    bias[...] = early_bias[...] + bias_of(w1)
    total[...] = early[...] + jnp.dot(w1, held[1].reshape(-1, held.shape[3]), preferred_element_type=F32)


def late_half(side, w3, held, early, acc):
    rows = w3.shape[0]
    half = acc.shape[1]
    lanes = pl.ds(pl.multiple_of(side * half, half), half)
    acc[0:rows, :] = (
        early[:, lanes]
        + jnp.dot(w3, held[3, :, :, lanes].reshape(-1, half), preferred_element_type=F32)
    )
    acc[rows:, :] = jnp.zeros((acc.shape[0] - rows, half), F32)


def extra_row(bias, area, half):
    row = jnp.concatenate([bias, area, jnp.zeros((1, half - 256), F32)], axis=1)
    return jnp.broadcast_to(row, (8, half))


def partner_half_kernel(where, held, b3, weight, area, early, weighted, other, acc):
    w3 = weigh(where, 3, b3, weight)
    weighted[0] = w3
    late_half(1 - where[1], w3, held, early, acc)
    pieces_of(acc, extra_row(jnp.zeros((1, 128), F32), area[...], acc.shape[1]), other)


def own_half_kernel(where, held, weighted, early, early_bias, area, mine, acc):
    rows = early.shape[0]
    w3 = weighted[0]
    late_half(where[1], w3, held, early, acc)
    bias = early_bias[...] + bias_of(w3)
    bias = jnp.concatenate([bias[0:1], jnp.zeros((1, 128 - rows), F32)], axis=1)
    pieces_of(acc, extra_row(bias, area[...], acc.shape[1]), mine)


def grad_hidden_kernel(where, early, late, half, piece, out, *, replicas):
    first = lax.rem(pl.program_id(0), 2) == 0
    inverse = 1.0 / (piece[PIECE_ROWS : PIECE_ROWS + 1, 128:129] * (1.0 / replicas))
    chunk = out.shape[1]
    for m in range(out.shape[0]):
        lanes = slice(m * chunk, (m + 1) * chunk)
        product = lax.dot_general(
            jnp.where(first, early[0, :, lanes], late[0, :, lanes]), half[...], (((0,), (0,)), ((), ())), preferred_element_type=F32
        )
        out[m] = (product * inverse).astype(BF16)


def squares_of(pieces, inverse):
    half = pieces.shape[2]
    keep = lax.broadcasted_iota(jnp.int32, (8, half), 0) < PIECE_ROWS
    squares = jnp.zeros((8, half), F32)
    for r in range(PIECES):
        g = jnp.where(keep, pieces[r] * inverse, 0.0)
        squares = squares + g * g
    return squares


def in_order(pieces, inverse, out):
    for r in range(PIECES):
        low = PIECE_ROWS * r
        n = min(PIECE_ROWS, out.shape[0] - low)
        if n > 0:
            out[low : low + n, :] = pieces[r, 0:n, :] * inverse


def own_gradient_kernel(own, gradient, squares, *, replicas):
    inverse = 1.0 / (own[0, PIECE_ROWS : PIECE_ROWS + 1, 128:129] * (1.0 / replicas))
    squares[...] = squares_of(own, inverse)
    in_order(own, inverse, gradient)


def update_kernel(
    where, step, own, gradient, partner, squares, weight, intercept, new_weight, new_bias, other, *, replicas
):
    variables, features = weight.shape
    half = features // 2
    first = where[1] == 0
    inverse = 1.0 / (own[0, PIECE_ROWS : PIECE_ROWS + 1, 128:129] * (1.0 / replicas))
    a, b = (side[0, PIECE_ROWS : PIECE_ROWS + 1, 0:variables] for side in (own, partner))
    bias_grad = (jnp.where(first, a, b) + jnp.where(first, b, a)) * inverse
    in_order(partner, inverse, other)
    a, b = squares[...], squares_of(partner, inverse)
    both = jnp.where(first, a, b) + jnp.where(first, b, a)
    total = jnp.sum(jnp.sum(both, axis=0, keepdims=True), axis=1, keepdims=True)
    total = total + jnp.sum(bias_grad * bias_grad, axis=1, keepdims=True)
    count = variables * features + variables
    rms = jnp.sqrt(total / count + 1e-06)
    warm = (step[0] + 1).astype(F32) / WARMUP
    scale = warm * jnp.minimum(1.0, 1.0 / rms)
    a, b = gradient[...], other[...]
    new_weight[:, :half] = weight[:, :half] - scale * jnp.where(first, a, b)
    new_weight[:, half:] = weight[:, half:] - scale * jnp.where(first, b, a)
    new_bias[...] = intercept[...] - scale * bias_grad


def on_device(hidden, decoder_weight, decoder_intercept, analysis_truth, var_weight, lat_weight, area_bin, train_step):
    local, points, features = hidden.shape
    variables = decoder_weight.shape[0]
    rows = -(-variables // 8) * 8
    chunk = points // GROUPS
    members = local * GROUPS
    replicas = points * lax.axis_size("z") * lax.axis_size("x") * lax.axis_size("c") * GROUPS
    me, core = lax.axis_index("y"), lax.axis_index("c")
    where = jnp.stack([me, core]).astype(jnp.int32)

    def grant(mib):
        return pltpu.CompilerParams(vmem_limit_bytes=int(mib * MIB))

    intercept_row = decoder_intercept.reshape(1, variables)
    var_row = var_weight.reshape(1, variables)

    def turn(value, k):
        return value if k % GROUPS == 0 else lax.ppermute(value, "y", [(i, (i + k) % GROUPS) for i in range(GROUPS)])

    one_residual = jax.ShapeDtypeStruct((local, rows, chunk), F32)
    with jax.named_scope("forward_far"):
        far, half_weight = pl.pallas_call(
            far_kernel,
            out_shape=[one_residual, jax.ShapeDtypeStruct((rows, features), BF16)],
            in_specs=[SMEM, HBM, HBM],
            out_specs=[VMEM] * 2,
            scratch_shapes=[
                pltpu.VMEM((1, local, chunk, features), BF16),
                pltpu.VMEM((variables, features), F32),
                pltpu.SemaphoreType.DMA((1, local)),
                pltpu.SemaphoreType.DMA(()),
            ],
            compiler_params=grant(53.4),
            name="forward_far",
        )(where, hidden, decoder_weight)
        far = turn(far, 2)
    with jax.named_scope("forward_near"):
        after, before = pl.pallas_call(
            near_kernel,
            out_shape=[one_residual] * 2,
            in_specs=[SMEM, HBM, VMEM],
            out_specs=[VMEM] * 2,
            scratch_shapes=[
                pltpu.VMEM((2, local, chunk, features), BF16),
                pltpu.SemaphoreType.DMA((2, local)),
            ],
            compiler_params=grant(52),
            cost_estimate=pl.CostEstimate(
                flops=4 * rows * local * chunk * features, bytes_accessed=4 * local * chunk * features, transcendentals=0
            ),
            name="forward_near",
        )(where, hidden, half_weight)
        after, before = turn(after, 1), turn(before, 3)
    with jax.named_scope("forward_local"):
        here, area, point_weight, shift, held = pl.pallas_call(
            local_kernel,
            out_shape=[
                one_residual,
                jax.ShapeDtypeStruct((1, 128), F32),
                jax.ShapeDtypeStruct((rows, points), F32),
                jax.ShapeDtypeStruct((rows, chunk), F32),
                jax.ShapeDtypeStruct((GROUPS, local, chunk, features), BF16),
            ],
            in_specs=[SMEM, HBM] + [VMEM] * 6,
            out_specs=[VMEM] * 5,
            scratch_shapes=[pltpu.SemaphoreType.DMA((GROUPS, local))],
            compiler_params=grant(46),
            name="forward_local",
        )(where, hidden, half_weight, lat_weight.reshape(-1, 128), area_bin.reshape(1, points), intercept_row, analysis_truth, var_row)
    with jax.named_scope("early_pairs"):
        early = pl.pallas_call(
            lambda *refs: early_pairs_kernel(members, *refs),
            out_shape=jax.ShapeDtypeStruct((2 * local, rows, chunk), F32),
            in_specs=[VMEM] * 3,
            out_specs=VMEM,
            compiler_params=grant(4),
            name="early_pairs",
        )(here, far, shift)
    after, before, early, point_weight, held = lax.optimization_barrier((after, before, early, point_weight, held))
    one_bracket = jax.ShapeDtypeStruct((local, rows, chunk), BF16)
    with jax.named_scope("far_pairs"):
        far_bracket, near_sums = pl.pallas_call(
            lambda *refs: far_pairs_kernel(members, *refs),
            out_shape=[one_bracket, jax.ShapeDtypeStruct((2 * local, rows, chunk), F32)],
            in_specs=[VMEM] * 5,
            out_specs=[VMEM] * 2,
            scratch_shapes=[pltpu.VMEM((local, rows, chunk), F32)],
            compiler_params=grant(6),
            name="far_pairs",
        )(far, after, before, shift, early)
        far_bracket = turn(far_bracket, -2)
    with jax.named_scope("near_pairs"):
        here_bracket, after_bracket, before_bracket = pl.pallas_call(
            lambda *refs: near_pairs_kernel(members, *refs),
            out_shape=[one_bracket] * 3,
            in_specs=[VMEM] * 6,
            out_specs=[VMEM] * 3,
            scratch_shapes=[pltpu.VMEM((3 * local, rows, chunk), F32)],
            compiler_params=grant(6),
            cost_estimate=pl.CostEstimate(flops=600 * rows * chunk, bytes_accessed=64 * rows * chunk, transcendentals=60 * rows * chunk),
            name="near_pairs",
        )(here, after, before, shift, early, near_sums)
        returned = [here_bracket, turn(after_bracket, -1), far_bracket, turn(before_bracket, -3)]
    half = features // 2
    pieces = jax.ShapeDtypeStruct((PIECES, 8, half), F32)
    two_weighted = jax.ShapeDtypeStruct((GROUPS // 2, rows, local * chunk), BF16)
    sums = [pltpu.VMEM((PIECES * 8, half), F32)]
    with jax.named_scope("early_backward"):
        weighted_early, early_sum, early_bias = pl.pallas_call(
            early_backward_kernel,
            out_shape=[
                two_weighted,
                jax.ShapeDtypeStruct((rows, features), F32),
                jax.ShapeDtypeStruct((8, rows), F32),
            ],
            in_specs=[SMEM] + [VMEM] * 4,
            out_specs=[VMEM] * 3,
            compiler_params=grant(10),
            name="early_backward",
        )(where, held, returned[0], returned[2], point_weight)
    one_weighted = jax.ShapeDtypeStruct((1, rows, local * chunk), BF16)
    with jax.named_scope("next_backward"):
        weighted_next, early_sum, early_bias = pl.pallas_call(
            next_backward_kernel,
            out_shape=[
                one_weighted,
                jax.ShapeDtypeStruct((rows, features), F32),
                jax.ShapeDtypeStruct((8, rows), F32),
            ],
            in_specs=[SMEM] + [VMEM] * 5,
            out_specs=[VMEM] * 3,
            compiler_params=grant(10),
            name="next_backward",
        )(where, held, returned[1], point_weight, early_sum, early_bias)
    with jax.named_scope("backward_partner_half"):
        weighted_late, other = pl.pallas_call(
            partner_half_kernel,
            out_shape=[one_weighted, pieces],
            in_specs=[SMEM] + [VMEM] * 5,
            out_specs=[VMEM] * 2,
            scratch_shapes=sums,
            compiler_params=grant(10),
            name="backward_partner_half",
        )(where, held, returned[3], point_weight, area, early_sum)
        swap = [(0, 1), (1, 0)]
        other = lax.ppermute(other, "c", swap)
    with jax.named_scope("backward_own_half"):
        mine = pl.pallas_call(
            own_half_kernel,
            out_shape=pieces,
            in_specs=[SMEM] + [VMEM] * 5,
            out_specs=VMEM,
            scratch_shapes=sums,
            compiler_params=grant(10),
            name="backward_own_half",
        )(where, held, weighted_late, early_sum, early_bias, area)
    with jax.named_scope("gradient_sum"):
        part = mine + other
        part = lax.all_to_all(part, ("x", "y"), 0, 0, tiled=True)
        depth = lax.axis_size("z")
        part = jnp.broadcast_to(jnp.sum(part, axis=0), (depth, 8, half))
        part = lax.all_to_all(part, "z", 0, 0, tiled=True)
        piece = jnp.sum(part, axis=0)
        own = lax.all_to_all(jnp.broadcast_to(piece, (PIECES, 8, half)), ("x", "y"), 0, 0, tiled=True)
    with jax.named_scope("grad_hidden"):
        grad_hidden = pl.pallas_call(
            lambda *refs: grad_hidden_kernel(*refs, replicas=replicas),
            out_shape=jax.ShapeDtypeStruct(hidden.shape, BF16),
            grid_spec=pltpu.PrefetchScalarGridSpec(
                num_scalar_prefetch=1,
                grid=(GROUPS,),
                in_specs=[
                    pl.BlockSpec((1, rows, local * chunk), lambda g, s: (lax.div(g, 2), 0, 0)),
                    pl.BlockSpec((1, rows, local * chunk), lambda g, s: (lax.div(g, 2), 0, 0)),
                    pl.BlockSpec((rows, features), lambda g, s: (0, 0)),
                    pl.BlockSpec((8, half), lambda g, s: (0, 0)),
                ],
                out_specs=pl.BlockSpec((local, chunk, features), lambda g, s: (0, lax.rem(s[0] + g, GROUPS), 0)),
            ),
            compiler_params=grant(12),
            cost_estimate=pl.CostEstimate(
                flops=2 * rows * local * points * features, bytes_accessed=2 * hidden.size, transcendentals=0
            ),
            name="grad_hidden",
        )(where, weighted_early, jnp.concatenate([weighted_next, weighted_late]), half_weight, piece)
        own, grad_hidden = lax.optimization_barrier((own, grad_hidden))
    with jax.named_scope("last_swap"):
        partner = lax.ppermute(own, "c", swap)
        gradient, squares = pl.pallas_call(
            lambda *refs: own_gradient_kernel(*refs, replicas=replicas),
            out_shape=[jax.ShapeDtypeStruct((variables, half), F32), jax.ShapeDtypeStruct((8, half), F32)],
            in_specs=[VMEM],
            out_specs=[VMEM] * 2,
            compiler_params=grant(4),
            name="own_gradient",
        )(own)
    with jax.named_scope("update"):
        new_weight, new_bias = pl.pallas_call(
            lambda *refs: update_kernel(*refs, replicas=replicas),
            out_shape=[
                jax.ShapeDtypeStruct((variables, features), F32),
                jax.ShapeDtypeStruct((1, variables), F32),
            ],
            in_specs=[SMEM, SMEM] + [VMEM] * 6,
            out_specs=[VMEM] * 2,
            scratch_shapes=[pltpu.VMEM((variables, half), F32)],
            compiler_params=grant(6),
            name="update",
        )(where, train_step, own, gradient, partner, squares, decoder_weight, intercept_row)
    return grad_hidden, new_weight, new_bias.reshape(variables)


def solution(mesh):
    fine = Mesh(mesh.devices.reshape(GROUPS, 8, 4, 2), ("y", "z", "x", "c"))
    space = ("z", "x", "c")
    return jax.shard_map(
        on_device,
        mesh=fine,
        in_specs=(P("y", space, None), P(), P(), P(None, space), P(), P(), P(space), P()),
        out_specs=(P("y", space, None), P(), P()),
        check_vma=False,
    )
```
